256 devices in a mesh: slab: 64 (over x, z, y_hi), case: 4 (over y_lo, core).
Axes of the slice: x: 4, y: 4 (y_hi: 2, y_lo: 2; y = y_hi * 2 + y_lo), z: 8, core: 2. Of those that a mesh axis runs over, the one named last changes fastest.
Arguments:
- tokens: bfloat16 [4, 128, 8, 8, 512], P('case', 'slab'), may hold values from -6 to 6
- cotangent: bfloat16 [4, 128, 8, 8, 512], P('case', 'slab'), may hold values from -6 to 6
- w_qkv: bfloat16 [512, 1536], replicated, may hold values from -4 to 4
- w_out: bfloat16 [512, 512], replicated, may hold values from -0.25 to 0.25
- w_up: bfloat16 [512, 2048], replicated, may hold values from -0.25 to 0.25
- w_down: bfloat16 [2048, 512], replicated, may hold values from -0.125 to 0.125
- gain_attn: float32 [512], replicated, may hold values from 0.1 to 1.9
- gain_mlp: float32 [512], replicated, may hold values from 0.1 to 1.9
Outputs:
- grad_tokens: bfloat16 [4, 128, 8, 8, 512], P('case', 'slab')
- grad_qkv: float32 [512, 1536], P('slab')
- grad_out: float32 [512, 512], P('slab')
- grad_up: float32 [512, 2048], P('slab')
- grad_down: float32 [2048, 512], P('slab')
- grad_gain_attn: float32 [512], P('slab')
- grad_gain_mlp: float32 [512], P('slab')
The draws below stay inside these ranges and needn't reach their ends.
All inputs are finite; a program needn't handle non-finite values.
Results may differ from the reference program's by a relative error of at most 0.022.
Values may be sent and summed in bfloat16 or wider, within the bound.
A program may use at most 128 MiB of HBM per device.

```python
import math
import jax
import jax.numpy as jnp
from jax import lax

D = 512
HEADS = 8
FF = 2048
GX = 8
GY = 8
Z = 128
CASES = 4
TOKENS_ALL = 32768


def draw_w_qkv(key, part):
    key = jax.random.fold_in(key, 11)
    base = jnp.clip(jax.random.normal(key, (D, 3 * D), jnp.float32), -4.5, 4.5) / math.sqrt(D)
    return base.astype(jnp.bfloat16)


def steps_of(rng, dims, pieces, least, top_value):
    def one(axis_at, parts):
        heights = jax.random.uniform(jax.random.fold_in(jax.random.fold_in(rng, 6), axis_at), (parts,), jnp.float32, least / len(pieces), top_value / len(pieces))
        return jnp.repeat(jnp.exp(heights), dims[axis_at] // parts).reshape((-1,) + (1,) * (len(dims) - axis_at - 1))

    level = one(*pieces[0])
    for cut in pieces[1:]:
        level = level * one(*cut)
    return level


def bell_draw(rng, shape, spread, limit, pieces=(), dtype=jnp.bfloat16):
    array = jax.random.normal(rng, shape, jnp.float32) * spread
    if len(pieces) > 0:
        array = steps_of(rng, shape, pieces, -0.22, 0.18) * array
    return jnp.clip(array, min=-limit, max=limit).astype(dtype)


def setup_inputs(seed: int = 0) -> dict:
    key_list = jax.random.split(jax.random.key(seed), 9)
    tokens = bell_draw(key_list[0], (CASES, Z, GY, GX, D), 1.0, 6.0, ((0, 4), (1, 64)))
    cotangent = bell_draw(key_list[1], (CASES, Z, GY, GX, D), 1.0, 6.0, ((0, 4), (1, 64)))
    w_qkv = draw_w_qkv(jax.random.fold_in(key_list[8], 71), 0)
    w_out = bell_draw(key_list[3], (D, D), D ** -0.5, 0.25)
    w_up = bell_draw(key_list[4], (D, FF), D ** -0.5, 0.25)
    w_down = bell_draw(key_list[5], (FF, D), FF ** -0.5, 0.125)
    gain_attn = jnp.clip(1.0 + 0.18 * jax.random.normal(key_list[6], (D,), jnp.float32), 0.1, 1.9)
    gain_mlp = jnp.clip(1.0 + 0.18 * jax.random.normal(key_list[7], (D,), jnp.float32), 0.1, 1.9)
    return dict(tokens=tokens, cotangent=cotangent, w_qkv=w_qkv, w_out=w_out, w_up=w_up, w_down=w_down, gain_attn=gain_attn, gain_mlp=gain_mlp)


epsilon = 1e-06
root_two_pi = math.sqrt(2.0 / math.pi)

def normalize(values, gain):
    inverse = lax.rsqrt(lax.optimization_barrier(jnp.mean(values * values, axis=-1, keepdims=True)) + epsilon)
    normed = values * inverse
    return (normed, inverse, (normed * gain).astype(jnp.bfloat16))

def norm_back(grad_normed, normed, inverse, gain):
    scaled = grad_normed * gain
    return inverse * (scaled - normed * lax.optimization_barrier(jnp.mean(scaled * normed, axis=-1, keepdims=True)))

def gelu_value(inputs):
    inner = root_two_pi * (inputs + 0.044715 * inputs * inputs * inputs)
    return 0.5 * inputs * (1.0 + jnp.tanh(inner))

def gelu_slope(inputs):
    tangent = jnp.tanh(root_two_pi * (inputs + 0.044715 * inputs * inputs * inputs))
    return 0.5 * (1.0 + tangent) + 0.5 * inputs * (1.0 - tangent * tangent) * root_two_pi * (1.0 + 3.0 * 0.044715 * inputs * inputs)

def line_probs(queries, key_rows):
    scale = queries.shape[-1] ** (-0.5)
    scores = jnp.einsum('blhe,bmhe->bhlm', queries.astype(jnp.float32), key_rows.astype(jnp.float32)) * scale
    top = lax.optimization_barrier(jnp.max(scores, axis=-1, keepdims=True))
    weights = jnp.exp(scores - top)
    return weights / lax.optimization_barrier(jnp.sum(weights, axis=-1, keepdims=True))

def attend_lines(queries, key_rows, value_rows):
    probs = line_probs(queries, key_rows)
    rounded = lax.optimization_barrier(probs.astype(jnp.bfloat16)).astype(jnp.float32)
    return jnp.einsum('bhlm,bmhe->blhe', rounded, value_rows.astype(jnp.float32))

def attend_back(queries, key_rows, value_rows, grad_lines):
    scale = queries.shape[-1] ** (-0.5)
    probs = line_probs(queries, key_rows)
    rounded = lax.optimization_barrier(probs.astype(jnp.bfloat16)).astype(jnp.float32)
    grad_float = grad_lines.astype(jnp.float32)
    grad_values = jnp.einsum('bhlm,blhe->bmhe', rounded, grad_float)
    grad_probs = jnp.einsum('blhe,bmhe->bhlm', grad_float, value_rows.astype(jnp.float32))
    grad_scores = probs * (grad_probs - lax.optimization_barrier(jnp.sum(probs * grad_probs, axis=-1, keepdims=True)))
    score_b = lax.optimization_barrier(grad_scores.astype(jnp.bfloat16)).astype(jnp.float32)
    grad_queries = jnp.einsum('bhlm,bmhe->blhe', score_b, key_rows.astype(jnp.float32)) * scale
    grad_keys = jnp.einsum('bhlm,blhe->bmhe', score_b, queries.astype(jnp.float32)) * scale
    return (grad_queries, grad_keys, grad_values)

def lines_x(grid):
    return grid.reshape(grid.shape[0] * grid.shape[1], grid.shape[2], grid.shape[3], grid.shape[4])

def lines_y(grid):
    return jnp.swapaxes(grid, 1, 2).reshape(grid.shape[0] * grid.shape[2], grid.shape[1], grid.shape[3], grid.shape[4])

def unlines_y(lines, shape):
    return jnp.swapaxes(lines.reshape(shape[0], shape[2], shape[1], shape[3], shape[4]), 1, 2)

def lines_z(grid):
    return jnp.transpose(grid, (1, 2, 0, 3, 4)).reshape(grid.shape[1] * grid.shape[2], grid.shape[0], grid.shape[3], grid.shape[4])

def unlines_z(lines, shape):
    return jnp.transpose(lines.reshape(shape[1], shape[2], shape[0], shape[3], shape[4]), (2, 0, 1, 3, 4))

def case_step(totals, inputs):
    tokens_case, cotangent_case, w_qkv, w_out, w_up, w_down, gain_attn, gain_mlp = inputs
    depth, height, across, width = tokens_case.shape
    count = depth * height * across
    head_size = width // HEADS
    shape = (depth, height, across, HEADS, head_size)
    flat = tokens_case.reshape(count, width).astype(jnp.float32)
    normed_one, inverse_one, hidden_one = normalize(flat, gain_attn)
    projected = jnp.dot(hidden_one, w_qkv, preferred_element_type=jnp.float32).astype(jnp.bfloat16)
    queries = projected[:, :width].reshape(shape)
    key_rows = projected[:, width:2 * width].reshape(shape)
    value_rows = projected[:, 2 * width:].reshape(shape)
    out_x = attend_lines(lines_x(queries), lines_x(key_rows), lines_x(value_rows)).reshape(shape)
    out_y = unlines_y(attend_lines(lines_y(queries), lines_y(key_rows), lines_y(value_rows)), shape)
    out_z = unlines_z(attend_lines(lines_z(queries), lines_z(key_rows), lines_z(value_rows)), shape).astype(jnp.bfloat16)
    mixed = (out_x + out_y + out_z.astype(jnp.float32)).reshape(count, width).astype(jnp.bfloat16)
    residual = (flat + jnp.dot(mixed, w_out, preferred_element_type=jnp.float32)).astype(jnp.bfloat16)
    normed_two, inverse_two, hidden_two = normalize(residual.astype(jnp.float32), gain_mlp)
    upper = jnp.dot(hidden_two, w_up, preferred_element_type=jnp.float32)
    active = gelu_value(upper).astype(jnp.bfloat16)
    grad_rows = cotangent_case.reshape(count, width)
    grad_active = jnp.dot(grad_rows, w_down.T, preferred_element_type=jnp.float32)
    total_down = jnp.dot(active.T, grad_rows, preferred_element_type=jnp.float32)
    grad_upper = (grad_active * gelu_slope(upper)).astype(jnp.bfloat16)
    total_up = jnp.dot(hidden_two.T, grad_upper, preferred_element_type=jnp.float32)
    grad_hidden_two = jnp.dot(grad_upper, w_up.T, preferred_element_type=jnp.float32)
    total_gain_two = lax.optimization_barrier(jnp.sum(grad_hidden_two * normed_two, axis=0))
    grad_residual = grad_rows.astype(jnp.float32) + norm_back(grad_hidden_two, normed_two, inverse_two, gain_mlp)
    grad_res_b = grad_residual.astype(jnp.bfloat16)
    total_out = jnp.dot(mixed.T, grad_res_b, preferred_element_type=jnp.float32)
    grad_mixed = jnp.dot(grad_res_b, w_out.T, preferred_element_type=jnp.float32).astype(jnp.bfloat16).reshape(shape)
    back_x = attend_back(lines_x(queries), lines_x(key_rows), lines_x(value_rows), lines_x(grad_mixed))
    back_y = attend_back(lines_y(queries), lines_y(key_rows), lines_y(value_rows), lines_y(grad_mixed))
    back_z = attend_back(lines_z(queries), lines_z(key_rows), lines_z(value_rows), lines_z(grad_mixed))
    columns = []
    columns_z = []
    for which in range(3):
        part_x = back_x[which].reshape(shape)
        part_y = unlines_y(back_y[which], shape)
        columns.append((part_x + part_y).reshape(count, width))
        columns_z.append(unlines_z(back_z[which], shape).astype(jnp.bfloat16).reshape(count, width))
    grad_proj = jnp.concatenate(columns, axis=1).astype(jnp.bfloat16)
    grad_proj_z = jnp.concatenate(columns_z, axis=1)
    total_qkv = jnp.dot(hidden_one.T, grad_proj, preferred_element_type=jnp.float32) + jnp.dot(hidden_one.T, grad_proj_z, preferred_element_type=jnp.float32)
    grad_hidden_one = jnp.dot(grad_proj, w_qkv.T, preferred_element_type=jnp.float32) + jnp.dot(grad_proj_z, w_qkv.T, preferred_element_type=jnp.float32)
    total_gain_one = lax.optimization_barrier(jnp.sum(grad_hidden_one * normed_one, axis=0))
    grad_tokens = (grad_residual + norm_back(grad_hidden_one, normed_one, inverse_one, gain_attn)).astype(jnp.bfloat16)
    updated = (totals[0] + total_qkv, totals[1] + total_out, totals[2] + total_up, totals[3] + total_down, totals[4] + total_gain_one, totals[5] + total_gain_two)
    return (updated, grad_tokens.reshape(depth, height, across, width))

def reference(tokens, cotangent, w_qkv, w_out, w_up, w_down, gain_attn, gain_mlp):
    width = tokens.shape[-1]
    hidden_units = w_up.shape[1]
    start = (jnp.zeros((width, 3 * width), jnp.float32), jnp.zeros((width, width), jnp.float32), jnp.zeros((width, hidden_units), jnp.float32), jnp.zeros((hidden_units, width), jnp.float32), jnp.zeros((width,), jnp.float32), jnp.zeros((width,), jnp.float32))

    def step(totals, pair):
        return case_step(totals, (pair[0], pair[1], w_qkv, w_out, w_up, w_down, gain_attn, gain_mlp))
    totals, grad_tokens = lax.scan(step, start, (tokens, cotangent))
    factor = 1.0 / math.sqrt(TOKENS_ALL)
    return (grad_tokens, totals[0] * factor, totals[1] * factor, totals[2] * factor, totals[3] * factor, totals[4] * factor, totals[5] * factor)
```

```python
import math

import jax
import jax.numpy as jnp
from jax import lax
from jax.experimental import pallas as pl
from jax.experimental.pallas import tpu as pltpu
from jax.sharding import PartitionSpec as P

HEADS = 8
epsilon = 1e-06
root_two_pi = math.sqrt(2.0 / math.pi)
MESH = pl.DeviceIdType.MESH
F32 = jnp.float32
BF16 = jnp.bfloat16


def normalize(values, gain):
    inverse = lax.rsqrt(jnp.mean(values * values, axis=-1, keepdims=True) + epsilon)
    normed = values * inverse
    return (normed, inverse, (normed * gain).astype(jnp.bfloat16))


def norm_back(grad_normed, normed, inverse, gain):
    scaled = grad_normed * gain
    return inverse * (scaled - normed * jnp.mean(scaled * normed, axis=-1, keepdims=True))


def gelu_value(inputs):
    inner = root_two_pi * (inputs + 0.044715 * inputs * inputs * inputs)
    return 0.5 * inputs * (1.0 + jnp.tanh(inner))


def gelu_slope(inputs):
    tangent = jnp.tanh(root_two_pi * (inputs + 0.044715 * inputs * inputs * inputs))
    return 0.5 * (1.0 + tangent) + 0.5 * inputs * (1.0 - tangent * tangent) * root_two_pi * (
        1.0 + 3.0 * 0.044715 * inputs * inputs
    )


def line_probs(queries, key_rows):
    scale = queries.shape[-1] ** (-0.5)
    scores = (
        jnp.einsum("blhe,bmhe->bhlm", queries, key_rows, preferred_element_type=jnp.float32) * scale
    )
    top = jnp.max(scores, axis=-1, keepdims=True)
    weights = jnp.exp(scores - top)
    return weights / jnp.sum(weights, axis=-1, keepdims=True)


def attend_lines(queries, key_rows, value_rows):
    probs = line_probs(queries, key_rows).astype(jnp.bfloat16)
    return jnp.einsum("bhlm,bmhe->blhe", probs, value_rows, preferred_element_type=jnp.float32)


def attend_back(queries, key_rows, value_rows, grad_lines):
    scale = queries.shape[-1] ** (-0.5)
    probs = line_probs(queries, key_rows)
    rounded = probs.astype(jnp.bfloat16)
    grad_values = jnp.einsum(
        "bhlm,blhe->bmhe", rounded, grad_lines, preferred_element_type=jnp.float32
    )
    grad_probs = jnp.einsum(
        "blhe,bmhe->bhlm", grad_lines, value_rows, preferred_element_type=jnp.float32
    )
    grad_scores = probs * (grad_probs - jnp.sum(probs * grad_probs, axis=-1, keepdims=True))
    score_b = grad_scores.astype(jnp.bfloat16)
    grad_queries = (
        jnp.einsum("bhlm,bmhe->blhe", score_b, key_rows, preferred_element_type=jnp.float32) * scale
    )
    grad_keys = (
        jnp.einsum("bhlm,blhe->bmhe", score_b, queries, preferred_element_type=jnp.float32) * scale
    )
    return (grad_queries, grad_keys, grad_values)


def lines_x(grid):
    return grid.reshape(grid.shape[0] * grid.shape[1], grid.shape[2], grid.shape[3], grid.shape[4])


def lines_y(grid):
    return jnp.swapaxes(grid, 1, 2).reshape(
        grid.shape[0] * grid.shape[2], grid.shape[1], grid.shape[3], grid.shape[4]
    )


def unlines_y(lines, shape):
    return jnp.swapaxes(lines.reshape(shape[0], shape[2], shape[1], shape[3], shape[4]), 1, 2)


def pencil_lines(block):
    shape = block.shape
    merged = block.reshape(shape[0], shape[1], shape[2] * 2, shape[3] // 2)
    return jnp.transpose(merged, (1, 0, 2, 3))


def pencil_block(lines, shape):
    return jnp.transpose(lines, (1, 0, 2, 3)).reshape(shape)


WIDE = 1792
PART = 896


def places():
    slab, case = lax.axis_index("slab"), lax.axis_index("case")
    return slab // 16, (slab // 2) % 8, slab % 2, case // 2, case % 2


def device(x, z, y_hi, y_lo, core):
    return ((x * 8 + z) * 2 + y_hi, y_lo * 2 + core)


class Ring:
    def __init__(self, me, dev, part, relay, fin, ss, rs):
        self.me, self.dev, self.part, self.relay, self.fin, self.ss, self.rs = me, dev, part, relay, fin, ss, rs
        self.right, self.left, self.over = (me + 1) % 4, (me + 3) % 4, (me + 2) % 4
        self.copies = []

    def send(self, src, dst, to):
        n = len(self.copies)
        copy = pltpu.make_async_remote_copy(
            src_ref=src,
            dst_ref=dst,
            send_sem=self.ss.at[n],
            recv_sem=self.rs.at[n],
            device_id=self.dev(to),
            device_id_type=MESH,
        )
        copy.start()
        self.copies.append(copy)

    def start(self):
        self.send(self.part(self.over, 0), self.relay.at[0], self.right)
        self.send(self.part(self.over, 1), self.relay.at[1], self.left)
        self.send(self.part(self.right, 1), self.fin.at[1], self.right)
        self.send(self.part(self.left, 0), self.fin.at[2], self.left)

    def middle(self):
        for h, to, slot in ((0, self.right, 0), (1, self.left, 3)):
            self.copies[h].wait_recv()
            ref = self.part(to, h)
            ref[...] = (ref[...].astype(F32) + self.relay[h].astype(F32)).astype(BF16)
            self.send(ref, self.fin.at[slot], to)

    def finish(self):
        for copy in self.copies[2:]:
            copy.wait_recv()

    def result(self, h):
        a, b = (0, 2) if h == 0 else (1, 3)
        own = self.part(self.me, h)[...].astype(F32)
        return (own + self.fin[a].astype(F32) + self.fin[b].astype(F32)).astype(BF16)

    def drain(self):
        for copy in self.copies:
            copy.wait_send()


def reduce_kernel(
    factor,
    h1, gp, mixed, grb, h2, gu, act, cot, gains,
    o_qkv, o_out, o_up, o_down, o_g1, o_g2,
    b_h1, b_gp, b_mixed, b_grb, b_h2, b_gu, b_act, b_cot,
    down32, buf, relay_a, fin_a, relay_b, fin_b, a1, b1, relay_a2, fin_a2, relay_b2, fin_b2,
    zbuf, zrecv, gath,
    ss_core, rs_core, ss_ring, rs_ring, ss_z, rs_z, ss_g, rs_g,
):
    x, z, y_hi, y_lo, core = places()
    y = y_hi * 2 + y_lo
    barrier = pltpu.get_barrier_semaphore()
    peers = [
        device(x, z, y_hi, y_lo, 1 - core),
        device(x, z, y_hi, 1 - y_lo, core),
        device(x, z, y_hi, 1 - y_lo, 1 - core),
        device(x, z, 1 - y_hi, 1 - y_lo, core),
        device((x + 1) % 4, z, y_hi, y_lo, core),
        device((x + 3) % 4, z, y_hi, y_lo, core),
    ] + [device(x, (z + d) % 8, y_hi, y_lo, core) for d in range(1, 8)]
    for peer in peers:
        pl.semaphore_signal(barrier, inc=1, device_id=peer, device_id_type=MESH)
    pl.semaphore_wait(barrier, len(peers))

    other = device(x, z, y_hi, y_lo, 1 - core)
    wide = ((h2, b_h2, 0), (gu, b_gu, 1024), (act, b_act, 0), (cot, b_cot, 256), (mixed, b_mixed, 0),
            (grb, b_grb, 256), (h1, b_h1, 0), (gp, b_gp, 768))
    core_copies = []
    for n, (src, dst, half) in enumerate(wide):
        if half:
            there = src.at[:, pl.ds(pl.multiple_of((1 - core) * half, 128), half)]
        else:
            there = src
        copy = pltpu.make_async_remote_copy(
            src_ref=there,
            dst_ref=dst.at[pl.ds(128, 128)],
            send_sem=ss_core.at[n],
            recv_sem=rs_core.at[n],
            device_id=other,
            device_id_type=MESH,
        )
        copy.start()
        core_copies.append(copy)
    for src, dst, half in wide:
        if half:
            dst[0:128, :] = src[:, pl.ds(pl.multiple_of(core * half, 128), half)]
        else:
            dst[0:128, :] = src[...]
    for copy in core_copies:
        copy.wait_recv()

    def product(a, b):
        return lax.dot_general(a, b, (((0,), (0,)), ((), ())), preferred_element_type=F32)

    def put(at, upper, lower):
        width = upper.shape[-1]
        both = jnp.concatenate([upper, lower], axis=1).astype(BF16)
        buf[:, :, :, :, at : at + width] = both.reshape(4, 8, 2, 16, width)

    down32[...] = product(b_act[...], b_cot[...]).reshape(64, 32, 256)
    for i in range(4):
        lower = product(b_h2[...], b_gu[:, 256 * i : 256 * i + 256]).reshape(64, 8, 256)
        if i < 3:
            upper = product(b_h1[...], b_gp[:, 256 * i : 256 * i + 256]).reshape(64, 8, 256)
        else:
            upper = product(b_mixed[...], b_grb[...]).reshape(64, 8, 256)
        put(256 * i if i < 3 else PART, upper, lower)
    put(PART + 256, down32[:, 0:8, :], down32[:, 16:24, :])
    put(PART + 512, down32[:, 8:16, :], down32[:, 24:32, :])
    buf[:, :, :, :, 768:PART] = gains[...].reshape(4, 8, 2, 16, 128)
    buf[:, :, :, :, WIDE - 128 : WIDE] = jnp.zeros((4, 8, 2, 16, 128), BF16)

    def lanes(lo):
        return pl.ds(pl.multiple_of(lo * PART, 128), PART)

    def dev_x(i):
        return device(i, z, y_hi, y_lo, core)

    def dev_y(i):
        return device(x, z, i // 2, i % 2, core)

    def dev_z(i):
        return device(x, i, y_hi, y_lo, core)

    ring_a = Ring(x, dev_x, lambda i, h: buf.at[i, pl.ds(2 * h, 2)], relay_a, fin_a, ss_ring.at[0], rs_ring.at[0])
    ring_b = Ring(
        y, dev_y, lambda i, h: buf.at[pl.ds(2 * h, 2), pl.ds(4, 4), i // 2, :, lanes(i % 2)],
        relay_b, fin_b, ss_ring.at[1], rs_ring.at[1],
    )
    ring_a2 = Ring(
        y, dev_y, lambda i, h: a1.at[pl.ds(2 * h, 2), i // 2, :, lanes(i % 2)],
        relay_a2, fin_a2, ss_ring.at[2], rs_ring.at[2],
    )
    ring_b2 = Ring(x, dev_x, lambda i, h: b1.at[i, pl.ds(2 * h, 2)], relay_b2, fin_b2, ss_ring.at[3], rs_ring.at[3])
    ring_a.start()
    ring_b.start()
    ring_a.middle()
    ring_b.middle()
    ring_a.finish()
    for h in range(2):
        a1[2 * h : 2 * h + 2] = ring_a.result(h)
    ring_a2.start()
    ring_b.finish()
    for h in range(2):
        b1[2 * h : 2 * h + 2] = ring_b.result(h)
    ring_b2.start()
    ring_a2.middle()
    ring_b2.middle()
    ring_a2.finish()
    for h in range(2):
        zbuf[2 * h : 2 * h + 2] = ring_a2.result(h)
    ring_b2.finish()
    for h in range(2):
        zbuf[4 + 2 * h : 6 + 2 * h] = ring_b2.result(h)
    z_copies = []
    for d in range(1, 8):
        to = (z + d) % 8
        copy = pltpu.make_async_remote_copy(
            src_ref=zbuf.at[to],
            dst_ref=zrecv.at[d - 1],
            send_sem=ss_z.at[d - 1],
            recv_sem=rs_z.at[d - 1],
            device_id=dev_z(to),
            device_id_type=MESH,
        )
        copy.start()
        z_copies.append(copy)
    total = zbuf[z].astype(F32)
    for d in range(7):
        z_copies[d].wait_recv()
        total = total + zrecv[d].astype(F32)
    mine = y_lo * 2 + core
    gath[mine] = total.astype(BF16)
    g_copies = []
    for n, (dy, dc) in enumerate(((0, 1), (1, 0), (1, 1))):
        yl, co = (y_lo + dy) % 2, (core + dc) % 2
        copy = pltpu.make_async_remote_copy(
            src_ref=gath.at[mine],
            dst_ref=gath.at[mine],
            send_sem=ss_g.at[n],
            recv_sem=rs_g.at[n],
            device_id=device(x, z, y_hi, yl, co),
            device_id_type=MESH,
        )
        copy.start()
        g_copies.append(copy)
    for copy in g_copies:
        copy.wait_recv()
    g1 = jnp.zeros((8, 128), F32)
    g2 = jnp.zeros((8, 128), F32)
    for c in range(2):
        low = gath[c].astype(F32) * factor
        high = gath[2 + c].astype(F32) * factor
        o_qkv[:, 768 * c : 768 * c + 768] = low[0:8, 0:768]
        o_out[:, 256 * c : 256 * c + 256] = high[0:8, 0:256]
        o_up[:, 1024 * c : 1024 * c + 768] = low[8:16, 0:768]
        o_up[:, 1024 * c + 768 : 1024 * c + 1024] = high[8:16, 0:256]
        at = slice(256 * c, 256 * c + 256)
        o_down[0:8, at] = high[0:8, 256:512]
        o_down[8:16, at] = high[0:8, 512:768]
        o_down[16:24, at] = high[8:16, 256:512]
        o_down[24:32, at] = high[8:16, 512:768]
        g1 = g1 + low[0:8, 768:PART]
        g2 = g2 + low[8:16, 768:PART]
    o_g1[...] = g1
    o_g2[...] = g2
    for copy in core_copies + z_copies + g_copies:
        copy.wait_send()
    for ring in (ring_a, ring_b, ring_a2, ring_b2):
        ring.drain()


def reduce_weights(factor, *arrays):
    vm = pltpu.VMEM
    dma = pltpu.SemaphoreType.DMA
    shapes = ((8, 1536), (8, 512), (8, 2048), (32, 512), (8, 128), (8, 128))
    return pl.pallas_call(
        lambda *refs: reduce_kernel(factor, *refs),
        out_shape=[jax.ShapeDtypeStruct(s, F32) for s in shapes],
        in_specs=[pl.BlockSpec(memory_space=vm)] * 9,
        out_specs=[pl.BlockSpec(memory_space=vm)] * 6,
        scratch_shapes=[
            vm((256, 512), BF16), vm((256, 768), BF16), vm((256, 512), BF16), vm((256, 256), BF16),
            vm((256, 512), BF16), vm((256, 1024), BF16), vm((256, 2048), BF16), vm((256, 256), BF16),
            vm((64, 32, 256), F32),
            vm((4, 8, 2, 16, WIDE), BF16),
            vm((2, 2, 2, 16, WIDE), BF16), vm((4, 2, 2, 16, WIDE), BF16),
            vm((2, 2, 4, 16, PART), BF16), vm((4, 2, 4, 16, PART), BF16),
            vm((4, 2, 16, WIDE), BF16), vm((4, 4, 16, PART), BF16),
            vm((2, 2, 16, PART), BF16), vm((4, 2, 16, PART), BF16),
            vm((2, 2, 16, PART), BF16), vm((4, 2, 16, PART), BF16),
            vm((8, 16, PART), BF16), vm((7, 16, PART), BF16), vm((4, 16, PART), BF16),
            dma((8,)), dma((8,)), dma((4, 6)), dma((4, 6)), dma((7,)), dma((7,)), dma((3,)), dma((3,)),
        ],
        compiler_params=pltpu.CompilerParams(
            collective_id=1, has_side_effects=True, vmem_limit_bytes=40 * 1024 * 1024
        ),
        cost_estimate=pl.CostEstimate(flops=800_000_000, bytes_accessed=4_000_000, transcendentals=0),
    )(*arrays)


def body(tokens, cotangent, w_qkv, w_out, w_up, w_down, gain_attn, gain_mlp):
    depth_dev, height, across, width = tokens.shape[1:]
    count = depth_dev * height * across
    head_size = width // HEADS
    shape = (depth_dev, height, across, HEADS, head_size)
    pencil_shape = (depth_dev, height * across, HEADS // 2, 2 * head_size)
    flat = tokens.reshape(count, width).astype(jnp.float32)
    normed_one, inverse_one, hidden_one = normalize(flat, gain_attn)
    projected = jnp.dot(hidden_one, w_qkv, preferred_element_type=jnp.float32).astype(jnp.bfloat16)
    queries = projected[:, :width].reshape(shape)
    key_rows = projected[:, width : 2 * width].reshape(shape)
    value_rows = projected[:, 2 * width :].reshape(shape)
    query_block = projected[:, :width].reshape(pencil_shape)
    key_block = projected[:, width : 2 * width].reshape(pencil_shape)
    value_block = projected[:, 2 * width :].reshape(pencil_shape)
    pieces = (
        lax.all_to_all(query_block, "slab", split_axis=1, concat_axis=0, tiled=True),
        lax.all_to_all(key_block, "slab", split_axis=1, concat_axis=0, tiled=True),
        lax.all_to_all(value_block, "slab", split_axis=1, concat_axis=0, tiled=True),
    )
    line_out = attend_lines(
        pencil_lines(pieces[0]), pencil_lines(pieces[1]), pencil_lines(pieces[2])
    ).astype(jnp.bfloat16)
    out_z = lax.all_to_all(
        pencil_block(line_out, pieces[0].shape), "slab", split_axis=0, concat_axis=1, tiled=True
    )
    out_x = attend_lines(lines_x(queries), lines_x(key_rows), lines_x(value_rows)).reshape(shape)
    out_y = unlines_y(attend_lines(lines_y(queries), lines_y(key_rows), lines_y(value_rows)), shape)
    mixed = (
        (out_x + out_y + out_z.reshape(shape).astype(jnp.float32))
        .reshape(count, width)
        .astype(jnp.bfloat16)
    )
    residual = (flat + jnp.dot(mixed, w_out, preferred_element_type=jnp.float32)).astype(
        jnp.bfloat16
    )
    normed_two, inverse_two, hidden_two = normalize(residual.astype(jnp.float32), gain_mlp)
    upper = jnp.dot(hidden_two, w_up, preferred_element_type=jnp.float32)
    active = gelu_value(upper).astype(jnp.bfloat16)
    factor = 1.0 / math.sqrt(count * lax.axis_size("slab") * lax.axis_size("case"))
    grad_rows = cotangent.reshape(count, width)
    grad_active = jnp.dot(grad_rows, w_down.T, preferred_element_type=jnp.float32)
    grad_upper = (grad_active * gelu_slope(upper)).astype(jnp.bfloat16)
    grad_hidden_two = jnp.dot(grad_upper, w_up.T, preferred_element_type=jnp.float32)
    total_gain_two = jnp.sum(grad_hidden_two * normed_two, axis=0)
    grad_residual = grad_rows.astype(jnp.float32) + norm_back(
        grad_hidden_two, normed_two, inverse_two, gain_mlp
    )
    grad_res_b = grad_residual.astype(jnp.bfloat16)
    grad_flat = jnp.dot(grad_res_b, w_out.T, preferred_element_type=jnp.float32).astype(
        jnp.bfloat16
    )
    grad_mixed = grad_flat.reshape(shape)
    grad_block = grad_flat.reshape(pencil_shape)
    pieces = pieces + (
        lax.all_to_all(grad_block, "slab", split_axis=1, concat_axis=0, tiled=True),
    )
    line_grads = attend_back(
        pencil_lines(pieces[0]),
        pencil_lines(pieces[1]),
        pencil_lines(pieces[2]),
        pencil_lines(pieces[3]),
    )
    sent_back = tuple(
        (pencil_block(piece.astype(jnp.bfloat16), pieces[0].shape) for piece in line_grads)
    )
    back_z = (
        lax.all_to_all(sent_back[0], "slab", split_axis=0, concat_axis=1, tiled=True),
        lax.all_to_all(sent_back[1], "slab", split_axis=0, concat_axis=1, tiled=True),
        lax.all_to_all(sent_back[2], "slab", split_axis=0, concat_axis=1, tiled=True),
    )
    back_x = attend_back(
        lines_x(queries), lines_x(key_rows), lines_x(value_rows), lines_x(grad_mixed)
    )
    back_y = attend_back(
        lines_y(queries), lines_y(key_rows), lines_y(value_rows), lines_y(grad_mixed)
    )
    columns = []
    for which in range(3):
        part_x = back_x[which].reshape(shape)
        part_y = unlines_y(back_y[which], shape)
        columns.append(
            (part_x + part_y).reshape(count, width)
            + back_z[which].reshape(count, width).astype(jnp.float32)
        )
    grad_proj = jnp.concatenate(columns, axis=1).astype(jnp.bfloat16)
    grad_hidden_one = jnp.dot(grad_proj, w_qkv.T, preferred_element_type=jnp.float32)
    total_gain_one = jnp.sum(grad_hidden_one * normed_one, axis=0)
    grad_tokens = (
        grad_residual + norm_back(grad_hidden_one, normed_one, inverse_one, gain_attn)
    ).astype(jnp.bfloat16)
    gains = jnp.concatenate(
        [total_gain_one.reshape(64, 8, 1), total_gain_two.reshape(64, 8, 1)], axis=1
    )
    gains = jnp.broadcast_to(gains, (64, 16, 128)).astype(jnp.bfloat16)
    sums = reduce_weights(
        factor, hidden_one, grad_proj, mixed, grad_res_b, hidden_two, grad_upper, active, grad_rows, gains
    )
    return (
        grad_tokens.reshape(tokens.shape),
        sums[0],
        sums[1],
        sums[2],
        sums[3],
        sums[4][:, 0],
        sums[5][:, 0],
    )


def solution(mesh):
    placed = (
        P("case", "slab", None, None, None),
        P("case", "slab", None, None, None),
        P(),
        P(),
        P(),
        P(),
        P(),
        P(),
    )
    return jax.shard_map(
        body,
        mesh=mesh,
        in_specs=placed,
        out_specs=(
            P("case", "slab", None, None, None),
            P("slab", None),
            P("slab", None),
            P("slab", None),
            P("slab", None),
            P("slab"),
            P("slab"),
        ),
        check_vma=False,
    )
```

```python
import functools
import math
import types

import jax
import jax.numpy as jnp
from jax import lax
from jax.experimental import pallas as pl
from jax.experimental.pallas import tpu as pltpu
from jax.sharding import PartitionSpec as P

MESH = pl.DeviceIdType.MESH
F32 = jnp.float32
BF16 = jnp.bfloat16
EPSILON = 1e-06
ROOT = math.sqrt(2.0 / math.pi)
LOWEST = -1e30
SLABS = 64


def places():
    slab, case = lax.axis_index("slab"), lax.axis_index("case")
    return slab // 16, (slab // 2) % 8, slab % 2, case // 2, case % 2


def device(x, z, y_hi, y_lo, core):
    return ((x * 8 + z) * 2 + y_hi, y_lo * 2 + core)


def remote(src, dst, send_sem, recv_sem, to):
    copy = pltpu.make_async_remote_copy(
        src_ref=src, dst_ref=dst, send_sem=send_sem, recv_sem=recv_sem, device_id=to, device_id_type=MESH
    )
    copy.start()
    return copy


def nn(a, b):
    return lax.dot_general(a, b, (((1,), (0,)), ((), ())), preferred_element_type=F32)


def nt(a, b):
    return lax.dot_general(a, b, (((1,), (1,)), ((), ())), preferred_element_type=F32)


def tn(a, b):
    return lax.dot_general(a, b, (((0,), (0,)), ((), ())), preferred_element_type=F32)


def to_rows(grid):
    first, second = grid[0], grid[1]
    low = lax.broadcasted_iota(jnp.int32, first.shape, 1) < 4
    even = jnp.where(low, first, pltpu.roll(second, 4, 1))
    odd = jnp.where(low, pltpu.roll(first, 4, 1), second)
    return jnp.stack([even, odd], axis=1).reshape(128, first.shape[-1])


def to_grid(rows):
    split = rows.reshape(8, 2, 8, rows.shape[-1])
    even, odd = split[:, 0], split[:, 1]
    low = lax.broadcasted_iota(jnp.int32, even.shape, 1) < 4
    first = jnp.where(low, even, pltpu.roll(odd, 4, 1))
    second = jnp.where(low, pltpu.roll(even, 4, 1), odd)
    return first, second


def norm_stats(values):
    inverse = lax.rsqrt(jnp.mean(values * values, axis=-1, keepdims=True) + EPSILON)
    return values * inverse, inverse


def norm_back(grad_normed, normed, inverse, gain):
    scaled = grad_normed * gain
    return inverse * (scaled - normed * jnp.mean(scaled * normed, axis=-1, keepdims=True))


def two_heads(pair):
    lane = lax.broadcasted_iota(jnp.int32, (128, 128), 1)
    first = jnp.where(lane < 64, 1.0, 0.0).astype(BF16)
    second = jnp.where(lane < 64, 0.0, 1.0).astype(BF16)
    return jnp.concatenate([pair * first, pair * second], axis=0)


def over_keys(across):
    return jnp.concatenate([across[:, 0:128], across[:, 128:256]], axis=0)


def line_probs(scores, mask):
    if mask is not None:
        scores = jnp.where(mask, scores, LOWEST)
    weights = jnp.exp(scores - jnp.max(scores, axis=0, keepdims=True))
    return weights * (1.0 / jnp.sum(weights, axis=0, keepdims=True))


def line_masks():
    keys = lax.broadcasted_iota(jnp.int32, (128, 256), 0)
    queries = lax.broadcasted_iota(jnp.int32, (128, 256), 1) & 127
    apart = keys ^ queries
    return (apart & 0x74) == 0, (apart & 0x0F) == 0


def pair_scores(queries, keys):
    return nt(keys, two_heads(queries * jnp.array(0.125, BF16)))


def pair_out(probs, values):
    return tn(over_keys(probs), two_heads(values))


def score_grads(probs, grad_probs):
    return probs * (grad_probs - jnp.sum(probs * grad_probs, axis=0, keepdims=True))


def pair_back(rounded, grad_scores, queries, keys, grads):
    both = two_heads(grads)
    grad_values = nn(rounded, both)
    grad_keys = nn(grad_scores, two_heads(queries * jnp.array(0.125, BF16)))
    grad_queries = tn(over_keys(grad_scores), two_heads(keys)) * 0.125
    return grad_queries, grad_keys, grad_values


class Ring:
    def __init__(self, me, dev, part, relay, fin, ss, rs):
        self.me, self.dev, self.part, self.relay, self.fin, self.ss, self.rs = me, dev, part, relay, fin, ss, rs
        self.right, self.left, self.over = (me + 1) % 4, (me + 3) % 4, (me + 2) % 4
        self.copies = []

    def send(self, src, dst, to):
        n = len(self.copies)
        self.copies.append(remote(src, dst, self.ss.at[n], self.rs.at[n], self.dev(to)))

    def start(self):
        self.send(self.part(self.over, 0), self.relay.at[0], self.right)
        self.send(self.part(self.over, 1), self.relay.at[1], self.left)
        self.send(self.part(self.right, 1), self.fin.at[1], self.right)
        self.send(self.part(self.left, 0), self.fin.at[2], self.left)

    def middle(self):
        for h, to, slot in ((0, self.right, 0), (1, self.left, 3)):
            self.copies[h].wait_recv()
            ref = self.part(to, h)
            ref[...] = (ref[...].astype(F32) + self.relay[h].astype(F32)).astype(BF16)
            self.send(ref, self.fin.at[slot], to)

    def finish(self):
        for copy in self.copies[2:]:
            copy.wait_recv()

    def result(self, h):
        a, b = (0, 2) if h == 0 else (1, 3)
        own = self.part(self.me, h)[...].astype(F32)
        return (own + self.fin[a].astype(F32) + self.fin[b].astype(F32)).astype(BF16)

    def drain(self):
        for copy in self.copies:
            copy.wait_send()


def sum_shapes(wide):
    vm, dma, part = pltpu.VMEM, pltpu.SemaphoreType.DMA, wide // 2
    return dict(
        buf=vm((4, 8, 2, 16, wide), BF16),
        relay_a=vm((2, 2, 2, 16, wide), BF16), fin_a=vm((4, 2, 2, 16, wide), BF16),
        relay_b=vm((2, 2, 4, 16, part), BF16), fin_b=vm((4, 2, 4, 16, part), BF16),
        a1=vm((4, 2, 16, wide), BF16), b1=vm((4, 4, 16, part), BF16),
        relay_a2=vm((2, 2, 16, part), BF16), fin_a2=vm((4, 2, 16, part), BF16),
        relay_b2=vm((2, 2, 16, part), BF16), fin_b2=vm((4, 2, 16, part), BF16),
        zbuf=vm((8, 16, part), BF16), zrecv=vm((7, 16, part), BF16), gath=vm((4, 16, part), BF16),
        ss_ring=dma((4, 6)), rs_ring=dma((4, 6)), ss_z=dma((7,)), rs_z=dma((7,)), ss_g=dma((3,)), rs_g=dma((3,)),
    )


class Sum:
    def __init__(self, ref):
        self.ref = ref
        x, z, y_hi, y_lo, core = places()
        self.place = (x, z, y_hi, y_lo, core)
        y = y_hi * 2 + y_lo
        part = ref.zbuf.shape[-1]

        def lanes(lo):
            return pl.ds(pl.multiple_of(lo * part, 128), part)

        def dev_x(i):
            return device(i, z, y_hi, y_lo, core)

        def dev_y(i):
            return device(x, z, i // 2, i % 2, core)

        sems = [(ref.ss_ring.at[i], ref.rs_ring.at[i]) for i in range(4)]
        self.a = Ring(x, dev_x, lambda i, h: ref.buf.at[i, pl.ds(2 * h, 2)], ref.relay_a, ref.fin_a, *sems[0])
        self.b = Ring(
            y, dev_y, lambda i, h: ref.buf.at[pl.ds(2 * h, 2), pl.ds(4, 4), i // 2, :, lanes(i % 2)],
            ref.relay_b, ref.fin_b, *sems[1],
        )
        self.a2 = Ring(
            y, dev_y, lambda i, h: ref.a1.at[pl.ds(2 * h, 2), i // 2, :, lanes(i % 2)],
            ref.relay_a2, ref.fin_a2, *sems[2],
        )
        self.b2 = Ring(x, dev_x, lambda i, h: ref.b1.at[i, pl.ds(2 * h, 2)], ref.relay_b2, ref.fin_b2, *sems[3])
        self.copies = []

    def put(self, at, upper, lower):
        width = upper.shape[-1]
        both = jnp.concatenate([upper, lower], axis=1).astype(BF16)
        self.ref.buf[:, :, :, :, at : at + width] = both.reshape(4, 8, 2, 16, width)

    def start(self):
        self.a.start()
        self.b.start()

    def middle(self):
        self.a.middle()
        self.b.middle()

    def second(self):
        self.a.finish()
        for h in range(2):
            self.ref.a1[2 * h : 2 * h + 2] = self.a.result(h)
        self.a2.start()
        self.b.finish()
        for h in range(2):
            self.ref.b1[2 * h : 2 * h + 2] = self.b.result(h)
        self.b2.start()

    def second_middle(self):
        self.a2.middle()
        self.b2.middle()

    def along_z(self):
        ref = self.ref
        x, z, y_hi, y_lo, core = self.place
        self.a2.finish()
        for h in range(2):
            ref.zbuf[2 * h : 2 * h + 2] = self.a2.result(h)
        self.b2.finish()
        for h in range(2):
            ref.zbuf[4 + 2 * h : 6 + 2 * h] = self.b2.result(h)
        for d in range(1, 8):
            to = (z + d) % 8
            self.copies.append(
                remote(ref.zbuf.at[to], ref.zrecv.at[d - 1], ref.ss_z.at[d - 1], ref.rs_z.at[d - 1],
                       device(x, to, y_hi, y_lo, core))
            )

    def gather(self):
        ref = self.ref
        x, z, y_hi, y_lo, core = self.place
        total = ref.zbuf[z].astype(F32)
        for d in range(7):
            self.copies[d].wait_recv()
            total = total + ref.zrecv[d].astype(F32)
        mine = y_lo * 2 + core
        ref.gath[mine] = total.astype(BF16)
        for n, (dy, dc) in enumerate(((0, 1), (1, 0), (1, 1))):
            to = device(x, z, y_hi, (y_lo + dy) % 2, (core + dc) % 2)
            self.copies.append(remote(ref.gath.at[mine], ref.gath.at[mine], ref.ss_g.at[n], ref.rs_g.at[n], to))

    def finish(self):
        for copy in self.copies[7:]:
            copy.wait_recv()
        gath = self.ref.gath
        return [jnp.concatenate([gath[c].astype(F32), gath[2 + c].astype(F32)], axis=1) for c in range(2)]

    def drain(self):
        for copy in self.copies:
            copy.wait_send()
        for ring in (self.a, self.b, self.a2, self.b2):
            ring.drain()


class Exchange:
    def __init__(self, send, recv, ss, rs):
        self.send, self.recv, self.ss, self.rs = send, recv, ss, rs

    def start(self):
        me, case = lax.axis_index("slab"), lax.axis_index("case")

        def one(d, carry):
            to = (me + d) % SLABS
            remote(self.send.at[to], self.recv.at[me], self.ss, self.rs, (to, case))
            return carry

        lax.fori_loop(1, SLABS, one, 0)
        self.recv[me] = self.send[me]

    def wait(self):
        got = self.recv.at[pl.ds(0, SLABS - 1)]
        pltpu.make_async_copy(got, got, self.rs).wait()

    def drain(self):
        sent = self.send.at[pl.ds(0, SLABS - 1)]
        pltpu.make_async_copy(sent, sent, self.ss).wait()


def by_pair(blocks):
    width = blocks[0].shape[-1]
    return jnp.stack([b.reshape(16, 8, width) for b in blocks], axis=1).reshape(SLABS, 8, width)


def scratch():
    vm, dma = pltpu.VMEM, pltpu.SemaphoreType.DMA
    return dict(
        wq=vm((512, 1536), BF16), wo=vm((512, 512), BF16), wu=vm((512, 2048), BF16), wd=vm((2048, 512), BF16),
        sw=dma((4,)),
        qkv=vm((128, 1536), BF16),
        qsend=vm((SLABS, 8, 384), BF16), qrecv=vm((SLABS, 8, 384), BF16),
        osend=vm((SLABS, 8, 128), BF16), orecv=vm((SLABS, 8, 128), BF16),
        gsend=vm((SLABS, 8, 128), BF16), grecv=vm((SLABS, 8, 128), BF16),
        dsend=vm((SLABS, 8, 384), BF16), drecv=vm((SLABS, 8, 384), BF16),
        ss_x=dma((4,)), rs_x=dma((4,)),
        z32=vm((3, 512, 128), F32), o32=vm((512, 128), F32), g32=vm((512, 128), F32), d32=vm((3, 512, 128), F32),
        px=vm((4, 128, 256), F32), py=vm((4, 128, 256), F32), pz=vm((4, 128, 256), F32),
        oxy=vm((128, 512), F32), dxy=vm((128, 1536), F32), gmix=vm((128, 512), BF16),
        gact=vm((128, 2048), F32), flat=vm((128, 512), F32), gres=vm((128, 512), F32),
        b_h1=vm((256, 512), BF16), b_mixed=vm((256, 512), BF16), b_h2=vm((256, 512), BF16), b_act=vm((256, 2048), BF16),
        cot=vm((128, 512), BF16), gu=vm((128, 2048), BF16), grb=vm((128, 512), BF16), gp=vm((128, 1536), BF16),
        b_cot=vm((256, 256), BF16), b_gu=vm((256, 1024), BF16), b_grb=vm((256, 256), BF16), b_gp=vm((256, 768), BF16),
        ss_core=dma((8,)), rs_core=dma((8,)),
        down32=vm((SLABS, 32, 256), F32), gain32=vm((SLABS, 8, 128), F32),
        one=sum_shapes(1280), two=sum_shapes(512),
    )


def kernel(factor, tree, tok, cot, wq_h, wo_h, wu_h, wd_h, ga, gm, o_tok, o_qkv, o_out, o_up, o_down, o_g1, o_g2, *refs):
    r = jax.tree.unflatten(tree, refs)
    r, r_one, r_two = types.SimpleNamespace(**r), types.SimpleNamespace(**r["one"]), types.SimpleNamespace(**r["two"])
    x, z, y_hi, y_lo, core = places()
    slab, case = lax.axis_index("slab"), lax.axis_index("case")
    other = device(x, z, y_hi, y_lo, 1 - core)

    loads = [
        pltpu.make_async_copy(src, dst, r.sw.at[n])
        for n, (src, dst) in enumerate(((wq_h, r.wq), (wo_h, r.wo), (wd_h, r.wd), (wu_h, r.wu)))
    ]
    for load in loads:
        load.start()

    barrier = pltpu.get_barrier_semaphore()

    def greet(d, carry):
        pl.semaphore_signal(barrier, inc=1, device_id=((slab + d) % SLABS, case), device_id_type=MESH)
        return carry

    lax.fori_loop(1, SLABS, greet, 0)
    for peer in (
        other,
        device(x, z, y_hi, 1 - y_lo, core),
        device(x, z, y_hi, 1 - y_lo, 1 - core),
        device(x, z, 1 - y_hi, 1 - y_lo, core),
    ):
        pl.semaphore_signal(barrier, inc=1, device_id=peer, device_id_type=MESH)

    gain_one, gain_two = ga[...], gm[...]
    r.flat[...] = to_rows(tok[...].astype(F32))
    normed_one, inverse_one = norm_stats(r.flat[...])
    r.b_h1[0:128, :] = (normed_one * gain_one).astype(BF16)
    r.cot[...] = to_rows(cot[...].astype(F32)).astype(BF16)
    loads[0].wait()
    for i in range(3):
        r.qkv[:, 512 * i : 512 * i + 512] = nn(r.b_h1[0:128, :], r.wq[:, 512 * i : 512 * i + 512]).astype(BF16)
    for i in range(3):
        r.qsend[:, :, 128 * i : 128 * i + 128] = by_pair(
            [r.qkv[:, 512 * i + 128 * j : 512 * i + 128 * j + 128].astype(F32) for j in range(4)]
        ).astype(BF16)
    pl.semaphore_wait(barrier, SLABS + 3)
    ex_q = Exchange(r.qsend, r.qrecv, r.ss_x.at[0], r.rs_x.at[0])
    ex_o = Exchange(r.osend, r.orecv, r.ss_x.at[1], r.rs_x.at[1])
    ex_g = Exchange(r.gsend, r.grecv, r.ss_x.at[2], r.rs_x.at[2])
    ex_d = Exchange(r.dsend, r.drecv, r.ss_x.at[3], r.rs_x.at[3])
    ex_q.start()

    core_copies = []

    def to_core_full(ref):
        n = len(core_copies)
        core_copies.append(
            remote(ref.at[pl.ds(0, 128)], ref.at[pl.ds(128, 128)], r.ss_core.at[n], r.rs_core.at[n], other)
        )

    def to_core_half(src, dst):
        n, half = len(core_copies), dst.shape[-1]
        theirs = src.at[:, pl.ds(pl.multiple_of((1 - core) * half, 128), half)]
        core_copies.append(remote(theirs, dst.at[pl.ds(128, 128)], r.ss_core.at[n], r.rs_core.at[n], other))
        dst[0:128, :] = src[:, pl.ds(pl.multiple_of(core * half, 128), half)]

    to_core_full(r.b_h1)
    to_core_half(r.cot, r.b_cot)

    def pair(j):
        return [r.qkv[:, 512 * i + 128 * j : 512 * i + 128 * j + 128] for i in range(3)]

    mask_x, mask_y = line_masks()
    for j in range(4):
        queries, keys, values = pair(j)
        scores = pair_scores(queries, keys)
        r.px[j] = line_probs(scores, mask_x)
        r.py[j] = line_probs(scores, mask_y)
        r.oxy[:, 128 * j : 128 * j + 128] = pair_out((r.px[j] + r.py[j]).astype(BF16), values)

    ex_q.wait()
    for i in range(3):
        r.z32[i] = r.qrecv[:, :, 128 * i : 128 * i + 128].astype(F32).reshape(512, 128)

    def line(j):
        return [r.z32[i, pl.ds(j, 128, stride=4), :].astype(BF16) for i in range(3)]

    for j in range(4):
        queries, keys, values = line(j)
        probs = line_probs(pair_scores(queries, keys), None)
        r.pz[j] = probs
        r.o32[pl.ds(j, 128, stride=4), :] = pair_out(probs.astype(BF16), values)
    r.osend[...] = r.o32[...].reshape(SLABS, 8, 128).astype(BF16)
    ex_o.start()
    loads[2].wait()
    for i in range(4):
        at = slice(512 * i, 512 * i + 512)
        r.gact[:, at] = nt(r.cot[...], r.wd[at, :])

    loads[1].wait()
    loads[3].wait()
    ex_o.wait()
    from_z = r.orecv[...].astype(F32).reshape(16, 4, 8, 128)
    for j in range(4):
        at = slice(128 * j, 128 * j + 128)
        r.b_mixed[0:128, at] = (r.oxy[:, at] + from_z[:, j].reshape(128, 128)).astype(BF16)
    residual = (r.flat[...] + nn(r.b_mixed[0:128, :], r.wo[...])).astype(BF16)
    normed_two, inverse_two = norm_stats(residual.astype(F32))
    r.b_h2[0:128, :] = (normed_two * gain_two).astype(BF16)
    grad_hidden_two = jnp.zeros((128, 512), F32)
    for i in range(4):
        at = slice(512 * i, 512 * i + 512)
        u = nn(r.b_h2[0:128, :], r.wu[:, at])
        square = u * u
        tangent = jnp.tanh(ROOT * u * (1.0 + 0.044715 * square))
        half = 0.5 * (1.0 + tangent)
        r.b_act[0:128, at] = (u * half).astype(BF16)
        slope = half + 0.5 * u * (1.0 - tangent * tangent) * ROOT * (1.0 + 3.0 * 0.044715 * square)
        r.gu[:, at] = (r.gact[:, at] * slope).astype(BF16)
        grad_hidden_two = grad_hidden_two + nt(r.gu[:, at], r.wu[:, at])
    r.gres[...] = r.cot[...].astype(F32) + norm_back(grad_hidden_two, normed_two, inverse_two, gain_two)
    r.grb[...] = r.gres[...].astype(BF16)
    r.gmix[...] = nt(r.grb[...], r.wo[...]).astype(BF16)
    r.gsend[...] = by_pair([r.gmix[:, 128 * j : 128 * j + 128].astype(F32) for j in range(4)]).astype(BF16)
    ex_g.start()
    to_core_full(r.b_act)
    to_core_half(r.gu, r.b_gu)
    to_core_full(r.b_h2)
    to_core_full(r.b_mixed)
    to_core_half(r.grb, r.b_grb)
    ones = jnp.ones((128, 128), BF16)
    r.gain32[...] = tn((grad_hidden_two * normed_two).astype(BF16), ones).reshape(SLABS, 8, 128)

    one, two = Sum(r_one), Sum(r_two)
    for copy in core_copies:
        copy.wait_recv()
    r.down32[...] = tn(r.b_act[...], r.b_cot[...]).reshape(SLABS, 32, 256)
    for i in range(2):
        one.put(
            256 * i,
            tn(r.b_h2[...], r.b_gu[:, 256 * i : 256 * i + 256]).reshape(SLABS, 8, 256),
            tn(r.b_h2[...], r.b_gu[:, 512 + 256 * i : 768 + 256 * i]).reshape(SLABS, 8, 256),
        )
    one.put(512, r.down32[:, 0:8, :], r.down32[:, 16:24, :])
    one.put(768, r.down32[:, 8:16, :], r.down32[:, 24:32, :])
    upper = tn(r.b_mixed[...], r.b_grb[...]).reshape(SLABS, 8, 256)
    one.put(1024, upper[:, :, 0:128], r.gain32[...])
    one.put(1152, upper[:, :, 128:256], jnp.zeros((SLABS, 8, 128), F32))
    one.start()

    ex_g.wait()
    r.g32[...] = r.grecv[...].astype(F32).reshape(512, 128)
    for j in range(4):
        queries, keys, values = line(j)
        grads = r.g32[pl.ds(j, 128, stride=4), :].astype(BF16)
        probs = r.pz[j]
        grad_scores = score_grads(probs, nt(values, two_heads(grads))).astype(BF16)
        back = pair_back(probs.astype(BF16), grad_scores, queries, keys, grads)
        for i in range(3):
            r.d32[i, pl.ds(j, 128, stride=4), :] = back[i]
    for i in range(3):
        r.dsend[:, :, 128 * i : 128 * i + 128] = r.d32[i].reshape(SLABS, 8, 128).astype(BF16)
    ex_d.start()

    for j in range(4):
        queries, keys, values = pair(j)
        grads = r.gmix[:, 128 * j : 128 * j + 128]
        grad_probs = nt(values, two_heads(grads))
        probs_x, probs_y = r.px[j], r.py[j]
        grad_scores = (score_grads(probs_x, grad_probs) + score_grads(probs_y, grad_probs)).astype(BF16)
        back = pair_back((probs_x + probs_y).astype(BF16), grad_scores, queries, keys, grads)
        for i in range(3):
            r.dxy[:, 512 * i + 128 * j : 512 * i + 128 * j + 128] = back[i]

    one.middle()

    ex_d.wait()
    for i in range(3):
        from_z = r.drecv[:, :, 128 * i : 128 * i + 128].astype(F32).reshape(16, 4, 8, 128)
        for j in range(4):
            at = slice(512 * i + 128 * j, 512 * i + 128 * j + 128)
            r.gp[:, at] = (r.dxy[:, at] + from_z[:, j].reshape(128, 128)).astype(BF16)
    to_core_half(r.gp, r.b_gp)
    grad_hidden_one = nt(r.gp[...], r.wq[...])
    normed_one, inverse_one = norm_stats(r.flat[...])
    first, second = to_grid(r.gres[...] + norm_back(grad_hidden_one, normed_one, inverse_one, gain_one))
    o_tok[0] = first.astype(BF16)
    o_tok[1] = second.astype(BF16)
    gains = tn((grad_hidden_one * normed_one).astype(BF16), ones).reshape(SLABS, 8, 128)
    one.second()
    core_copies[-1].wait_recv()
    parts = [tn(r.b_h1[...], r.b_gp[:, 256 * i : 256 * i + 256]).reshape(SLABS, 8, 256) for i in range(3)]
    two.put(0, parts[0], parts[2])
    two.put(256, parts[1][:, :, 0:128], gains)
    two.put(384, parts[1][:, :, 128:256], jnp.zeros((SLABS, 8, 128), F32))
    two.start()
    one.second_middle()
    two.middle()
    one.along_z()
    two.second()
    one.gather()
    two.second_middle()
    two.along_z()
    gain = jnp.zeros((8, 128), F32)
    for c, full in enumerate(one.finish()):
        full = full * factor
        o_up[:, 1024 * c : 1024 * c + 512] = full[0:8, 0:512]
        o_up[:, 1024 * c + 512 : 1024 * c + 1024] = full[8:16, 0:512]
        at = slice(256 * c, 256 * c + 256)
        o_down[0:8, at] = full[0:8, 512:768]
        o_down[8:16, at] = full[0:8, 768:1024]
        o_down[16:24, at] = full[8:16, 512:768]
        o_down[24:32, at] = full[8:16, 768:1024]
        o_out[:, at] = full[0:8, 1024:1280]
        gain = gain + full[8:16, 1024:1152]
    o_g2[...] = gain
    two.gather()
    gain = jnp.zeros((8, 128), F32)
    for c, full in enumerate(two.finish()):
        full = full * factor
        o_qkv[:, 768 * c : 768 * c + 512] = full[0:8, 0:512]
        o_qkv[:, 768 * c + 512 : 768 * c + 768] = full[8:16, 0:256]
        gain = gain + full[8:16, 256:384]
    o_g1[...] = gain

    for exchange in (ex_q, ex_o, ex_g, ex_d):
        exchange.drain()
    for copy in core_copies:
        copy.wait_send()
    one.drain()
    two.drain()


def body(tokens, cotangent, w_qkv, w_out, w_up, w_down, gain_attn, gain_mlp):
    width = tokens.shape[-1]
    factor = 1.0 / math.sqrt(128 * lax.axis_size("slab") * lax.axis_size("case"))
    shapes = scratch()
    leaves, tree = jax.tree.flatten(shapes)
    vmem, any_space = pl.BlockSpec(memory_space=pltpu.VMEM), pl.BlockSpec(memory_space=pl.ANY)
    outs = ((8, 1536), (8, 512), (8, 2048), (32, 512), (8, 128), (8, 128))
    result = pl.pallas_call(
        functools.partial(kernel, factor, tree),
        out_shape=[jax.ShapeDtypeStruct((2, 8, 8, width), BF16)] + [jax.ShapeDtypeStruct(s, F32) for s in outs],
        in_specs=[vmem, vmem] + [any_space] * 4 + [vmem, vmem],
        out_specs=[vmem] * 7,
        scratch_shapes=leaves,
        compiler_params=pltpu.CompilerParams(
            collective_id=1, has_side_effects=True, vmem_limit_bytes=56 * 1024 * 1024
        ),
        cost_estimate=pl.CostEstimate(flops=3_500_000_000, bytes_accessed=7_000_000, transcendentals=0),
    )(
        tokens.reshape(2, 8, 8, width),
        cotangent.reshape(2, 8, 8, width),
        w_qkv,
        w_out,
        w_up,
        w_down,
        gain_attn.reshape(1, width),
        gain_mlp.reshape(1, width),
    )
    return (
        result[0].reshape(tokens.shape),
        result[1],
        result[2],
        result[3],
        result[4],
        result[5][:, 0],
        result[6][:, 0],
    )


def solution(mesh):
    grid = P("case", "slab", None, None, None)
    return jax.shard_map(
        body,
        mesh=mesh,
        in_specs=(grid, grid, P(), P(), P(), P(), P(), P()),
        out_specs=(grid, P("slab", None), P("slab", None), P("slab", None), P("slab", None), P("slab"), P("slab")),
        check_vma=False,
    )
```

```python
import functools
import math
import types

import jax
import jax.numpy as jnp
from jax import lax
from jax.experimental import pallas as pl
from jax.experimental.pallas import tpu as pltpu
from jax.sharding import PartitionSpec as P

MESH = pl.DeviceIdType.MESH
F32 = jnp.float32
BF16 = jnp.bfloat16
EPSILON = 1e-06
ROOT = math.sqrt(2.0 / math.pi)
LOWEST = -1e30
SLABS = 64


def places():
    slab, case = lax.axis_index("slab"), lax.axis_index("case")
    return slab // 16, (slab // 2) % 8, slab % 2, case // 2, case % 2


def device(x, z, y_hi, y_lo, core):
    return ((x * 8 + z) * 2 + y_hi, y_lo * 2 + core)


def remote(src, dst, send_sem, recv_sem, to):
    copy = pltpu.make_async_remote_copy(
        src_ref=src, dst_ref=dst, send_sem=send_sem, recv_sem=recv_sem, device_id=to, device_id_type=MESH
    )
    copy.start()
    return copy


def nn(a, b):
    return lax.dot_general(a, b, (((1,), (0,)), ((), ())), preferred_element_type=F32)


def nt(a, b):
    return lax.dot_general(a, b, (((1,), (1,)), ((), ())), preferred_element_type=F32)


def tn(a, b):
    return lax.dot_general(a, b, (((0,), (0,)), ((), ())), preferred_element_type=F32)


def to_rows(grid):
    first, second = grid[0], grid[1]
    low = lax.broadcasted_iota(jnp.int32, first.shape, 1) < 4
    even = jnp.where(low, first, pltpu.roll(second, 4, 1))
    odd = jnp.where(low, pltpu.roll(first, 4, 1), second)
    return jnp.stack([even, odd], axis=1).reshape(128, first.shape[-1])


def to_grid(rows):
    split = rows.reshape(8, 2, 8, rows.shape[-1])
    even, odd = split[:, 0], split[:, 1]
    low = lax.broadcasted_iota(jnp.int32, even.shape, 1) < 4
    first = jnp.where(low, even, pltpu.roll(odd, 4, 1))
    second = jnp.where(low, pltpu.roll(even, 4, 1), odd)
    return first, second


def norm_stats(values):
    inverse = lax.rsqrt(jnp.mean(values * values, axis=-1, keepdims=True) + EPSILON)
    return values * inverse, inverse


def norm_back(grad_normed, normed, inverse, gain):
    scaled = grad_normed * gain
    return inverse * (scaled - normed * jnp.mean(scaled * normed, axis=-1, keepdims=True))


def two_heads(pair):
    lane = lax.broadcasted_iota(jnp.int32, (128, 128), 1)
    first = jnp.where(lane < 64, 1.0, 0.0).astype(BF16)
    second = jnp.where(lane < 64, 0.0, 1.0).astype(BF16)
    return jnp.concatenate([pair * first, pair * second], axis=0)


def over_keys(across):
    return jnp.concatenate([across[:, 0:128], across[:, 128:256]], axis=0)


def line_probs(scores, mask):
    if mask is not None:
        scores = jnp.where(mask, scores, LOWEST)
    weights = jnp.exp(scores - jnp.max(scores, axis=0, keepdims=True))
    return weights * (1.0 / jnp.sum(weights, axis=0, keepdims=True))


def line_masks():
    keys = lax.broadcasted_iota(jnp.int32, (128, 256), 0)
    queries = lax.broadcasted_iota(jnp.int32, (128, 256), 1) & 127
    apart = keys ^ queries
    return (apart & 0x74) == 0, (apart & 0x0F) == 0


def pair_scores(queries, keys):
    return nt(keys, two_heads(queries * jnp.array(0.125, BF16)))


def pair_out(probs, values):
    return tn(over_keys(probs), two_heads(values))


def score_grads(probs, grad_probs):
    return probs * (grad_probs - jnp.sum(probs * grad_probs, axis=0, keepdims=True))


def pair_back(rounded, grad_scores, queries, keys, grads):
    both = two_heads(grads)
    grad_values = nn(rounded, both)
    grad_keys = nn(grad_scores, two_heads(queries * jnp.array(0.125, BF16)))
    grad_queries = tn(over_keys(grad_scores), two_heads(keys)) * 0.125
    return grad_queries, grad_keys, grad_values


class Ring:
    def __init__(self, me, dev, part, relay, fin, ss, rs):
        self.me, self.dev, self.part, self.relay, self.fin, self.ss, self.rs = me, dev, part, relay, fin, ss, rs
        self.right, self.left, self.over = (me + 1) % 4, (me + 3) % 4, (me + 2) % 4
        self.copies = []

    def send(self, src, dst, to):
        n = len(self.copies)
        self.copies.append(remote(src, dst, self.ss.at[n], self.rs.at[n], self.dev(to)))

    def start(self):
        if self.relay is None:
            for n, to in enumerate((self.over, self.right, self.left)):
                for h in range(2):
                    self.send(self.part(to, h), self.fin.at[n, h], to)
            return
        self.send(self.part(self.over, 0), self.relay.at[0], self.right)
        self.send(self.part(self.over, 1), self.relay.at[1], self.left)
        self.send(self.part(self.right, 1), self.fin.at[0, 1], self.right)
        self.send(self.part(self.left, 0), self.fin.at[0, 0], self.left)

    def middle(self):
        for h, to in ((0, self.right), (1, self.left)):
            self.copies[h].wait_recv()
            ref = self.part(to, h)
            ref[...] = (ref[...].astype(F32) + self.relay[h].astype(F32)).astype(BF16)
            self.send(ref, self.fin.at[1, h], to)

    def finish(self):
        for copy in self.copies[0 if self.relay is None else 2 :]:
            copy.wait_recv()

    def result(self, h):
        total = self.part(self.me, h)[...].astype(F32)
        for n in range(3 if self.relay is None else 2):
            total = total + self.fin[n, h].astype(F32)
        return total.astype(BF16)

    def drain(self):
        for copy in self.copies:
            copy.wait_send()


def sum_shapes(wide, relays):
    vm, dma, part = pltpu.VMEM, pltpu.SemaphoreType.DMA, wide // 2
    shapes = dict(
        buf=vm((4, 8, 2, 16, wide), BF16),
        fin_a=vm((3, 2, 2, 2, 16, wide), BF16), fin_b=vm((3, 2, 2, 4, 16, part), BF16),
        a1=vm((4, 2, 16, wide), BF16), b1=vm((4, 4, 16, part), BF16),
        fin_a2=vm((3, 2, 2, 16, part), BF16), fin_b2=vm((3, 2, 2, 16, part), BF16),
        zbuf=vm((8, 16, part), BF16), zrecv=vm((7, 16, part), BF16), gath=vm((4, 16, part), BF16),
        ss_ring=dma((4, 6)), rs_ring=dma((4, 6)), ss_z=dma((7,)), rs_z=dma((7,)), ss_g=dma((3,)), rs_g=dma((3,)),
    )
    if relays:
        shapes.update(relay_a=vm((2, 2, 2, 16, wide), BF16), relay_b=vm((2, 2, 4, 16, part), BF16))
    return shapes


class Sum:
    def __init__(self, ref):
        self.ref = ref
        x, z, y_hi, y_lo, core = places()
        self.place = (x, z, y_hi, y_lo, core)
        y = y_hi * 2 + y_lo
        part = ref.zbuf.shape[-1]

        def lanes(lo):
            return pl.ds(pl.multiple_of(lo * part, 128), part)

        def dev_x(i):
            return device(i, z, y_hi, y_lo, core)

        def dev_y(i):
            return device(x, z, i // 2, i % 2, core)

        sems = [(ref.ss_ring.at[i], ref.rs_ring.at[i]) for i in range(4)]
        relay_a, relay_b = getattr(ref, "relay_a", None), getattr(ref, "relay_b", None)
        self.a = Ring(x, dev_x, lambda i, h: ref.buf.at[i, pl.ds(2 * h, 2)], relay_a, ref.fin_a, *sems[0])
        self.b = Ring(
            y, dev_y, lambda i, h: ref.buf.at[pl.ds(2 * h, 2), pl.ds(4, 4), i // 2, :, lanes(i % 2)],
            relay_b, ref.fin_b, *sems[1],
        )
        self.a2 = Ring(
            y, dev_y, lambda i, h: ref.a1.at[pl.ds(2 * h, 2), i // 2, :, lanes(i % 2)],
            None, ref.fin_a2, *sems[2],
        )
        self.b2 = Ring(x, dev_x, lambda i, h: ref.b1.at[i, pl.ds(2 * h, 2)], None, ref.fin_b2, *sems[3])
        self.copies = []

    def put(self, at, upper, lower):
        width = upper.shape[-1]
        both = jnp.concatenate([upper, lower], axis=1).astype(BF16)
        self.ref.buf[:, :, :, :, at : at + width] = both.reshape(4, 8, 2, 16, width)

    def start(self):
        self.a.start()
        self.b.start()

    def middle(self):
        self.a.middle()
        self.b.middle()

    def second(self):
        self.a.finish()
        for h in range(2):
            self.ref.a1[2 * h : 2 * h + 2] = self.a.result(h)
        self.a2.start()
        self.b.finish()
        for h in range(2):
            self.ref.b1[2 * h : 2 * h + 2] = self.b.result(h)
        self.b2.start()

    def along_z(self):
        ref = self.ref
        x, z, y_hi, y_lo, core = self.place
        self.a2.finish()
        for h in range(2):
            ref.zbuf[2 * h : 2 * h + 2] = self.a2.result(h)
        self.b2.finish()
        for h in range(2):
            ref.zbuf[4 + 2 * h : 6 + 2 * h] = self.b2.result(h)
        for d in range(1, 8):
            to = (z + d) % 8
            self.copies.append(
                remote(ref.zbuf.at[to], ref.zrecv.at[d - 1], ref.ss_z.at[d - 1], ref.rs_z.at[d - 1],
                       device(x, to, y_hi, y_lo, core))
            )

    def gather(self):
        ref = self.ref
        x, z, y_hi, y_lo, core = self.place
        total = ref.zbuf[z].astype(F32)
        for d in range(7):
            self.copies[d].wait_recv()
            total = total + ref.zrecv[d].astype(F32)
        mine = y_lo * 2 + core
        ref.gath[mine] = total.astype(BF16)
        for n, (dy, dc) in enumerate(((0, 1), (1, 0), (1, 1))):
            to = device(x, z, y_hi, (y_lo + dy) % 2, (core + dc) % 2)
            self.copies.append(remote(ref.gath.at[mine], ref.gath.at[mine], ref.ss_g.at[n], ref.rs_g.at[n], to))

    def finish(self):
        for copy in self.copies[7:]:
            copy.wait_recv()
        gath = self.ref.gath
        return [jnp.concatenate([gath[c].astype(F32), gath[2 + c].astype(F32)], axis=1) for c in range(2)]

    def drain(self):
        for copy in self.copies:
            copy.wait_send()
        for ring in (self.a, self.b, self.a2, self.b2):
            ring.drain()


class Exchange:
    def __init__(self, send, recv, ss, rs, shared=1):
        self.send, self.recv, self.ss, self.rs, self.shared = send, recv, ss, rs, shared

    def start(self):
        me = lax.axis_index("slab")
        x, z, y_hi, y_lo, core = places()

        def one(n, carry):
            kz, kx, ky = n // 8, (n // 2) % 4, n % 2
            dz = 4 + ((kz + 1) // 2) * (1 - 2 * (kz % 2))
            dx = 2 + ((kx + 1) // 2) * (1 - 2 * (kx % 2))
            to = device((x + dx) % 4, (z + dz) % 8, (y_hi + 1 - ky) % 2, y_lo, core)
            remote(self.send.at[to[0] // self.shared], self.recv.at[me], self.ss, self.rs, to)
            return carry

        lax.fori_loop(0, SLABS - 1, one, 0)
        self.recv[me] = self.send[me // self.shared]

    def wait(self):
        got = self.recv.at[pl.ds(0, SLABS - 1)]
        pltpu.make_async_copy(got, got, self.rs).wait()

    def drain(self):
        sent = self.recv.at[pl.ds(0, SLABS - 1)]
        pltpu.make_async_copy(sent, sent, self.ss).wait()


def by_pair(blocks):
    width = blocks[0].shape[-1]
    return jnp.stack([b.reshape(16, 8, width) for b in blocks], axis=1).reshape(SLABS, 8, width)


def scratch():
    vm, dma = pltpu.VMEM, pltpu.SemaphoreType.DMA
    return dict(
        wq=vm((512, 1536), BF16), wo=vm((512, 512), BF16), wu=vm((512, 2048), BF16), wd=vm((2048, 512), BF16),
        sw=dma((4,)),
        qkv=vm((128, 1536), BF16),
        qsend=vm((SLABS, 8, 384), BF16), qrecv=vm((SLABS, 8, 384), BF16),
        osend=vm((SLABS, 8, 128), BF16), orecv=vm((SLABS, 8, 128), BF16),
        gsend=vm((SLABS, 8, 128), BF16), grecv=vm((SLABS, 8, 128), BF16),
        dsend=vm((SLABS, 8, 384), BF16), drecv=vm((SLABS, 8, 384), BF16),
        hsend=vm((16, 8, 512), BF16), hrecv=vm((SLABS, 8, 512), BF16),
        ss_x=dma((5,)), rs_x=dma((5,)),
        z32=vm((3, 512, 128), F32), o32=vm((512, 128), F32), g32=vm((512, 128), F32), d32=vm((3, 512, 128), F32),
        px=vm((4, 128, 256), F32), py=vm((4, 128, 256), F32), pz=vm((4, 128, 256), F32),
        oxy=vm((128, 512), F32), dxy=vm((128, 1536), F32), gmix=vm((128, 512), BF16),
        gact=vm((128, 2048), F32), flat=vm((128, 512), F32), gres=vm((128, 512), F32),
        b_h1=vm((256, 512), BF16), b_mixed=vm((256, 512), BF16), b_h2=vm((256, 512), BF16), b_act=vm((256, 2048), BF16),
        cot=vm((128, 512), BF16), gu=vm((128, 2048), BF16), grb=vm((128, 512), BF16), gp=vm((128, 1536), BF16),
        b_cot=vm((256, 256), BF16), b_gu=vm((256, 1024), BF16), b_grb=vm((256, 256), BF16), b_gp=vm((256, 768), BF16),
        ss_core=dma((10,)), rs_core=dma((10,)),
        zpart=vm((512, 384), F32), zpart_b=vm((512, 384), BF16), zpeer=vm((2, 512, 128), BF16),
        down32=vm((SLABS, 32, 256), F32), out32=vm((512, 256), F32), qkv32=vm((512, 768), F32),
        one=sum_shapes(1024, True), two=sum_shapes(512, False),
    )


def kernel(factor, tree, tok, cot, wq_h, wo_h, wu_h, wd_h, ga, gm, o_tok, o_qkv, o_out, o_up, o_down, o_g1, o_g2, *refs):
    r = jax.tree.unflatten(tree, refs)
    r, r_one, r_two = types.SimpleNamespace(**r), types.SimpleNamespace(**r["one"]), types.SimpleNamespace(**r["two"])
    x, z, y_hi, y_lo, core = places()
    slab, case = lax.axis_index("slab"), lax.axis_index("case")
    other = device(x, z, y_hi, y_lo, 1 - core)

    loads = [
        pltpu.make_async_copy(src, dst, r.sw.at[n])
        for n, (src, dst) in enumerate(((wq_h, r.wq), (wo_h, r.wo), (wd_h, r.wd), (wu_h, r.wu)))
    ]
    for load in loads:
        load.start()

    barrier = pltpu.get_barrier_semaphore()

    def greet(d, carry):
        pl.semaphore_signal(barrier, inc=1, device_id=((slab + d) % SLABS, case), device_id_type=MESH)
        return carry

    lax.fori_loop(1, SLABS, greet, 0)
    for peer in (
        other,
        device(x, z, y_hi, 1 - y_lo, core),
        device(x, z, y_hi, 1 - y_lo, 1 - core),
        device(x, z, 1 - y_hi, 1 - y_lo, core),
    ):
        pl.semaphore_signal(barrier, inc=1, device_id=peer, device_id_type=MESH)

    gain_one, gain_two = ga[...], gm[...]
    r.flat[...] = to_rows(tok[...].astype(F32))
    normed_one, inverse_one = norm_stats(r.flat[...])
    hidden_one = normed_one * gain_one
    r.b_h1[0:128, :] = hidden_one.astype(BF16)
    r.hsend[...] = hidden_one.reshape(16, 8, 512).astype(BF16)
    r.cot[...] = to_rows(cot[...].astype(F32)).astype(BF16)
    loads[0].wait()
    for i in range(3):
        r.qkv[:, 512 * i : 512 * i + 512] = nn(r.b_h1[0:128, :], r.wq[:, 512 * i : 512 * i + 512]).astype(BF16)
    for i in range(3):
        r.qsend[:, :, 128 * i : 128 * i + 128] = by_pair(
            [r.qkv[:, 512 * i + 128 * j : 512 * i + 128 * j + 128].astype(F32) for j in range(4)]
        ).astype(BF16)
    pl.semaphore_wait(barrier, SLABS + 3)
    ex_q = Exchange(r.qsend, r.qrecv, r.ss_x.at[0], r.rs_x.at[0])
    ex_o = Exchange(r.osend, r.orecv, r.ss_x.at[1], r.rs_x.at[1])
    ex_g = Exchange(r.gsend, r.grecv, r.ss_x.at[2], r.rs_x.at[2])
    ex_d = Exchange(r.dsend, r.drecv, r.ss_x.at[3], r.rs_x.at[3])
    ex_h = Exchange(r.hsend, r.hrecv, r.ss_x.at[4], r.rs_x.at[4], shared=4)
    ex_q.start()

    core_copies = []

    def to_core_full(ref):
        n = len(core_copies)
        core_copies.append(
            remote(ref.at[pl.ds(0, 128)], ref.at[pl.ds(128, 128)], r.ss_core.at[n], r.rs_core.at[n], other)
        )

    def to_core_half(src, dst):
        n, half = len(core_copies), dst.shape[-1]
        theirs = src.at[:, pl.ds(pl.multiple_of((1 - core) * half, 128), half)]
        core_copies.append(remote(theirs, dst.at[pl.ds(128, 128)], r.ss_core.at[n], r.rs_core.at[n], other))
        dst[0:128, :] = src[:, pl.ds(pl.multiple_of(core * half, 128), half)]

    to_core_full(r.b_h1)
    to_core_half(r.cot, r.b_cot)

    def pair(j):
        return [r.qkv[:, 512 * i + 128 * j : 512 * i + 128 * j + 128] for i in range(3)]

    mask_x, mask_y = line_masks()
    for j in range(4):
        queries, keys, values = pair(j)
        scores = pair_scores(queries, keys)
        r.px[j] = line_probs(scores, mask_x)
        r.py[j] = line_probs(scores, mask_y)
        r.oxy[:, 128 * j : 128 * j + 128] = pair_out((r.px[j] + r.py[j]).astype(BF16), values)

    loads[2].wait()
    for i in range(4):
        at = slice(512 * i, 512 * i + 512)
        r.gact[:, at] = nt(r.cot[...], r.wd[at, :])

    ex_q.wait()
    for i in range(3):
        r.z32[i] = r.qrecv[:, :, 128 * i : 128 * i + 128].astype(F32).reshape(512, 128)

    def line(j):
        return [r.z32[i, pl.ds(j, 128, stride=4), :].astype(BF16) for i in range(3)]

    for j in range(4):
        queries, keys, values = line(j)
        probs = line_probs(pair_scores(queries, keys), None)
        r.pz[j] = probs
        r.o32[pl.ds(j, 128, stride=4), :] = pair_out(probs.astype(BF16), values)
    r.osend[...] = r.o32[...].reshape(SLABS, 8, 128).astype(BF16)
    ex_o.start()
    ex_h.start()

    loads[1].wait()
    loads[3].wait()
    ex_o.wait()
    from_z = r.orecv[...].astype(F32).reshape(16, 4, 8, 128)
    for j in range(4):
        at = slice(128 * j, 128 * j + 128)
        r.b_mixed[0:128, at] = (r.oxy[:, at] + from_z[:, j].reshape(128, 128)).astype(BF16)
    residual = (r.flat[...] + nn(r.b_mixed[0:128, :], r.wo[...])).astype(BF16)
    normed_two, inverse_two = norm_stats(residual.astype(F32))
    r.b_h2[0:128, :] = (normed_two * gain_two).astype(BF16)
    grad_hidden_two = jnp.zeros((128, 512), F32)
    for i in range(4):
        at = slice(512 * i, 512 * i + 512)
        u = nn(r.b_h2[0:128, :], r.wu[:, at])
        square = u * u
        tangent = jnp.tanh(ROOT * u * (1.0 + 0.044715 * square))
        half = 0.5 * (1.0 + tangent)
        r.b_act[0:128, at] = (u * half).astype(BF16)
        slope = half + 0.5 * u * (1.0 - tangent * tangent) * ROOT * (1.0 + 3.0 * 0.044715 * square)
        r.gu[:, at] = (r.gact[:, at] * slope).astype(BF16)
        grad_hidden_two = grad_hidden_two + nt(r.gu[:, at], r.wu[:, at])
    r.gres[...] = r.cot[...].astype(F32) + norm_back(grad_hidden_two, normed_two, inverse_two, gain_two)
    r.grb[...] = r.gres[...].astype(BF16)
    r.gmix[...] = nt(r.grb[...], r.wo[...]).astype(BF16)
    r.gsend[...] = by_pair([r.gmix[:, 128 * j : 128 * j + 128].astype(F32) for j in range(4)]).astype(BF16)
    ex_g.start()
    to_core_full(r.b_act)
    to_core_half(r.gu, r.b_gu)
    to_core_full(r.b_h2)
    to_core_full(r.b_mixed)
    to_core_half(r.grb, r.b_grb)

    for j in range(4):
        queries, keys, values = pair(j)
        grads = r.gmix[:, 128 * j : 128 * j + 128]
        grad_probs = nt(values, two_heads(grads))
        probs_x, probs_y = r.px[j], r.py[j]
        grad_scores = (score_grads(probs_x, grad_probs) + score_grads(probs_y, grad_probs)).astype(BF16)
        back = pair_back((probs_x + probs_y).astype(BF16), grad_scores, queries, keys, grads)
        for i in range(3):
            at = slice(512 * i + 128 * j, 512 * i + 128 * j + 128)
            r.dxy[:, at] = back[i]
            r.gp[:, at] = back[i].astype(BF16)
    to_core_half(r.gp, r.b_gp)

    one, two = Sum(r_one), Sum(r_two)
    for copy in core_copies:
        copy.wait_recv()
    r.down32[...] = tn(r.b_act[...], r.b_cot[...]).reshape(SLABS, 32, 256)
    for i in range(2):
        one.put(
            256 * i,
            tn(r.b_h2[...], r.b_gu[:, 256 * i : 256 * i + 256]).reshape(SLABS, 8, 256),
            tn(r.b_h2[...], r.b_gu[:, 512 + 256 * i : 768 + 256 * i]).reshape(SLABS, 8, 256),
        )
    one.put(512, r.down32[:, 0:8, :], r.down32[:, 16:24, :])
    one.put(768, r.down32[:, 8:16, :], r.down32[:, 24:32, :])
    one.start()
    r.out32[...] = tn(r.b_mixed[...], r.b_grb[...])
    for i in range(3):
        at = slice(256 * i, 256 * i + 256)
        r.qkv32[:, at] = tn(r.b_h1[...], r.b_gp[:, at])

    ex_g.wait()
    r.g32[...] = r.grecv[...].astype(F32).reshape(512, 128)
    for j in range(4):
        queries, keys, values = line(j)
        grads = r.g32[pl.ds(j, 128, stride=4), :].astype(BF16)
        probs = r.pz[j]
        grad_scores = score_grads(probs, nt(values, two_heads(grads))).astype(BF16)
        back = pair_back(probs.astype(BF16), grad_scores, queries, keys, grads)
        for i in range(3):
            r.d32[i, pl.ds(j, 128, stride=4), :] = back[i]

    ex_h.wait()
    hidden_lines = r.hrecv[...].astype(F32).reshape(512, 512).astype(BF16)
    r.zpart[...] = tn(hidden_lines, jnp.concatenate([r.d32[i].astype(BF16) for i in range(3)], axis=1))
    r.zpart_b[...] = r.zpart[...].astype(BF16)

    def outer(owner):
        return pl.ds(pl.multiple_of(owner * 256, 128), 128)

    z_copies = [
        remote(r.zpart_b.at[:, outer(1 - core)], r.zpeer.at[0], r.ss_core.at[8], r.rs_core.at[8], other),
        remote(r.zpart_b.at[:, pl.ds(128, 128)], r.zpeer.at[1], r.ss_core.at[9], r.rs_core.at[9], other),
    ]
    one.middle()
    for i in range(3):
        r.dsend[:, :, 128 * i : 128 * i + 128] = r.d32[i].reshape(SLABS, 8, 128).astype(BF16)
    pair_at = slab % 4
    at_outer = pl.ds(pl.multiple_of(core * 256 + pair_at * 128, 128), 128)
    at_keys = pl.ds(pl.multiple_of((1 - core) * 512 + (pair_at % 2) * 128, 128), 128)
    owned = jnp.where(core == pair_at // 2, 1.0, 0.0)
    z_copies[0].wait_recv()
    r.qkv32[:, at_outer] = r.qkv32[:, at_outer] + (r.zpart[:, outer(core)] + r.zpeer[0].astype(F32))
    z_copies[1].wait_recv()
    r.qkv32[:, at_keys] = r.qkv32[:, at_keys] + owned * (r.zpart[:, 128:256] + r.zpeer[1].astype(F32))

    def rows(ref, at):
        return ref[:, at : at + 256].reshape(SLABS, 8, 256)

    two.put(0, rows(r.qkv32, 0), rows(r.qkv32, 256))
    two.put(256, rows(r.qkv32, 512), rows(r.out32, 0))
    two.start()
    ex_d.start()
    one.second()
    two.second()
    one.along_z()
    two.along_z()

    ex_d.wait()
    for i in range(3):
        from_z = r.drecv[:, :, 128 * i : 128 * i + 128].astype(F32).reshape(16, 4, 8, 128)
        for j in range(4):
            at = slice(512 * i + 128 * j, 512 * i + 128 * j + 128)
            r.dxy[:, at] = r.dxy[:, at] + from_z[:, j].reshape(128, 128)
    grad_hidden_one = nt(r.dxy[...].astype(BF16), r.wq[...])
    normed_one, inverse_one = norm_stats(r.flat[...])
    first, second = to_grid(r.gres[...] + norm_back(grad_hidden_one, normed_one, inverse_one, gain_one))
    o_tok[0] = first.astype(BF16)
    o_tok[1] = second.astype(BF16)

    one.gather()
    two.gather()
    own_rows = pl.ds(pl.multiple_of((slab // 2) * 16, 16), 16)

    def weight_rows(ref):
        both = ref[own_rows, :].astype(F32)
        return jnp.where(slab % 2 == 0, both[0:8], both[8:16])

    for c, full in enumerate(one.finish()):
        full = full * factor
        o_up[:, 1024 * c : 1024 * c + 512] = full[0:8, 0:512]
        o_up[:, 1024 * c + 512 : 1024 * c + 1024] = full[8:16, 0:512]
        at = slice(256 * c, 256 * c + 256)
        o_down[0:8, at] = full[0:8, 512:768]
        o_down[8:16, at] = full[0:8, 768:1024]
        o_down[16:24, at] = full[8:16, 512:768]
        o_down[24:32, at] = full[8:16, 768:1024]
    o_g2[...] = jnp.broadcast_to(jnp.sum(o_up[...] * weight_rows(r.wu), axis=1, keepdims=True), (8, 128))
    for c, full in enumerate(two.finish()):
        full = full * factor
        o_qkv[:, 768 * c : 768 * c + 256] = full[0:8, 0:256]
        o_qkv[:, 768 * c + 256 : 768 * c + 512] = full[8:16, 0:256]
        o_qkv[:, 768 * c + 512 : 768 * c + 768] = full[0:8, 256:512]
        o_out[:, 256 * c : 256 * c + 256] = full[8:16, 256:512]
    o_g1[...] = jnp.broadcast_to(jnp.sum(o_qkv[...] * weight_rows(r.wq), axis=1, keepdims=True), (8, 128))

    for exchange in (ex_q, ex_o, ex_h, ex_g, ex_d):
        exchange.drain()
    for copy in core_copies + z_copies:
        copy.wait_send()
    one.drain()
    two.drain()


def results_kernel(tok, qkv, out, up, down, g1, g2, gain_one, gain_two, o_tok, o_qkv, o_out, o_up, o_down, o_g1, o_g2):
    for src, dst in ((tok, o_tok), (qkv, o_qkv), (out, o_out), (up, o_up), (down, o_down)):
        dst[...] = src[...]
    row = lax.broadcasted_iota(jnp.int32, (8, 128), 0)
    lane = lax.broadcasted_iota(jnp.int32, (8, 128), 1)
    for src, gain, dst in ((g1, gain_one, o_g1), (g2, gain_two, o_g2)):
        dst[...] = jnp.sum(jnp.where(row == lane, src[...], 0.0), axis=0)[0:8] / gain[...]


def body(tokens, cotangent, w_qkv, w_out, w_up, w_down, gain_attn, gain_mlp):
    width = tokens.shape[-1]
    factor = 1.0 / math.sqrt(128 * lax.axis_size("slab") * lax.axis_size("case"))
    shapes = scratch()
    leaves, tree = jax.tree.flatten(shapes)
    vmem, any_space = pl.BlockSpec(memory_space=pltpu.VMEM), pl.BlockSpec(memory_space=pl.ANY)
    outs = ((8, 1536), (8, 512), (8, 2048), (32, 512), (8, 128), (8, 128))
    result = pl.pallas_call(
        functools.partial(kernel, factor, tree),
        out_shape=[jax.ShapeDtypeStruct((2, 8, 8, width), BF16)] + [jax.ShapeDtypeStruct(s, F32) for s in outs],
        in_specs=[vmem, vmem] + [any_space] * 4 + [vmem, vmem],
        out_specs=[vmem] * 7,
        scratch_shapes=leaves,
        compiler_params=pltpu.CompilerParams(
            collective_id=1, has_side_effects=True, vmem_limit_bytes=56 * 1024 * 1024
        ),
        cost_estimate=pl.CostEstimate(flops=3_500_000_000, bytes_accessed=7_000_000, transcendentals=0),
    )(
        tokens.reshape(2, 8, 8, width),
        cotangent.reshape(2, 8, 8, width),
        w_qkv,
        w_out,
        w_up,
        w_down,
        gain_attn.reshape(1, width),
        gain_mlp.reshape(1, width),
    )
    first = lax.axis_index("slab") * 8
    gains = [lax.dynamic_slice(g, (first,), (8,)) for g in (gain_attn, gain_mlp)]
    result = pl.pallas_call(
        results_kernel,
        out_shape=[jax.ShapeDtypeStruct((2, 8, 8, width), BF16)]
        + [jax.ShapeDtypeStruct(s, F32) for s in outs[:4] + ((8,), (8,))],
        in_specs=[vmem] * 9,
        out_specs=[vmem] * 7,
    )(*result, *gains)
    return (result[0].reshape(tokens.shape), *result[1:])


def solution(mesh):
    grid = P("case", "slab", None, None, None)
    return jax.shard_map(
        body,
        mesh=mesh,
        in_specs=(grid, grid, P(), P(), P(), P(), P(), P()),
        out_specs=(grid, P("slab", None), P("slab", None), P("slab", None), P("slab", None), P("slab"), P("slab")),
        check_vma=False,
    )
```

```python
import functools
import math
import types

import jax
import jax.numpy as jnp
from jax import lax
from jax.experimental import pallas as pl
from jax.experimental.pallas import tpu as pltpu
from jax.sharding import PartitionSpec as P

MESH = pl.DeviceIdType.MESH
F32 = jnp.float32
BF16 = jnp.bfloat16
EPSILON = 1e-06
ROOT = math.sqrt(2.0 / math.pi)
LOWEST = -1e30
SLABS = 64


def places():
    slab, case = lax.axis_index("slab"), lax.axis_index("case")
    return slab // 16, (slab // 2) % 8, slab % 2, case // 2, case % 2


def device(x, z, y_hi, y_lo, core):
    return ((x * 8 + z) * 2 + y_hi, y_lo * 2 + core)


def remote(src, dst, send_sem, recv_sem, to):
    copy = pltpu.make_async_remote_copy(
        src_ref=src, dst_ref=dst, send_sem=send_sem, recv_sem=recv_sem, device_id=to, device_id_type=MESH
    )
    copy.start()
    return copy


def nn(a, b):
    return lax.dot_general(a, b, (((1,), (0,)), ((), ())), preferred_element_type=F32)


def nt(a, b):
    return lax.dot_general(a, b, (((1,), (1,)), ((), ())), preferred_element_type=F32)


def tn(a, b):
    return lax.dot_general(a, b, (((0,), (0,)), ((), ())), preferred_element_type=F32)


def to_rows(grid):
    first, second = grid[0], grid[1]
    low = lax.broadcasted_iota(jnp.int32, first.shape, 1) < 4
    even = jnp.where(low, first, pltpu.roll(second, 4, 1))
    odd = jnp.where(low, pltpu.roll(first, 4, 1), second)
    return jnp.stack([even, odd], axis=1).reshape(128, first.shape[-1])


def to_grid(rows):
    split = rows.reshape(8, 2, 8, rows.shape[-1])
    even, odd = split[:, 0], split[:, 1]
    low = lax.broadcasted_iota(jnp.int32, even.shape, 1) < 4
    first = jnp.where(low, even, pltpu.roll(odd, 4, 1))
    second = jnp.where(low, pltpu.roll(even, 4, 1), odd)
    return first, second


def norm_stats(values):
    inverse = lax.rsqrt(jnp.mean(values * values, axis=-1, keepdims=True) + EPSILON)
    return values * inverse, inverse


def norm_back(grad_normed, normed, inverse, gain):
    scaled = grad_normed * gain
    return inverse * (scaled - normed * jnp.mean(scaled * normed, axis=-1, keepdims=True))


def two_heads(pair):
    lane = lax.broadcasted_iota(jnp.int32, (128, 128), 1)
    first = jnp.where(lane < 64, 1.0, 0.0).astype(BF16)
    second = jnp.where(lane < 64, 0.0, 1.0).astype(BF16)
    return jnp.concatenate([pair * first, pair * second], axis=0)


def over_keys(across):
    return jnp.concatenate([across[:, 0:128], across[:, 128:256]], axis=0)


def line_probs(scores, mask):
    if mask is not None:
        scores = jnp.where(mask, scores, LOWEST)
    weights = jnp.exp(scores - jnp.max(scores, axis=0, keepdims=True))
    return weights * (1.0 / jnp.sum(weights, axis=0, keepdims=True))


def line_masks():
    keys = lax.broadcasted_iota(jnp.int32, (128, 256), 0)
    queries = lax.broadcasted_iota(jnp.int32, (128, 256), 1) & 127
    apart = keys ^ queries
    return (apart & 0x74) == 0, (apart & 0x0F) == 0


def pair_scores(queries, keys):
    return nt(keys, two_heads(queries * jnp.array(0.125, BF16)))


def pair_out(probs, values):
    return tn(over_keys(probs), two_heads(values))


def score_grads(probs, grad_probs):
    return probs * (grad_probs - jnp.sum(probs * grad_probs, axis=0, keepdims=True))


def pair_back(rounded, grad_scores, queries, keys, grads):
    both = two_heads(grads)
    grad_values = nn(rounded, both)
    grad_keys = nn(grad_scores, two_heads(queries * jnp.array(0.125, BF16)))
    grad_queries = tn(over_keys(grad_scores), two_heads(keys)) * 0.125
    return grad_queries, grad_keys, grad_values


class Ring:
    def __init__(self, me, dev, part, relay, fin, ss, rs):
        self.me, self.dev, self.part, self.relay, self.fin, self.ss, self.rs = me, dev, part, relay, fin, ss, rs
        self.right, self.left, self.over = (me + 1) % 4, (me + 3) % 4, (me + 2) % 4
        self.copies = []

    def send(self, src, dst, to):
        n = len(self.copies)
        self.copies.append(remote(src, dst, self.ss.at[n], self.rs.at[n], self.dev(to)))

    def start(self):
        if self.relay is None:
            for n, to in enumerate((self.over, self.right, self.left)):
                for h in range(2):
                    self.send(self.part(to, h), self.fin.at[n, h], to)
            return
        self.send(self.part(self.over, 0), self.relay.at[0], self.right)
        self.send(self.part(self.over, 1), self.relay.at[1], self.left)
        self.send(self.part(self.right, 1), self.fin.at[0, 1], self.right)
        self.send(self.part(self.left, 0), self.fin.at[0, 0], self.left)

    def middle(self):
        for h, to in ((0, self.right), (1, self.left)):
            self.copies[h].wait_recv()
            ref = self.part(to, h)
            ref[...] = (ref[...].astype(F32) + self.relay[h].astype(F32)).astype(BF16)
            self.send(ref, self.fin.at[1, h], to)

    def finish(self):
        for copy in self.copies[0 if self.relay is None else 2 :]:
            copy.wait_recv()

    def result(self, h):
        total = self.part(self.me, h)[...].astype(F32)
        for n in range(3 if self.relay is None else 2):
            total = total + self.fin[n, h].astype(F32)
        return total.astype(BF16)

    def drain(self):
        for copy in self.copies:
            copy.wait_send()


def sum_shapes(wide, relays):
    vm, dma, part = pltpu.VMEM, pltpu.SemaphoreType.DMA, wide // 2
    shapes = dict(
        buf=vm((4, 8, 2, 16, wide), BF16),
        fin_a=vm((3, 2, 2, 2, 16, wide), BF16), fin_b=vm((3, 2, 2, 4, 16, part), BF16),
        cbuf=vm((8, 4, 16, part), BF16), crecv=vm((32, 16, part), BF16), gath=vm((4, 16, part), BF16),
        ss_ring=dma((2, 6)), rs_ring=dma((2, 6)), ss_c=dma((1,)), rs_c=dma((1,)), ss_g=dma((3,)), rs_g=dma((3,)),
    )
    if relays:
        shapes.update(relay_a=vm((2, 2, 2, 16, wide), BF16), relay_b=vm((2, 2, 4, 16, part), BF16))
    return shapes


def far_first(k, half):
    return half + ((k + 1) // 2) * (1 - 2 * (k % 2))


class Sum:
    def __init__(self, ref):
        self.ref = ref
        x, z, y_hi, y_lo, core = places()
        self.place = (x, z, y_hi, y_lo, core)
        y = y_hi * 2 + y_lo
        part = ref.gath.shape[-1]

        def lanes(lo):
            return pl.ds(pl.multiple_of(lo * part, 128), part)

        def dev_x(i):
            return device(i, z, y_hi, y_lo, core)

        def dev_y(i):
            return device(x, z, i // 2, i % 2, core)

        sems = [(ref.ss_ring.at[i], ref.rs_ring.at[i]) for i in range(2)]
        relay_a, relay_b = getattr(ref, "relay_a", None), getattr(ref, "relay_b", None)
        self.a = Ring(x, dev_x, lambda i, h: ref.buf.at[i, pl.ds(2 * h, 2)], relay_a, ref.fin_a, *sems[0])
        self.b = Ring(
            y, dev_y, lambda i, h: ref.buf.at[pl.ds(2 * h, 2), pl.ds(4, 4), i // 2, :, lanes(i % 2)],
            relay_b, ref.fin_b, *sems[1],
        )
        self.copies = []

    def put(self, at, upper, lower):
        width = upper.shape[-1]
        both = jnp.concatenate([upper, lower], axis=1).astype(BF16)
        self.ref.buf[:, :, :, :, at : at + width] = both.reshape(4, 8, 2, 16, width)

    def start(self):
        self.a.start()
        self.b.start()

    def middle(self):
        self.a.middle()
        self.b.middle()

    def second(self):
        ref = self.ref
        x, z, y_hi, y_lo, core = self.place
        y = y_hi * 2 + y_lo
        part = ref.gath.shape[-1]
        self.a.finish()
        for h in range(2):
            done = self.a.result(h)
            for i in range(4):
                ref.cbuf[2 * h : 2 * h + 2, i] = done[:, i // 2, :, (i % 2) * part : (i % 2) * part + part]
        self.b.finish()
        for h in range(2):
            done = self.b.result(h)
            for i in range(2):
                ref.cbuf[4:8, 2 * h + i] = done[i]

        def one(n, carry):
            to_z = (z + far_first(n // 4, 4)) % 8
            step = far_first(n % 4, 2)
            low = 1 - to_z // 4
            to = low * ((y + step) % 4) + (1 - low) * ((x + step) % 4)
            to_x, to_y = low * x + (1 - low) * to, low * to + (1 - low) * y
            remote(ref.cbuf.at[to_z, to], ref.crecv.at[z * 4 + low * y + (1 - low) * x], ref.ss_c.at[0], ref.rs_c.at[0],
                   device(to_x, to_z, to_y // 2, to_y % 2, core))
            return carry

        lax.fori_loop(0, 31, one, 0)
        low = 1 - z // 4
        own = low * y + (1 - low) * x
        ref.crecv[z * 4 + own] = ref.cbuf[z, own]

    def gather(self):
        ref = self.ref
        x, z, y_hi, y_lo, core = self.place
        got = ref.crecv.at[pl.ds(0, 31)]
        pltpu.make_async_copy(got, got, ref.rs_c.at[0]).wait()
        mine = y_lo * 2 + core
        ref.gath[mine] = jnp.sum(ref.crecv[...].astype(F32), axis=0).astype(BF16)
        self.copies = share(ref.gath, ref.ss_g, ref.rs_g)

    def finish(self):
        for copy in self.copies:
            copy.wait_recv()
        gath = self.ref.gath
        return [jnp.concatenate([gath[c].astype(F32), gath[2 + c].astype(F32)], axis=1) for c in range(2)]

    def drain(self):
        sent = self.ref.crecv.at[pl.ds(0, 31)]
        pltpu.make_async_copy(sent, sent, self.ref.ss_c.at[0]).wait()
        for copy in self.copies:
            copy.wait_send()
        for ring in (self.a, self.b):
            ring.drain()


def share(ref, send_sem, recv_sem):
    x, z, y_hi, y_lo, core = places()
    mine = y_lo * 2 + core
    return [
        remote(ref.at[mine], ref.at[mine], send_sem.at[n], recv_sem.at[n],
               device(x, z, y_hi, (y_lo + dy) % 2, (core + dc) % 2))
        for n, (dy, dc) in enumerate(((1, 1), (1, 0), (0, 1)))
    ]


class Exchange:
    def __init__(self, send, recv, ss, rs, shared=1):
        self.send, self.recv, self.ss, self.rs, self.shared = send, recv, ss, rs, shared

    def start(self):
        me = lax.axis_index("slab")
        x, z, y_hi, y_lo, core = places()

        def one(n, carry):
            kz, kx, ky = n // 8, (n // 2) % 4, n % 2
            dz, dx = far_first(kz, 4), far_first(kx, 2)
            to = device((x + dx) % 4, (z + dz) % 8, (y_hi + 1 - ky) % 2, y_lo, core)
            remote(self.send.at[to[0] // self.shared], self.recv.at[me], self.ss, self.rs, to)
            return carry

        lax.fori_loop(0, SLABS - 1, one, 0)
        self.recv[me] = self.send[me // self.shared]

    def wait(self):
        got = self.recv.at[pl.ds(0, SLABS - 1)]
        pltpu.make_async_copy(got, got, self.rs).wait()

    def drain(self):
        sent = self.recv.at[pl.ds(0, SLABS - 1)]
        pltpu.make_async_copy(sent, sent, self.ss).wait()


def by_pair(blocks):
    width = blocks[0].shape[-1]
    return jnp.stack([b.reshape(16, 8, width) for b in blocks], axis=1).reshape(SLABS, 8, width)


def scratch():
    vm, dma = pltpu.VMEM, pltpu.SemaphoreType.DMA
    return dict(
        wq=vm((512, 1536), BF16), wo=vm((512, 512), BF16), wu=vm((512, 2048), BF16), wd=vm((2048, 512), BF16),
        sw=dma((4,)),
        qkv=vm((128, 1536), BF16),
        qsend=vm((SLABS, 8, 384), BF16), qrecv=vm((SLABS, 8, 384), BF16),
        osend=vm((SLABS, 8, 128), BF16), orecv=vm((SLABS, 8, 128), BF16),
        gsend=vm((SLABS, 8, 128), BF16), grecv=vm((SLABS, 8, 128), BF16),
        dsend=vm((SLABS, 8, 384), BF16), drecv=vm((SLABS, 8, 384), BF16),
        hsend=vm((16, 8, 512), BF16), hrecv=vm((SLABS, 8, 512), BF16),
        psend=vm((SLABS, 8, 384), BF16), precv=vm((SLABS, 8, 384), BF16), pgath=vm((4, 8, 1536), BF16),
        ss_x=dma((6,)), rs_x=dma((6,)), ss_p=dma((3,)), rs_p=dma((3,)),
        z32=vm((3, 512, 128), F32), o32=vm((512, 128), F32), g32=vm((512, 128), F32), d32=vm((3, 512, 128), F32),
        px=vm((4, 128, 256), F32), py=vm((4, 128, 256), F32), pz=vm((4, 128, 256), F32),
        oxy=vm((128, 512), F32), dxy=vm((128, 1536), F32), gmix=vm((128, 512), BF16),
        gact=vm((128, 2048), F32), flat=vm((128, 512), F32), gres=vm((128, 512), F32),
        b_h1=vm((256, 512), BF16), b_mixed=vm((256, 512), BF16), b_h2=vm((256, 512), BF16), b_act=vm((256, 2048), BF16),
        cot=vm((128, 512), BF16), gu=vm((128, 2048), BF16), grb=vm((128, 512), BF16), gp=vm((128, 1536), BF16),
        b_cot=vm((256, 256), BF16), b_gu=vm((256, 1024), BF16), b_grb=vm((256, 256), BF16), b_gp=vm((256, 768), BF16),
        ss_core=dma((8,)), rs_core=dma((8,)),
        down32=vm((SLABS, 32, 256), F32),
        one=sum_shapes(1024, True), two=sum_shapes(512, False),
    )


def kernel(factor, tree, tok, cot, wq_h, wo_h, wu_h, wd_h, ga, gm, o_tok, o_qkv, o_out, o_up, o_down, o_g1, o_g2, *refs):
    r = jax.tree.unflatten(tree, refs)
    r, r_one, r_two = types.SimpleNamespace(**r), types.SimpleNamespace(**r["one"]), types.SimpleNamespace(**r["two"])
    x, z, y_hi, y_lo, core = places()
    slab, case = lax.axis_index("slab"), lax.axis_index("case")
    other = device(x, z, y_hi, y_lo, 1 - core)

    loads = [
        pltpu.make_async_copy(src, dst, r.sw.at[n])
        for n, (src, dst) in enumerate(((wq_h, r.wq), (wo_h, r.wo), (wd_h, r.wd), (wu_h, r.wu)))
    ]
    for load in loads:
        load.start()

    barrier = pltpu.get_barrier_semaphore()

    def greet(d, carry):
        pl.semaphore_signal(barrier, inc=1, device_id=((slab + d) % SLABS, case), device_id_type=MESH)
        return carry

    lax.fori_loop(1, SLABS, greet, 0)
    def greet_y(n, carry):
        peer = device(x, n // 2, n % 2, 1 - y_lo, core)
        pl.semaphore_signal(barrier, inc=1, device_id=peer, device_id_type=MESH)
        return carry

    lax.fori_loop(0, 16, greet_y, 0)
    for peer in (other, device(x, z, y_hi, 1 - y_lo, 1 - core)):
        pl.semaphore_signal(barrier, inc=1, device_id=peer, device_id_type=MESH)

    gain_one, gain_two = ga[...], gm[...]
    r.flat[...] = to_rows(tok[...].astype(F32))
    normed_one, inverse_one = norm_stats(r.flat[...])
    hidden_one = normed_one * gain_one
    r.b_h1[0:128, :] = hidden_one.astype(BF16)
    r.hsend[...] = hidden_one.reshape(16, 8, 512).astype(BF16)
    r.cot[...] = to_rows(cot[...].astype(F32)).astype(BF16)
    loads[0].wait()
    for i in range(3):
        r.qkv[:, 512 * i : 512 * i + 512] = nn(r.b_h1[0:128, :], r.wq[:, 512 * i : 512 * i + 512]).astype(BF16)
    for i in range(3):
        r.qsend[:, :, 128 * i : 128 * i + 128] = by_pair(
            [r.qkv[:, 512 * i + 128 * j : 512 * i + 128 * j + 128].astype(F32) for j in range(4)]
        ).astype(BF16)
    pl.semaphore_wait(barrier, SLABS - 1 + 16 + 2)
    ex_q = Exchange(r.qsend, r.qrecv, r.ss_x.at[0], r.rs_x.at[0])
    ex_o = Exchange(r.osend, r.orecv, r.ss_x.at[1], r.rs_x.at[1])
    ex_g = Exchange(r.gsend, r.grecv, r.ss_x.at[2], r.rs_x.at[2])
    ex_d = Exchange(r.dsend, r.drecv, r.ss_x.at[3], r.rs_x.at[3])
    ex_h = Exchange(r.hsend, r.hrecv, r.ss_x.at[4], r.rs_x.at[4], shared=4)
    ex_p = Exchange(r.psend, r.precv, r.ss_x.at[5], r.rs_x.at[5])
    ex_q.start()

    core_copies = []

    def to_core_full(ref):
        n = len(core_copies)
        core_copies.append(
            remote(ref.at[pl.ds(0, 128)], ref.at[pl.ds(128, 128)], r.ss_core.at[n], r.rs_core.at[n], other)
        )

    def to_core_half(src, dst):
        n, half = len(core_copies), dst.shape[-1]
        theirs = src.at[:, pl.ds(pl.multiple_of((1 - core) * half, 128), half)]
        core_copies.append(remote(theirs, dst.at[pl.ds(128, 128)], r.ss_core.at[n], r.rs_core.at[n], other))
        dst[0:128, :] = src[:, pl.ds(pl.multiple_of(core * half, 128), half)]

    to_core_full(r.b_h1)
    to_core_half(r.cot, r.b_cot)

    def pair(j):
        return [r.qkv[:, 512 * i + 128 * j : 512 * i + 128 * j + 128] for i in range(3)]

    mask_x, mask_y = line_masks()
    for j in range(4):
        queries, keys, values = pair(j)
        scores = pair_scores(queries, keys)
        r.px[j] = line_probs(scores, mask_x)
        r.py[j] = line_probs(scores, mask_y)
        r.oxy[:, 128 * j : 128 * j + 128] = pair_out((r.px[j] + r.py[j]).astype(BF16), values)

    loads[2].wait()
    for i in range(4):
        at = slice(512 * i, 512 * i + 512)
        r.gact[:, at] = nt(r.cot[...], r.wd[at, :])

    ex_q.wait()
    for i in range(3):
        r.z32[i] = r.qrecv[:, :, 128 * i : 128 * i + 128].astype(F32).reshape(512, 128)

    def line(j):
        return [r.z32[i, pl.ds(j, 128, stride=4), :].astype(BF16) for i in range(3)]

    for j in range(4):
        queries, keys, values = line(j)
        probs = line_probs(pair_scores(queries, keys), None)
        r.pz[j] = probs
        r.o32[pl.ds(j, 128, stride=4), :] = pair_out(probs.astype(BF16), values)
    r.osend[...] = r.o32[...].reshape(SLABS, 8, 128).astype(BF16)
    ex_o.start()
    ex_h.start()

    loads[1].wait()
    loads[3].wait()
    ex_o.wait()
    from_z = r.orecv[...].astype(F32).reshape(16, 4, 8, 128)
    for j in range(4):
        at = slice(128 * j, 128 * j + 128)
        r.b_mixed[0:128, at] = (r.oxy[:, at] + from_z[:, j].reshape(128, 128)).astype(BF16)
    residual = (r.flat[...] + nn(r.b_mixed[0:128, :], r.wo[...])).astype(BF16)
    normed_two, inverse_two = norm_stats(residual.astype(F32))
    r.b_h2[0:128, :] = (normed_two * gain_two).astype(BF16)
    grad_hidden_two = jnp.zeros((128, 512), F32)
    for i in range(4):
        at = slice(512 * i, 512 * i + 512)
        u = nn(r.b_h2[0:128, :], r.wu[:, at])
        square = u * u
        tangent = jnp.tanh(ROOT * u * (1.0 + 0.044715 * square))
        half = 0.5 * (1.0 + tangent)
        r.b_act[0:128, at] = (u * half).astype(BF16)
        slope = half + 0.5 * u * (1.0 - tangent * tangent) * ROOT * (1.0 + 3.0 * 0.044715 * square)
        r.gu[:, at] = (r.gact[:, at] * slope).astype(BF16)
        grad_hidden_two = grad_hidden_two + nt(r.gu[:, at], r.wu[:, at])
    r.gres[...] = r.cot[...].astype(F32) + norm_back(grad_hidden_two, normed_two, inverse_two, gain_two)
    r.grb[...] = r.gres[...].astype(BF16)
    r.gmix[...] = nt(r.grb[...], r.wo[...]).astype(BF16)
    r.gsend[...] = by_pair([r.gmix[:, 128 * j : 128 * j + 128].astype(F32) for j in range(4)]).astype(BF16)
    ex_g.start()
    to_core_full(r.b_act)
    to_core_half(r.gu, r.b_gu)
    to_core_full(r.b_h2)
    to_core_full(r.b_mixed)
    to_core_half(r.grb, r.b_grb)

    one, two = Sum(r_one), Sum(r_two)
    for copy in core_copies[1:5]:
        copy.wait_recv()
    r.down32[...] = tn(r.b_act[...], r.b_cot[...]).reshape(SLABS, 32, 256)
    for i in range(2):
        one.put(
            256 * i,
            tn(r.b_h2[...], r.b_gu[:, 256 * i : 256 * i + 256]).reshape(SLABS, 8, 256),
            tn(r.b_h2[...], r.b_gu[:, 512 + 256 * i : 768 + 256 * i]).reshape(SLABS, 8, 256),
        )
    one.put(512, r.down32[:, 0:8, :], r.down32[:, 16:24, :])
    one.put(768, r.down32[:, 8:16, :], r.down32[:, 24:32, :])
    one.start()

    for j in range(4):
        queries, keys, values = pair(j)
        grads = r.gmix[:, 128 * j : 128 * j + 128]
        grad_probs = nt(values, two_heads(grads))
        probs_x, probs_y = r.px[j], r.py[j]
        grad_scores = (score_grads(probs_x, grad_probs) + score_grads(probs_y, grad_probs)).astype(BF16)
        back = pair_back((probs_x + probs_y).astype(BF16), grad_scores, queries, keys, grads)
        for i in range(3):
            at = slice(512 * i + 128 * j, 512 * i + 128 * j + 128)
            r.dxy[:, at] = back[i]
            r.gp[:, at] = back[i].astype(BF16)
    to_core_half(r.gp, r.b_gp)

    for copy in core_copies[0:1] + core_copies[5:]:
        copy.wait_recv()

    def qkv_part(i):
        return tn(r.b_h1[...], r.b_gp[:, 256 * i : 256 * i + 256]).reshape(SLABS, 8, 256)

    two.put(0, qkv_part(0), qkv_part(1))
    two.put(256, qkv_part(2), tn(r.b_mixed[...], r.b_grb[...]).reshape(SLABS, 8, 256))
    two.start()

    ex_g.wait()
    r.g32[...] = r.grecv[...].astype(F32).reshape(512, 128)
    for j in range(4):
        queries, keys, values = line(j)
        grads = r.g32[pl.ds(j, 128, stride=4), :].astype(BF16)
        probs = r.pz[j]
        grad_scores = score_grads(probs, nt(values, two_heads(grads))).astype(BF16)
        back = pair_back(probs.astype(BF16), grad_scores, queries, keys, grads)
        for i in range(3):
            r.d32[i, pl.ds(j, 128, stride=4), :] = back[i]

    ex_h.wait()
    hidden_lines = r.hrecv[...].astype(F32).reshape(512, 512).astype(BF16)
    for i in range(3):
        r.psend[:, :, 128 * i : 128 * i + 128] = tn(hidden_lines, r.d32[i].astype(BF16)).reshape(SLABS, 8, 128).astype(BF16)
    ex_p.start()
    one.middle()
    for i in range(3):
        r.dsend[:, :, 128 * i : 128 * i + 128] = r.d32[i].reshape(SLABS, 8, 128).astype(BF16)
    ex_d.start()
    two.second()
    one.second()
    ex_p.wait()
    lines = jnp.sum(r.precv[...].astype(F32).reshape(16, 4, 8, 384), axis=0).astype(BF16)
    case_at = y_lo * 2 + core
    for i in range(3):
        for j in range(4):
            at = 512 * i + 128 * j
            r.pgath[case_at, :, at : at + 128] = lines[j, :, 128 * i : 128 * i + 128]
    p_copies = share(r.pgath, r.ss_p, r.rs_p)

    ex_d.wait()
    for i in range(3):
        from_z = r.drecv[:, :, 128 * i : 128 * i + 128].astype(F32).reshape(16, 4, 8, 128)
        for j in range(4):
            at = slice(512 * i + 128 * j, 512 * i + 128 * j + 128)
            r.dxy[:, at] = r.dxy[:, at] + from_z[:, j].reshape(128, 128)
    grad_hidden_one = nt(r.dxy[...].astype(BF16), r.wq[...])
    normed_one, inverse_one = norm_stats(r.flat[...])
    first, second = to_grid(r.gres[...] + norm_back(grad_hidden_one, normed_one, inverse_one, gain_one))
    o_tok[0] = first.astype(BF16)
    o_tok[1] = second.astype(BF16)

    two.gather()
    one.gather()
    own_rows = pl.ds(pl.multiple_of((slab // 2) * 16, 16), 16)

    def weight_rows(ref):
        both = ref[own_rows, :].astype(F32)
        return jnp.where(slab % 2 == 0, both[0:8], both[8:16])

    for c, full in enumerate(one.finish()):
        full = full * factor
        o_up[:, 1024 * c : 1024 * c + 512] = full[0:8, 0:512]
        o_up[:, 1024 * c + 512 : 1024 * c + 1024] = full[8:16, 0:512]
        at = slice(256 * c, 256 * c + 256)
        o_down[0:8, at] = full[0:8, 512:768]
        o_down[8:16, at] = full[0:8, 768:1024]
        o_down[16:24, at] = full[8:16, 512:768]
        o_down[24:32, at] = full[8:16, 768:1024]

    def over_gain(rows, gain):
        lane = lax.broadcasted_iota(jnp.int32, (8, 512), 1)
        row = lax.broadcasted_iota(jnp.int32, (8, 512), 0)
        own = jnp.sum(jnp.where(lane == slab * 8 + row, gain, 0.0), axis=1, keepdims=True)
        return jnp.broadcast_to(jnp.sum(rows, axis=1, keepdims=True) / own, (8, 128))

    o_g2[...] = over_gain(o_up[...] * weight_rows(r.wu), gain_two)
    for copy in p_copies:
        copy.wait_recv()
    o_qkv[...] = jnp.sum(r.pgath[...].astype(F32), axis=0) * factor
    for c, full in enumerate(two.finish()):
        full = full * factor
        o_qkv[:, 768 * c : 768 * c + 256] += full[0:8, 0:256]
        o_qkv[:, 768 * c + 256 : 768 * c + 512] += full[8:16, 0:256]
        o_qkv[:, 768 * c + 512 : 768 * c + 768] += full[0:8, 256:512]
        o_out[:, 256 * c : 256 * c + 256] = full[8:16, 256:512]
    o_g1[...] = over_gain(o_qkv[...] * weight_rows(r.wq), gain_one)

    for exchange in (ex_q, ex_o, ex_h, ex_g, ex_p, ex_d):
        exchange.drain()
    for copy in core_copies + p_copies:
        copy.wait_send()
    one.drain()
    two.drain()


def results_kernel(tok, qkv, out, up, down, g1, g2, o_tok, o_qkv, o_out, o_up, o_down, o_g1, o_g2):
    for src, dst in ((tok, o_tok), (qkv, o_qkv), (out, o_out), (up, o_up), (down, o_down)):
        dst[...] = src[...]
    row = lax.broadcasted_iota(jnp.int32, (8, 128), 0)
    lane = lax.broadcasted_iota(jnp.int32, (8, 128), 1)
    for src, dst in ((g1, o_g1), (g2, o_g2)):
        dst[...] = jnp.sum(jnp.where(row == lane, src[...], 0.0), axis=0)[0:8]


def body(tokens, cotangent, w_qkv, w_out, w_up, w_down, gain_attn, gain_mlp):
    width = tokens.shape[-1]
    factor = 1.0 / math.sqrt(128 * lax.axis_size("slab") * lax.axis_size("case"))
    shapes = scratch()
    leaves, tree = jax.tree.flatten(shapes)
    vmem, any_space = pl.BlockSpec(memory_space=pltpu.VMEM), pl.BlockSpec(memory_space=pl.ANY)
    outs = ((8, 1536), (8, 512), (8, 2048), (32, 512), (8, 128), (8, 128))
    result = pl.pallas_call(
        functools.partial(kernel, factor, tree),
        out_shape=[jax.ShapeDtypeStruct((2, 8, 8, width), BF16)] + [jax.ShapeDtypeStruct(s, F32) for s in outs],
        in_specs=[vmem, vmem] + [any_space] * 4 + [vmem, vmem],
        out_specs=[vmem] * 7,
        scratch_shapes=leaves,
        compiler_params=pltpu.CompilerParams(
            collective_id=1, has_side_effects=True, vmem_limit_bytes=56 * 1024 * 1024
        ),
        cost_estimate=pl.CostEstimate(flops=3_500_000_000, bytes_accessed=7_000_000, transcendentals=0),
    )(
        tokens.reshape(2, 8, 8, width),
        cotangent.reshape(2, 8, 8, width),
        w_qkv,
        w_out,
        w_up,
        w_down,
        gain_attn.reshape(1, width),
        gain_mlp.reshape(1, width),
    )
    result = pl.pallas_call(
        results_kernel,
        out_shape=[jax.ShapeDtypeStruct((2, 8, 8, width), BF16)]
        + [jax.ShapeDtypeStruct(s, F32) for s in outs[:4] + ((8,), (8,))],
        in_specs=[vmem] * 7,
        out_specs=[vmem] * 7,
    )(*result)
    return (result[0].reshape(tokens.shape), *result[1:])


def solution(mesh):
    grid = P("case", "slab", None, None, None)
    return jax.shard_map(
        body,
        mesh=mesh,
        in_specs=(grid, grid, P(), P(), P(), P(), P(), P()),
        out_specs=(grid, P("slab", None), P("slab", None), P("slab", None), P("slab", None), P("slab"), P("slab")),
        check_vma=False,
    )
```

```python
import functools
import math
import types

import jax
import jax.numpy as jnp
from jax import lax
from jax.experimental import pallas as pl
from jax.experimental.pallas import tpu as pltpu
from jax.sharding import PartitionSpec as P

MESH = pl.DeviceIdType.MESH
F32 = jnp.float32
BF16 = jnp.bfloat16
EPSILON = 1e-06
ROOT = math.sqrt(2.0 / math.pi)
LOWEST = -1e30
SLABS = 64


def places():
    slab, case = lax.axis_index("slab"), lax.axis_index("case")
    return slab // 16, (slab // 2) % 8, slab % 2, case // 2, case % 2


def device(x, z, y_hi, y_lo, core):
    return ((x * 8 + z) * 2 + y_hi, y_lo * 2 + core)


def remote(src, dst, send_sem, recv_sem, to):
    copy = pltpu.make_async_remote_copy(
        src_ref=src, dst_ref=dst, send_sem=send_sem, recv_sem=recv_sem, device_id=to, device_id_type=MESH
    )
    copy.start()
    return copy


def nn(a, b):
    return lax.dot_general(a, b, (((1,), (0,)), ((), ())), preferred_element_type=F32)


def nt(a, b):
    return lax.dot_general(a, b, (((1,), (1,)), ((), ())), preferred_element_type=F32)


def tn(a, b):
    return lax.dot_general(a, b, (((0,), (0,)), ((), ())), preferred_element_type=F32)


def to_rows(grid):
    first, second = grid[0], grid[1]
    low = lax.broadcasted_iota(jnp.int32, first.shape, 1) < 4
    even = jnp.where(low, first, pltpu.roll(second, 4, 1))
    odd = jnp.where(low, pltpu.roll(first, 4, 1), second)
    return jnp.stack([even, odd], axis=1).reshape(128, first.shape[-1])


def to_grid(rows):
    split = rows.reshape(8, 2, 8, rows.shape[-1])
    even, odd = split[:, 0], split[:, 1]
    low = lax.broadcasted_iota(jnp.int32, even.shape, 1) < 4
    first = jnp.where(low, even, pltpu.roll(odd, 4, 1))
    second = jnp.where(low, pltpu.roll(even, 4, 1), odd)
    return first, second


def norm_stats(values):
    inverse = lax.rsqrt(jnp.mean(values * values, axis=-1, keepdims=True) + EPSILON)
    return values * inverse, inverse


def norm_back(grad_normed, normed, inverse, gain):
    scaled = grad_normed * gain
    return inverse * (scaled - normed * jnp.mean(scaled * normed, axis=-1, keepdims=True))


def two_heads(pair):
    lane = lax.broadcasted_iota(jnp.int32, (128, 128), 1)
    first = jnp.where(lane < 64, 1.0, 0.0).astype(BF16)
    second = jnp.where(lane < 64, 0.0, 1.0).astype(BF16)
    return jnp.concatenate([pair * first, pair * second], axis=0)


def over_keys(across):
    return jnp.concatenate([across[:, 0:128], across[:, 128:256]], axis=0)


def line_probs(scores, mask):
    if mask is not None:
        scores = jnp.where(mask, scores, LOWEST)
    weights = jnp.exp(scores - jnp.max(scores, axis=0, keepdims=True))
    return weights * (1.0 / jnp.sum(weights, axis=0, keepdims=True))


def line_masks():
    keys = lax.broadcasted_iota(jnp.int32, (128, 256), 0)
    queries = lax.broadcasted_iota(jnp.int32, (128, 256), 1) & 127
    apart = keys ^ queries
    return (apart & 0x74) == 0, (apart & 0x0F) == 0


def pair_scores(queries, keys):
    return nt(keys, two_heads(queries * jnp.array(0.125, BF16)))


def pair_out(probs, values):
    return tn(over_keys(probs), two_heads(values))


def score_grads(probs, grad_probs):
    return probs * (grad_probs - jnp.sum(probs * grad_probs, axis=0, keepdims=True))


def pair_back(rounded, grad_scores, queries, keys, grads):
    both = two_heads(grads)
    grad_values = nn(rounded, both)
    grad_keys = nn(grad_scores, two_heads(queries * jnp.array(0.125, BF16)))
    grad_queries = tn(over_keys(grad_scores), two_heads(keys)) * 0.125
    return grad_queries, grad_keys, grad_values


class Ring:
    def __init__(self, me, dev, part, relay, fin, ss, rs):
        self.me, self.dev, self.part, self.relay, self.fin, self.ss, self.rs = me, dev, part, relay, fin, ss, rs
        self.right, self.left, self.over = (me + 1) % 4, (me + 3) % 4, (me + 2) % 4
        self.copies = []

    def send(self, src, dst, to):
        n = len(self.copies)
        self.copies.append(remote(src, dst, self.ss.at[n], self.rs.at[n], self.dev(to)))

    def start(self):
        if self.relay is None:
            for n, to in enumerate((self.over, self.right, self.left)):
                for h in range(2):
                    self.send(self.part(to, h), self.fin.at[n, h], to)
            return
        self.send(self.part(self.over, 0), self.relay.at[0], self.right)
        self.send(self.part(self.over, 1), self.relay.at[1], self.left)
        self.send(self.part(self.right, 1), self.fin.at[0, 1], self.right)
        self.send(self.part(self.left, 0), self.fin.at[0, 0], self.left)

    def middle(self):
        for h, to in ((0, self.right), (1, self.left)):
            self.copies[h].wait_recv()
            ref = self.part(to, h)
            ref[...] = (ref[...].astype(F32) + self.relay[h].astype(F32)).astype(BF16)
            self.send(ref, self.fin.at[1, h], to)

    def finish(self):
        for copy in self.copies[0 if self.relay is None else 2 :]:
            copy.wait_recv()

    def result(self, h):
        total = self.part(self.me, h)[...].astype(F32)
        for n in range(3 if self.relay is None else 2):
            total = total + self.fin[n, h].astype(F32)
        return total.astype(BF16)

    def drain(self):
        for copy in self.copies:
            copy.wait_send()


def sum_shapes(wide, relays):
    vm, dma, part = pltpu.VMEM, pltpu.SemaphoreType.DMA, wide // 2
    shapes = dict(
        buf=vm((4, 8, 2, 16, wide), BF16),
        fin_a=vm((3, 2, 2, 2, 16, wide), BF16), fin_b=vm((3, 2, 2, 4, 16, part), BF16),
        a1=vm((4, 2, 16, wide), BF16), b1=vm((4, 4, 16, part), BF16),
        fin_a2=vm((3, 2, 2, 16, part), BF16), fin_b2=vm((3, 2, 2, 16, part), BF16),
        zbuf=vm((8, 16, part), BF16), zrecv=vm((7, 16, part), BF16), gath=vm((4, 16, part), BF16),
        ss_ring=dma((4, 6)), rs_ring=dma((4, 6)), ss_z=dma((7,)), rs_z=dma((7,)), ss_g=dma((3,)), rs_g=dma((3,)),
    )
    if relays:
        shapes.update(relay_a=vm((2, 2, 2, 16, wide), BF16), relay_b=vm((2, 2, 4, 16, part), BF16))
    return shapes


class Sum:
    def __init__(self, ref):
        self.ref = ref
        x, z, y_hi, y_lo, core = places()
        self.place = (x, z, y_hi, y_lo, core)
        y = y_hi * 2 + y_lo
        part = ref.zbuf.shape[-1]

        def lanes(lo):
            return pl.ds(pl.multiple_of(lo * part, 128), part)

        def dev_x(i):
            return device(i, z, y_hi, y_lo, core)

        def dev_y(i):
            return device(x, z, i // 2, i % 2, core)

        sems = [(ref.ss_ring.at[i], ref.rs_ring.at[i]) for i in range(4)]
        relay_a, relay_b = getattr(ref, "relay_a", None), getattr(ref, "relay_b", None)
        self.a = Ring(x, dev_x, lambda i, h: ref.buf.at[i, pl.ds(2 * h, 2)], relay_a, ref.fin_a, *sems[0])
        self.b = Ring(
            y, dev_y, lambda i, h: ref.buf.at[pl.ds(2 * h, 2), pl.ds(4, 4), i // 2, :, lanes(i % 2)],
            relay_b, ref.fin_b, *sems[1],
        )
        self.a2 = Ring(
            y, dev_y, lambda i, h: ref.a1.at[pl.ds(2 * h, 2), i // 2, :, lanes(i % 2)],
            None, ref.fin_a2, *sems[2],
        )
        self.b2 = Ring(x, dev_x, lambda i, h: ref.b1.at[i, pl.ds(2 * h, 2)], None, ref.fin_b2, *sems[3])
        self.copies = []

    def put(self, at, upper, lower):
        width = upper.shape[-1]
        both = jnp.concatenate([upper, lower], axis=1).astype(BF16)
        self.ref.buf[:, :, :, :, at : at + width] = both.reshape(4, 8, 2, 16, width)

    def start(self):
        self.a.start()
        self.b.start()

    def middle(self):
        self.a.middle()
        self.b.middle()

    def second(self):
        self.a.finish()
        for h in range(2):
            self.ref.a1[2 * h : 2 * h + 2] = self.a.result(h)
        self.a2.start()
        self.b.finish()
        for h in range(2):
            self.ref.b1[2 * h : 2 * h + 2] = self.b.result(h)
        self.b2.start()

    def along_z(self):
        ref = self.ref
        x, z, y_hi, y_lo, core = self.place
        self.a2.finish()
        for h in range(2):
            ref.zbuf[2 * h : 2 * h + 2] = self.a2.result(h)
        self.b2.finish()
        for h in range(2):
            ref.zbuf[4 + 2 * h : 6 + 2 * h] = self.b2.result(h)
        for d in range(1, 8):
            to = (z + d) % 8
            self.copies.append(
                remote(ref.zbuf.at[to], ref.zrecv.at[d - 1], ref.ss_z.at[d - 1], ref.rs_z.at[d - 1],
                       device(x, to, y_hi, y_lo, core))
            )

    def gather(self):
        ref = self.ref
        x, z, y_hi, y_lo, core = self.place
        total = ref.zbuf[z].astype(F32)
        for d in range(7):
            self.copies[d].wait_recv()
            total = total + ref.zrecv[d].astype(F32)
        mine = y_lo * 2 + core
        ref.gath[mine] = total.astype(BF16)
        self.copies += share(ref.gath, ref.ss_g, ref.rs_g)

    def finish(self):
        for copy in self.copies[7:]:
            copy.wait_recv()
        gath = self.ref.gath
        return [jnp.concatenate([gath[c].astype(F32), gath[2 + c].astype(F32)], axis=1) for c in range(2)]

    def drain(self):
        for copy in self.copies:
            copy.wait_send()
        for ring in (self.a, self.b, self.a2, self.b2):
            ring.drain()


def share(ref, send_sem, recv_sem):
    x, z, y_hi, y_lo, core = places()
    mine = y_lo * 2 + core
    return [
        remote(ref.at[mine], ref.at[mine], send_sem.at[n], recv_sem.at[n],
               device(x, z, y_hi, (y_lo + dy) % 2, (core + dc) % 2))
        for n, (dy, dc) in enumerate(((1, 1), (1, 0), (0, 1)))
    ]


def far_first(k, half):
    return half + ((k + 1) // 2) * (1 - 2 * (k % 2))


class Exchange:
    def __init__(self, send, recv, ss, rs, parts=False):
        self.send, self.recv, self.ss, self.rs, self.parts = send, recv, ss, rs, parts

    def landing(self, to):
        return self.recv.at[to % 4] if self.parts else self.recv

    def start(self):
        me = lax.axis_index("slab")
        x, z, y_hi, y_lo, core = places()

        def one(n, carry):
            kz, kx, ky = n // 8, (n // 2) % 4, n % 2
            dz, dx = far_first(kz, 4), far_first(kx, 2)
            to = device((x + dx) % 4, (z + dz) % 8, (y_hi + 1 - ky) % 2, y_lo, core)
            remote(self.send.at[to[0]], self.landing(to[0]).at[me], self.ss, self.rs, to)
            return carry

        lax.fori_loop(0, SLABS - 1, one, 0)
        self.landing(me)[me] = self.send[me]

    def wait(self):
        got = self.send.at[pl.ds(0, SLABS - 1)]
        pltpu.make_async_copy(got, got, self.rs).wait()

    def drain(self):
        sent = self.send.at[pl.ds(0, SLABS - 1)]
        pltpu.make_async_copy(sent, sent, self.ss).wait()


def by_pair(blocks):
    width = blocks[0].shape[-1]
    return jnp.stack([b.reshape(16, 8, width) for b in blocks], axis=1).reshape(SLABS, 8, width)


def scratch():
    vm, dma = pltpu.VMEM, pltpu.SemaphoreType.DMA
    return dict(
        wq=vm((512, 1536), BF16), wo=vm((512, 512), BF16), wu=vm((512, 2048), BF16), wd=vm((2048, 512), BF16),
        sw=dma((4,)),
        qkv=vm((128, 1536), BF16),
        qsend=vm((SLABS, 8, 384), BF16), qrecv=vm((SLABS, 8, 384), BF16),
        osend=vm((SLABS, 8, 128), BF16), orecv=vm((SLABS, 8, 128), BF16),
        gsend=vm((SLABS, 8, 128), BF16), grecv=vm((SLABS, 8, 128), BF16),
        dsend=vm((SLABS, 8, 384), BF16), drecv=vm((SLABS, 8, 384), BF16),
        hsend=vm((SLABS, 8, 128), BF16), hline=vm((4, SLABS, 8, 128), BF16), ss_h=dma((3,)), rs_h=dma((3,)),
        psend=vm((SLABS, 8, 384), BF16), precv=vm((SLABS, 8, 384), BF16), pgath=vm((4, 8, 1536), BF16),
        ss_x=dma((6,)), rs_x=dma((6,)), ss_p=dma((3,)), rs_p=dma((3,)),
        z32=vm((3, 512, 128), F32), o32=vm((512, 128), F32), g32=vm((512, 128), F32), d32=vm((3, 512, 128), F32),
        px=vm((4, 128, 256), F32), py=vm((4, 128, 256), F32), pz=vm((4, 128, 256), F32),
        oxy=vm((128, 512), F32), dxy=vm((128, 1536), F32), gmix=vm((128, 512), BF16),
        gact=vm((128, 2048), F32), flat=vm((128, 512), F32), gres=vm((128, 512), F32),
        b_h1=vm((256, 512), BF16), b_mixed=vm((256, 512), BF16), b_h2=vm((256, 512), BF16), b_act=vm((256, 2048), BF16),
        cot=vm((128, 512), BF16), gu=vm((128, 2048), BF16), grb=vm((128, 512), BF16), gp=vm((128, 1536), BF16),
        b_cot=vm((256, 256), BF16), b_gu=vm((256, 1024), BF16), b_grb=vm((256, 256), BF16), b_gp=vm((256, 768), BF16),
        ss_core=dma((8,)), rs_core=dma((8,)),
        down32=vm((SLABS, 32, 256), F32),
        one=sum_shapes(1024, True), two=sum_shapes(512, False),
    )


def kernel(factor, tree, tok, cot, wq_h, wo_h, wu_h, wd_h, ga, gm, o_tok, o_qkv, o_out, o_up, o_down, o_g1, o_g2, *refs):
    r = jax.tree.unflatten(tree, refs)
    r, r_one, r_two = types.SimpleNamespace(**r), types.SimpleNamespace(**r["one"]), types.SimpleNamespace(**r["two"])
    x, z, y_hi, y_lo, core = places()
    slab, case = lax.axis_index("slab"), lax.axis_index("case")
    other = device(x, z, y_hi, y_lo, 1 - core)

    loads = [
        pltpu.make_async_copy(src, dst, r.sw.at[n])
        for n, (src, dst) in enumerate(((wq_h, r.wq), (wo_h, r.wo), (wd_h, r.wd), (wu_h, r.wu)))
    ]
    for load in loads:
        load.start()

    barrier = pltpu.get_barrier_semaphore()

    def greet(d, carry):
        pl.semaphore_signal(barrier, inc=1, device_id=((slab + d) % SLABS, case), device_id_type=MESH)
        return carry

    lax.fori_loop(1, SLABS, greet, 0)
    for peer in (
        other,
        device(x, z, y_hi, 1 - y_lo, core),
        device(x, z, y_hi, 1 - y_lo, 1 - core),
        device(x, z, 1 - y_hi, 1 - y_lo, core),
    ):
        pl.semaphore_signal(barrier, inc=1, device_id=peer, device_id_type=MESH)

    gain_one, gain_two = ga[...], gm[...]
    r.flat[...] = to_rows(tok[...].astype(F32))
    normed_one, inverse_one = norm_stats(r.flat[...])
    hidden_one = normed_one * gain_one
    r.b_h1[0:128, :] = hidden_one.astype(BF16)
    r.hsend[...] = by_pair([hidden_one[:, 128 * j : 128 * j + 128] for j in range(4)]).astype(BF16)
    r.cot[...] = to_rows(cot[...].astype(F32)).astype(BF16)
    loads[0].wait()
    for i in range(3):
        r.qkv[:, 512 * i : 512 * i + 512] = nn(r.b_h1[0:128, :], r.wq[:, 512 * i : 512 * i + 512]).astype(BF16)
    for i in range(3):
        r.qsend[:, :, 128 * i : 128 * i + 128] = by_pair(
            [r.qkv[:, 512 * i + 128 * j : 512 * i + 128 * j + 128].astype(F32) for j in range(4)]
        ).astype(BF16)
    pl.semaphore_wait(barrier, SLABS + 3)
    ex_q = Exchange(r.qsend, r.qrecv, r.ss_x.at[0], r.rs_x.at[0])
    ex_o = Exchange(r.osend, r.orecv, r.ss_x.at[1], r.rs_x.at[1])
    ex_g = Exchange(r.gsend, r.grecv, r.ss_x.at[2], r.rs_x.at[2])
    ex_d = Exchange(r.dsend, r.drecv, r.ss_x.at[3], r.rs_x.at[3])
    ex_h = Exchange(r.hsend, r.hline, r.ss_x.at[4], r.rs_x.at[4], parts=True)
    ex_p = Exchange(r.psend, r.precv, r.ss_x.at[5], r.rs_x.at[5])
    ex_q.start()

    core_copies = []

    def to_core_full(ref):
        n = len(core_copies)
        core_copies.append(
            remote(ref.at[pl.ds(0, 128)], ref.at[pl.ds(128, 128)], r.ss_core.at[n], r.rs_core.at[n], other)
        )

    def to_core_half(src, dst):
        n, half = len(core_copies), dst.shape[-1]
        theirs = src.at[:, pl.ds(pl.multiple_of((1 - core) * half, 128), half)]
        core_copies.append(remote(theirs, dst.at[pl.ds(128, 128)], r.ss_core.at[n], r.rs_core.at[n], other))
        dst[0:128, :] = src[:, pl.ds(pl.multiple_of(core * half, 128), half)]

    to_core_full(r.b_h1)
    to_core_half(r.cot, r.b_cot)

    def pair(j):
        return [r.qkv[:, 512 * i + 128 * j : 512 * i + 128 * j + 128] for i in range(3)]

    mask_x, mask_y = line_masks()
    for j in range(4):
        queries, keys, values = pair(j)
        scores = pair_scores(queries, keys)
        r.px[j] = line_probs(scores, mask_x)
        r.py[j] = line_probs(scores, mask_y)
        r.oxy[:, 128 * j : 128 * j + 128] = pair_out((r.px[j] + r.py[j]).astype(BF16), values)

    loads[2].wait()
    for i in range(4):
        at = slice(512 * i, 512 * i + 512)
        r.gact[:, at] = nt(r.cot[...], r.wd[at, :])

    ex_q.wait()
    for i in range(3):
        r.z32[i] = r.qrecv[:, :, 128 * i : 128 * i + 128].astype(F32).reshape(512, 128)

    def line(j):
        return [r.z32[i, pl.ds(j, 128, stride=4), :].astype(BF16) for i in range(3)]

    for j in range(4):
        queries, keys, values = line(j)
        probs = line_probs(pair_scores(queries, keys), None)
        r.pz[j] = probs
        r.o32[pl.ds(j, 128, stride=4), :] = pair_out(probs.astype(BF16), values)
    r.osend[...] = r.o32[...].reshape(SLABS, 8, 128).astype(BF16)
    ex_o.start()
    ex_h.start()

    loads[1].wait()
    loads[3].wait()
    ex_o.wait()
    from_z = r.orecv[...].astype(F32).reshape(16, 4, 8, 128)
    for j in range(4):
        at = slice(128 * j, 128 * j + 128)
        r.b_mixed[0:128, at] = (r.oxy[:, at] + from_z[:, j].reshape(128, 128)).astype(BF16)
    residual = (r.flat[...] + nn(r.b_mixed[0:128, :], r.wo[...])).astype(BF16)
    normed_two, inverse_two = norm_stats(residual.astype(F32))
    r.b_h2[0:128, :] = (normed_two * gain_two).astype(BF16)
    ex_h.wait()
    h_at, h_copies = slab % 4, []
    for n, (dz, dy) in enumerate(((1, 1), (0, 1), (1, 0))):
        to = device(x, z + dz * (1 - 2 * (z % 2)), (y_hi + dy) % 2, y_lo, core)
        h_copies.append(remote(r.hline.at[h_at], r.hline.at[h_at], r.ss_h.at[n], r.rs_h.at[n], to))
    to_core_full(r.b_h2)
    to_core_full(r.b_mixed)
    grad_hidden_two = jnp.zeros((128, 512), F32)
    for i in range(4):
        at = slice(512 * i, 512 * i + 512)
        u = nn(r.b_h2[0:128, :], r.wu[:, at])
        square = u * u
        tangent = jnp.tanh(ROOT * u * (1.0 + 0.044715 * square))
        half = 0.5 * (1.0 + tangent)
        r.b_act[0:128, at] = (u * half).astype(BF16)
        slope = half + 0.5 * u * (1.0 - tangent * tangent) * ROOT * (1.0 + 3.0 * 0.044715 * square)
        r.gu[:, at] = (r.gact[:, at] * slope).astype(BF16)
        grad_hidden_two = grad_hidden_two + nt(r.gu[:, at], r.wu[:, at])
    r.gres[...] = r.cot[...].astype(F32) + norm_back(grad_hidden_two, normed_two, inverse_two, gain_two)
    r.grb[...] = r.gres[...].astype(BF16)
    r.gmix[...] = nt(r.grb[...], r.wo[...]).astype(BF16)
    r.gsend[...] = by_pair([r.gmix[:, 128 * j : 128 * j + 128].astype(F32) for j in range(4)]).astype(BF16)
    to_core_full(r.b_act)
    to_core_half(r.gu, r.b_gu)
    to_core_half(r.grb, r.b_grb)
    ex_g.start()

    one, two = Sum(r_one), Sum(r_two)
    for copy in core_copies[1:6]:
        copy.wait_recv()
    r.down32[...] = tn(r.b_act[...], r.b_cot[...]).reshape(SLABS, 32, 256)
    for i in range(2):
        one.put(
            256 * i,
            tn(r.b_h2[...], r.b_gu[:, 256 * i : 256 * i + 256]).reshape(SLABS, 8, 256),
            tn(r.b_h2[...], r.b_gu[:, 512 + 256 * i : 768 + 256 * i]).reshape(SLABS, 8, 256),
        )
    one.put(512, r.down32[:, 0:8, :], r.down32[:, 16:24, :])
    one.put(768, r.down32[:, 8:16, :], r.down32[:, 24:32, :])
    one.start()

    for j in range(4):
        queries, keys, values = pair(j)
        grads = r.gmix[:, 128 * j : 128 * j + 128]
        grad_probs = nt(values, two_heads(grads))
        probs_x, probs_y = r.px[j], r.py[j]
        grad_scores = (score_grads(probs_x, grad_probs) + score_grads(probs_y, grad_probs)).astype(BF16)
        back = pair_back((probs_x + probs_y).astype(BF16), grad_scores, queries, keys, grads)
        for i in range(3):
            at = slice(512 * i + 128 * j, 512 * i + 128 * j + 128)
            r.dxy[:, at] = back[i]
            r.gp[:, at] = back[i].astype(BF16)
    to_core_half(r.gp, r.b_gp)

    for copy in core_copies[0:1] + core_copies[6:]:
        copy.wait_recv()

    def qkv_part(i):
        return tn(r.b_h1[...], r.b_gp[:, 256 * i : 256 * i + 256]).reshape(SLABS, 8, 256)

    two.put(0, qkv_part(0), qkv_part(1))
    two.put(256, qkv_part(2), tn(r.b_mixed[...], r.b_grb[...]).reshape(SLABS, 8, 256))
    two.start()
    one.middle()

    ex_g.wait()
    r.g32[...] = r.grecv[...].astype(F32).reshape(512, 128)
    for j in range(4):
        queries, keys, values = line(j)
        grads = r.g32[pl.ds(j, 128, stride=4), :].astype(BF16)
        probs = r.pz[j]
        grad_scores = score_grads(probs, nt(values, two_heads(grads))).astype(BF16)
        back = pair_back(probs.astype(BF16), grad_scores, queries, keys, grads)
        for i in range(3):
            r.d32[i, pl.ds(j, 128, stride=4), :] = back[i]

    for i in range(3):
        r.dsend[:, :, 128 * i : 128 * i + 128] = r.d32[i].reshape(SLABS, 8, 128).astype(BF16)
    ex_d.start()
    two.second()
    one.second()

    for copy in h_copies:
        copy.wait_recv()
    line_grads = jnp.concatenate([r.d32[i].astype(BF16) for i in range(3)], axis=1)
    for i in range(4):
        hidden_lines = r.hline[i].astype(F32).reshape(512, 128).astype(BF16)
        r.psend[16 * i : 16 * i + 16] = tn(hidden_lines, line_grads).reshape(16, 8, 384).astype(BF16)
    ex_p.start()
    two.along_z()
    one.along_z()

    ex_d.wait()
    for i in range(3):
        from_z = r.drecv[:, :, 128 * i : 128 * i + 128].astype(F32).reshape(16, 4, 8, 128)
        for j in range(4):
            at = slice(512 * i + 128 * j, 512 * i + 128 * j + 128)
            r.dxy[:, at] = r.dxy[:, at] + from_z[:, j].reshape(128, 128)
    grad_hidden_one = nt(r.dxy[...].astype(BF16), r.wq[...])
    normed_one, inverse_one = norm_stats(r.flat[...])
    first, second = to_grid(r.gres[...] + norm_back(grad_hidden_one, normed_one, inverse_one, gain_one))
    o_tok[0] = first.astype(BF16)
    o_tok[1] = second.astype(BF16)

    two.gather()
    one.gather()
    ex_p.wait()
    lines = jnp.sum(r.precv[...].astype(F32).reshape(16, 4, 8, 384), axis=0).astype(BF16)
    case_at = y_lo * 2 + core
    for i in range(3):
        for j in range(4):
            at = 512 * i + 128 * j
            r.pgath[case_at, :, at : at + 128] = lines[j, :, 128 * i : 128 * i + 128]
    p_copies = share(r.pgath, r.ss_p, r.rs_p)

    own_rows = pl.ds(pl.multiple_of((slab // 2) * 16, 16), 16)

    def weight_rows(ref):
        both = ref[own_rows, :].astype(F32)
        return jnp.where(slab % 2 == 0, both[0:8], both[8:16])

    for c, full in enumerate(one.finish()):
        full = full * factor
        o_up[:, 1024 * c : 1024 * c + 512] = full[0:8, 0:512]
        o_up[:, 1024 * c + 512 : 1024 * c + 1024] = full[8:16, 0:512]
        at = slice(256 * c, 256 * c + 256)
        o_down[0:8, at] = full[0:8, 512:768]
        o_down[8:16, at] = full[0:8, 768:1024]
        o_down[16:24, at] = full[8:16, 512:768]
        o_down[24:32, at] = full[8:16, 768:1024]

    def over_gain(rows, gain):
        lane = lax.broadcasted_iota(jnp.int32, (8, 512), 1)
        row = lax.broadcasted_iota(jnp.int32, (8, 512), 0)
        own = jnp.sum(jnp.where(lane == slab * 8 + row, gain, 0.0), axis=1, keepdims=True)
        return jnp.broadcast_to(jnp.sum(rows, axis=1, keepdims=True) / own, (8, 128))

    o_g2[...] = over_gain(o_up[...] * weight_rows(r.wu), gain_two)
    for copy in p_copies:
        copy.wait_recv()
    o_qkv[...] = jnp.sum(r.pgath[...].astype(F32), axis=0) * factor
    for c, full in enumerate(two.finish()):
        full = full * factor
        o_qkv[:, 768 * c : 768 * c + 256] += full[0:8, 0:256]
        o_qkv[:, 768 * c + 256 : 768 * c + 512] += full[8:16, 0:256]
        o_qkv[:, 768 * c + 512 : 768 * c + 768] += full[0:8, 256:512]
        o_out[:, 256 * c : 256 * c + 256] = full[8:16, 256:512]
    o_g1[...] = over_gain(o_qkv[...] * weight_rows(r.wq), gain_one)

    for exchange in (ex_q, ex_o, ex_h, ex_g, ex_p, ex_d):
        exchange.drain()
    for copy in core_copies + h_copies + p_copies:
        copy.wait_send()
    one.drain()
    two.drain()


def results_kernel(tok, qkv, out, up, down, g1, g2, o_tok, o_qkv, o_out, o_up, o_down, o_g1, o_g2):
    for src, dst in ((tok, o_tok), (qkv, o_qkv), (out, o_out), (up, o_up), (down, o_down)):
        dst[...] = src[...]
    row = lax.broadcasted_iota(jnp.int32, (8, 128), 0)
    lane = lax.broadcasted_iota(jnp.int32, (8, 128), 1)
    for src, dst in ((g1, o_g1), (g2, o_g2)):
        dst[...] = jnp.sum(jnp.where(row == lane, src[...], 0.0), axis=0)[0:8]


def body(tokens, cotangent, w_qkv, w_out, w_up, w_down, gain_attn, gain_mlp):
    width = tokens.shape[-1]
    factor = 1.0 / math.sqrt(128 * lax.axis_size("slab") * lax.axis_size("case"))
    shapes = scratch()
    leaves, tree = jax.tree.flatten(shapes)
    vmem, any_space = pl.BlockSpec(memory_space=pltpu.VMEM), pl.BlockSpec(memory_space=pl.ANY)
    outs = ((8, 1536), (8, 512), (8, 2048), (32, 512), (8, 128), (8, 128))
    result = pl.pallas_call(
        functools.partial(kernel, factor, tree),
        out_shape=[jax.ShapeDtypeStruct((2, 8, 8, width), BF16)] + [jax.ShapeDtypeStruct(s, F32) for s in outs],
        in_specs=[vmem, vmem] + [any_space] * 4 + [vmem, vmem],
        out_specs=[vmem] * 7,
        scratch_shapes=leaves,
        compiler_params=pltpu.CompilerParams(
            collective_id=1, has_side_effects=True, vmem_limit_bytes=56 * 1024 * 1024
        ),
        cost_estimate=pl.CostEstimate(flops=3_500_000_000, bytes_accessed=7_000_000, transcendentals=0),
    )(
        tokens.reshape(2, 8, 8, width),
        cotangent.reshape(2, 8, 8, width),
        w_qkv,
        w_out,
        w_up,
        w_down,
        gain_attn.reshape(1, width),
        gain_mlp.reshape(1, width),
    )
    result = pl.pallas_call(
        results_kernel,
        out_shape=[jax.ShapeDtypeStruct((2, 8, 8, width), BF16)]
        + [jax.ShapeDtypeStruct(s, F32) for s in outs[:4] + ((8,), (8,))],
        in_specs=[vmem] * 7,
        out_specs=[vmem] * 7,
    )(*result)
    return (result[0].reshape(tokens.shape), *result[1:])


def solution(mesh):
    grid = P("case", "slab", None, None, None)
    return jax.shard_map(
        body,
        mesh=mesh,
        in_specs=(grid, grid, P(), P(), P(), P(), P(), P()),
        out_specs=(grid, P("slab", None), P("slab", None), P("slab", None), P("slab", None), P("slab"), P("slab")),
        check_vma=False,
    )
```

```python
import functools
import math
import types

import jax
import jax.numpy as jnp
from jax import lax
from jax.experimental import pallas as pl
from jax.experimental.pallas import tpu as pltpu
from jax.sharding import PartitionSpec as P

MESH = pl.DeviceIdType.MESH
F32 = jnp.float32
BF16 = jnp.bfloat16
EPSILON = 1e-06
ROOT = math.sqrt(2.0 / math.pi)
LOWEST = -1e30
SLABS = 64


def places():
    slab, case = lax.axis_index("slab"), lax.axis_index("case")
    return slab // 16, (slab // 2) % 8, slab % 2, case // 2, case % 2


def device(x, z, y_hi, y_lo, core):
    return ((x * 8 + z) * 2 + y_hi, y_lo * 2 + core)


def remote(src, dst, send_sem, recv_sem, to):
    copy = pltpu.make_async_remote_copy(
        src_ref=src, dst_ref=dst, send_sem=send_sem, recv_sem=recv_sem, device_id=to, device_id_type=MESH
    )
    copy.start()
    return copy


def nn(a, b):
    return lax.dot_general(a, b, (((1,), (0,)), ((), ())), preferred_element_type=F32)


def nt(a, b):
    return lax.dot_general(a, b, (((1,), (1,)), ((), ())), preferred_element_type=F32)


def tn(a, b):
    return lax.dot_general(a, b, (((0,), (0,)), ((), ())), preferred_element_type=F32)


def to_rows(grid):
    first, second = grid[0], grid[1]
    low = lax.broadcasted_iota(jnp.int32, first.shape, 1) < 4
    even = jnp.where(low, first, pltpu.roll(second, 4, 1))
    odd = jnp.where(low, pltpu.roll(first, 4, 1), second)
    return jnp.stack([even, odd], axis=1).reshape(128, first.shape[-1])


def to_grid(rows):
    split = rows.reshape(8, 2, 8, rows.shape[-1])
    even, odd = split[:, 0], split[:, 1]
    low = lax.broadcasted_iota(jnp.int32, even.shape, 1) < 4
    first = jnp.where(low, even, pltpu.roll(odd, 4, 1))
    second = jnp.where(low, pltpu.roll(even, 4, 1), odd)
    return first, second


def norm_stats(values):
    inverse = lax.rsqrt(jnp.mean(values * values, axis=-1, keepdims=True) + EPSILON)
    return values * inverse, inverse


def norm_back(grad_normed, normed, inverse, gain):
    scaled = grad_normed * gain
    return inverse * (scaled - normed * jnp.mean(scaled * normed, axis=-1, keepdims=True))


def two_heads(pair):
    lane = lax.broadcasted_iota(jnp.int32, (128, 128), 1)
    first = jnp.where(lane < 64, 1.0, 0.0).astype(BF16)
    second = jnp.where(lane < 64, 0.0, 1.0).astype(BF16)
    return jnp.concatenate([pair * first, pair * second], axis=0)


def over_keys(across):
    return jnp.concatenate([across[:, 0:128], across[:, 128:256]], axis=0)


def line_probs(scores, mask):
    if mask is not None:
        scores = jnp.where(mask, scores, LOWEST)
    weights = jnp.exp(scores - jnp.max(scores, axis=0, keepdims=True))
    return weights * (1.0 / jnp.sum(weights, axis=0, keepdims=True))


def line_masks():
    keys = lax.broadcasted_iota(jnp.int32, (128, 256), 0)
    queries = lax.broadcasted_iota(jnp.int32, (128, 256), 1) & 127
    apart = keys ^ queries
    return (apart & 0x74) == 0, (apart & 0x0F) == 0


def pair_scores(queries, keys):
    return nt(keys, two_heads(queries * jnp.array(0.125, BF16)))


def pair_out(probs, values):
    return tn(over_keys(probs), two_heads(values))


def score_grads(probs, grad_probs):
    return probs * (grad_probs - jnp.sum(probs * grad_probs, axis=0, keepdims=True))


def pair_back(rounded, grad_scores, queries, keys, grads):
    both = two_heads(grads)
    grad_values = nn(rounded, both)
    grad_keys = nn(grad_scores, two_heads(queries * jnp.array(0.125, BF16)))
    grad_queries = tn(over_keys(grad_scores), two_heads(keys)) * 0.125
    return grad_queries, grad_keys, grad_values


class Ring:
    def __init__(self, me, dev, part, relay, fin, ss, rs):
        self.me, self.dev, self.part, self.relay, self.fin, self.ss, self.rs = me, dev, part, relay, fin, ss, rs
        self.right, self.left, self.over = (me + 1) % 4, (me + 3) % 4, (me + 2) % 4
        self.copies = []

    def send(self, src, dst, to):
        n = len(self.copies)
        self.copies.append(remote(src, dst, self.ss.at[n], self.rs.at[n], self.dev(to)))

    def start(self):
        if self.relay is None:
            for n, to in enumerate((self.over, self.right, self.left)):
                for h in range(2):
                    self.send(self.part(to, h), self.fin.at[n, h], to)
            return
        self.send(self.part(self.over, 0), self.relay.at[0], self.right)
        self.send(self.part(self.over, 1), self.relay.at[1], self.left)
        self.send(self.part(self.right, 1), self.fin.at[0, 1], self.right)
        self.send(self.part(self.left, 0), self.fin.at[0, 0], self.left)

    def middle(self):
        for h, to in ((0, self.right), (1, self.left)):
            self.copies[h].wait_recv()
            ref = self.part(to, h)
            ref[...] = (ref[...].astype(F32) + self.relay[h].astype(F32)).astype(BF16)
            self.send(ref, self.fin.at[1, h], to)

    def finish(self):
        for copy in self.copies[0 if self.relay is None else 2 :]:
            copy.wait_recv()

    def result(self, h):
        total = self.part(self.me, h)[...].astype(F32)
        for n in range(3 if self.relay is None else 2):
            total = total + self.fin[n, h].astype(F32)
        return total.astype(BF16)

    def drain(self):
        for copy in self.copies:
            copy.wait_send()


def sum_shapes(wide, relays):
    vm, dma, part = pltpu.VMEM, pltpu.SemaphoreType.DMA, wide // 2
    shapes = dict(
        buf=vm((4, 8, 2, 16, wide), BF16),
        fin_a=vm((3, 2, 2, 2, 16, wide), BF16), fin_b=vm((3, 2, 2, 4, 16, part), BF16),
        a1=vm((4, 2, 16, wide), BF16), b1=vm((4, 4, 16, part), BF16),
        fin_a2=vm((3, 2, 2, 16, part), BF16), fin_b2=vm((3, 2, 2, 16, part), BF16),
        zbuf=vm((8, 16, part), BF16), zrecv=vm((7, 16, part), BF16), gath=vm((4, 16, part), BF16),
        ss_ring=dma((4, 6)), rs_ring=dma((4, 6)), ss_z=dma((7,)), rs_z=dma((7,)), ss_g=dma((3,)), rs_g=dma((3,)),
    )
    if relays:
        shapes.update(relay_a=vm((2, 2, 2, 16, wide), BF16), relay_b=vm((2, 2, 4, 16, part), BF16))
    return shapes


class Sum:
    def __init__(self, ref):
        self.ref = ref
        x, z, y_hi, y_lo, core = places()
        self.place = (x, z, y_hi, y_lo, core)
        y = y_hi * 2 + y_lo
        part = ref.zbuf.shape[-1]

        def lanes(lo):
            return pl.ds(pl.multiple_of(lo * part, 128), part)

        def dev_x(i):
            return device(i, z, y_hi, y_lo, core)

        def dev_y(i):
            return device(x, z, i // 2, i % 2, core)

        sems = [(ref.ss_ring.at[i], ref.rs_ring.at[i]) for i in range(4)]
        relay_a, relay_b = getattr(ref, "relay_a", None), getattr(ref, "relay_b", None)
        self.a = Ring(x, dev_x, lambda i, h: ref.buf.at[i, pl.ds(2 * h, 2)], relay_a, ref.fin_a, *sems[0])
        self.b = Ring(
            y, dev_y, lambda i, h: ref.buf.at[pl.ds(2 * h, 2), pl.ds(4, 4), i // 2, :, lanes(i % 2)],
            relay_b, ref.fin_b, *sems[1],
        )
        self.a2 = Ring(
            y, dev_y, lambda i, h: ref.a1.at[pl.ds(2 * h, 2), i // 2, :, lanes(i % 2)],
            None, ref.fin_a2, *sems[2],
        )
        self.b2 = Ring(x, dev_x, lambda i, h: ref.b1.at[i, pl.ds(2 * h, 2)], None, ref.fin_b2, *sems[3])
        self.copies = []

    def put(self, at, upper, lower):
        width = upper.shape[-1]
        both = jnp.concatenate([upper, lower], axis=1).astype(BF16)
        self.ref.buf[:, :, :, :, at : at + width] = both.reshape(4, 8, 2, 16, width)

    def start(self):
        self.a.start()
        self.b.start()

    def middle(self):
        self.a.middle()
        self.b.middle()

    def second(self):
        self.a.finish()
        for h in range(2):
            self.ref.a1[2 * h : 2 * h + 2] = self.a.result(h)
        self.a2.start()
        self.b.finish()
        for h in range(2):
            self.ref.b1[2 * h : 2 * h + 2] = self.b.result(h)
        self.b2.start()

    def along_z(self):
        ref = self.ref
        x, z, y_hi, y_lo, core = self.place
        self.a2.finish()
        for h in range(2):
            ref.zbuf[2 * h : 2 * h + 2] = self.a2.result(h)
        self.b2.finish()
        for h in range(2):
            ref.zbuf[4 + 2 * h : 6 + 2 * h] = self.b2.result(h)
        for d in range(1, 8):
            to = (z + d) % 8
            self.copies.append(
                remote(ref.zbuf.at[to], ref.zrecv.at[d - 1], ref.ss_z.at[d - 1], ref.rs_z.at[d - 1],
                       device(x, to, y_hi, y_lo, core))
            )

    def gather(self):
        ref = self.ref
        x, z, y_hi, y_lo, core = self.place
        total = ref.zbuf[z].astype(F32)
        for d in range(7):
            self.copies[d].wait_recv()
            total = total + ref.zrecv[d].astype(F32)
        mine = y_lo * 2 + core
        ref.gath[mine] = total.astype(BF16)
        self.copies += share(ref.gath, ref.ss_g, ref.rs_g)

    def finish(self):
        for copy in self.copies[7:]:
            copy.wait_recv()
        gath = self.ref.gath
        return [jnp.concatenate([gath[c].astype(F32), gath[2 + c].astype(F32)], axis=1) for c in range(2)]

    def drain(self):
        for copy in self.copies:
            copy.wait_send()
        for ring in (self.a, self.b, self.a2, self.b2):
            ring.drain()


def share(ref, send_sem, recv_sem):
    x, z, y_hi, y_lo, core = places()
    mine = y_lo * 2 + core
    return [
        remote(ref.at[mine], ref.at[mine], send_sem.at[n], recv_sem.at[n],
               device(x, z, y_hi, (y_lo + dy) % 2, (core + dc) % 2))
        for n, (dy, dc) in enumerate(((1, 1), (1, 0), (0, 1)))
    ]


def far_first(k, half):
    return half + ((k + 1) // 2) * (1 - 2 * (k % 2))


class Exchange:
    def __init__(self, send, recv, ss, rs):
        self.send, self.recv, self.ss, self.rs = send, recv, ss, rs

    def start(self):
        me = lax.axis_index("slab")
        x, z, y_hi, y_lo, core = places()

        def one(n, carry):
            kz, kx, ky = n // 8, (n // 2) % 4, n % 2
            dz, dx = far_first(kz, 4), far_first(kx, 2)
            to = device((x + dx) % 4, (z + dz) % 8, (y_hi + 1 - ky) % 2, y_lo, core)
            remote(self.send.at[to[0]], self.recv.at[me], self.ss, self.rs, to)
            return carry

        lax.fori_loop(0, SLABS - 1, one, 0)
        self.recv[me] = self.send[me]

    def wait(self):
        got = self.send.at[pl.ds(0, SLABS - 1)]
        pltpu.make_async_copy(got, got, self.rs).wait()

    def drain(self):
        sent = self.send.at[pl.ds(0, SLABS - 1)]
        pltpu.make_async_copy(sent, sent, self.ss).wait()


def by_pair(blocks):
    width = blocks[0].shape[-1]
    return jnp.stack([b.reshape(16, 8, width) for b in blocks], axis=1).reshape(SLABS, 8, width)


def scratch():
    vm, dma = pltpu.VMEM, pltpu.SemaphoreType.DMA
    return dict(
        wq=vm((512, 1536), BF16), wo=vm((512, 512), BF16), wu=vm((512, 2048), BF16), wd=vm((2048, 512), BF16),
        sw=dma((8,)),
        tok=vm((2, 8, 8, 512), BF16), cot_in=vm((2, 8, 8, 512), BF16), ga=vm((1, 512), F32), gm=vm((1, 512), F32),
        qkv=vm((128, 1536), BF16),
        qsend=vm((SLABS, 8, 512), BF16), qrecv=vm((SLABS, 8, 512), BF16),
        osend=vm((SLABS, 8, 128), BF16), orecv=vm((SLABS, 8, 128), BF16),
        gsend=vm((SLABS, 8, 128), BF16), grecv=vm((SLABS, 8, 128), BF16),
        dsend=vm((SLABS, 8, 384), BF16), drecv=vm((SLABS, 8, 384), BF16),
        hline=vm((4, SLABS, 8, 128), BF16), ss_h=dma((3,)), rs_h=dma((3,)),
        ss_x=dma((4,)), rs_x=dma((4,)),
        z32=vm((3, 512, 128), F32), o32=vm((512, 128), F32), g32=vm((512, 128), F32), d32=vm((3, 512, 128), F32),
        px=vm((4, 128, 256), F32), py=vm((4, 128, 256), F32), pz=vm((4, 128, 256), F32),
        oxy=vm((128, 512), F32), dxy=vm((128, 1536), F32), gmix=vm((128, 512), BF16),
        gact=vm((128, 2048), F32), flat=vm((128, 512), F32), gres=vm((128, 512), F32),
        b_h1=vm((256, 512), BF16), b_mixed=vm((256, 512), BF16), b_h2=vm((256, 512), BF16), b_act=vm((256, 2048), BF16),
        cot=vm((128, 512), BF16), gu=vm((128, 2048), BF16), grb=vm((128, 512), BF16), gp=vm((128, 1536), BF16),
        b_cot=vm((256, 256), BF16), b_gu=vm((256, 1024), BF16), b_grb=vm((256, 256), BF16), b_gp=vm((256, 768), BF16),
        ss_core=dma((13,)), rs_core=dma((13,)),
        zpart=vm((512, 384), F32), zpart_b=vm((512, 384), BF16), zpeer=vm((2, 512, 128), BF16),
        down32=vm((SLABS, 32, 256), F32), out32=vm((512, 256), F32), qkv32=vm((512, 768), F32),
        one=sum_shapes(1024, True), two=sum_shapes(512, False),
    )


def kernel(factor, tree, tok_h, cot_h, wq_h, wo_h, wu_h, wd_h, ga_h, gm_h, o_tok, o_qkv, o_out, o_up, o_down, o_g1, o_g2, *refs):
    r = jax.tree.unflatten(tree, refs)
    r, r_one, r_two = types.SimpleNamespace(**r), types.SimpleNamespace(**r["one"]), types.SimpleNamespace(**r["two"])
    x, z, y_hi, y_lo, core = places()
    slab, case = lax.axis_index("slab"), lax.axis_index("case")
    other = device(x, z, y_hi, y_lo, 1 - core)

    loads = [
        pltpu.make_async_copy(src, dst, r.sw.at[n])
        for n, (src, dst) in enumerate(
            ((tok_h, r.tok), (ga_h, r.ga), (wq_h, r.wq), (cot_h, r.cot_in), (gm_h, r.gm), (wd_h, r.wd), (wo_h, r.wo), (wu_h, r.wu))
        )
    ]
    for load in loads:
        load.start()

    barrier = pltpu.get_barrier_semaphore()

    def greet(d, carry):
        pl.semaphore_signal(barrier, inc=1, device_id=((slab + d) % SLABS, case), device_id_type=MESH)
        return carry

    lax.fori_loop(1, SLABS, greet, 0)
    for peer in (
        other,
        device(x, z, y_hi, 1 - y_lo, core),
        device(x, z, y_hi, 1 - y_lo, 1 - core),
        device(x, z, 1 - y_hi, 1 - y_lo, core),
    ):
        pl.semaphore_signal(barrier, inc=1, device_id=peer, device_id_type=MESH)

    loads[0].wait()
    loads[1].wait()
    gain_one = r.ga[...]
    r.flat[...] = to_rows(r.tok[...].astype(F32))
    normed_one, inverse_one = norm_stats(r.flat[...])
    hidden_one = normed_one * gain_one
    r.b_h1[0:128, :] = hidden_one.astype(BF16)
    r.qsend[:, :, 384:512] = by_pair([hidden_one[:, 128 * j : 128 * j + 128] for j in range(4)]).astype(BF16)
    loads[2].wait()
    for i in range(3):
        r.qkv[:, 512 * i : 512 * i + 512] = nn(r.b_h1[0:128, :], r.wq[:, 512 * i : 512 * i + 512]).astype(BF16)
    for i in range(3):
        r.qsend[:, :, 128 * i : 128 * i + 128] = by_pair(
            [r.qkv[:, 512 * i + 128 * j : 512 * i + 128 * j + 128].astype(F32) for j in range(4)]
        ).astype(BF16)
    pl.semaphore_wait(barrier, SLABS + 3)
    ex_q = Exchange(r.qsend, r.qrecv, r.ss_x.at[0], r.rs_x.at[0])
    ex_o = Exchange(r.osend, r.orecv, r.ss_x.at[1], r.rs_x.at[1])
    ex_g = Exchange(r.gsend, r.grecv, r.ss_x.at[2], r.rs_x.at[2])
    ex_d = Exchange(r.dsend, r.drecv, r.ss_x.at[3], r.rs_x.at[3])
    ex_q.start()

    core_copies = []

    def to_core_full(ref):
        n = len(core_copies)
        core_copies.append(
            remote(ref.at[pl.ds(0, 128)], ref.at[pl.ds(128, 128)], r.ss_core.at[n], r.rs_core.at[n], other)
        )

    def to_core_half(src, dst):
        n, half = len(core_copies), dst.shape[-1]
        theirs = src.at[:, pl.ds(pl.multiple_of((1 - core) * half, 128), half)]
        core_copies.append(remote(theirs, dst.at[pl.ds(128, 128)], r.ss_core.at[n], r.rs_core.at[n], other))
        dst[0:128, :] = src[:, pl.ds(pl.multiple_of(core * half, 128), half)]

    loads[3].wait()
    loads[4].wait()
    gain_two = r.gm[...]
    r.cot[...] = to_rows(r.cot_in[...].astype(F32)).astype(BF16)
    to_core_full(r.b_h1)
    to_core_half(r.cot, r.b_cot)

    def pair(j):
        return [r.qkv[:, 512 * i + 128 * j : 512 * i + 128 * j + 128] for i in range(3)]

    mask_x, mask_y = line_masks()
    for j in range(4):
        queries, keys, values = pair(j)
        scores = pair_scores(queries, keys)
        r.px[j] = line_probs(scores, mask_x)
        r.py[j] = line_probs(scores, mask_y)
        r.oxy[:, 128 * j : 128 * j + 128] = pair_out((r.px[j] + r.py[j]).astype(BF16), values)

    loads[5].wait()
    for i in range(4):
        at = slice(512 * i, 512 * i + 512)
        r.gact[:, at] = nt(r.cot[...], r.wd[at, :])

    ex_q.wait()
    for i in range(3):
        r.z32[i] = r.qrecv[:, :, 128 * i : 128 * i + 128].astype(F32).reshape(512, 128)

    def line(j):
        return [r.z32[i, pl.ds(j, 128, stride=4), :].astype(BF16) for i in range(3)]

    for j in range(4):
        queries, keys, values = line(j)
        probs = line_probs(pair_scores(queries, keys), None)
        r.pz[j] = probs
        r.o32[pl.ds(j, 128, stride=4), :] = pair_out(probs.astype(BF16), values)
    r.osend[...] = r.o32[...].reshape(SLABS, 8, 128).astype(BF16)
    ex_o.start()
    r.hline[slab % 4] = r.qrecv[:, :, 384:512]

    loads[6].wait()
    loads[7].wait()
    ex_o.wait()
    h_at, h_copies = slab % 4, []
    for n, (dz, dy) in enumerate(((1, 1), (0, 1), (1, 0))):
        to = device(x, z + dz * (1 - 2 * (z % 2)), (y_hi + dy) % 2, y_lo, core)
        h_copies.append(remote(r.hline.at[h_at], r.hline.at[h_at], r.ss_h.at[n], r.rs_h.at[n], to))
    from_z = r.orecv[...].astype(F32).reshape(16, 4, 8, 128)
    for j in range(4):
        at = slice(128 * j, 128 * j + 128)
        r.b_mixed[0:128, at] = (r.oxy[:, at] + from_z[:, j].reshape(128, 128)).astype(BF16)
    residual = (r.flat[...] + nn(r.b_mixed[0:128, :], r.wo[...])).astype(BF16)
    normed_two, inverse_two = norm_stats(residual.astype(F32))
    r.b_h2[0:128, :] = (normed_two * gain_two).astype(BF16)
    to_core_full(r.b_h2)
    to_core_full(r.b_mixed)
    grad_hidden_two = jnp.zeros((128, 512), F32)
    for i in range(4):
        at = slice(512 * i, 512 * i + 512)
        u = nn(r.b_h2[0:128, :], r.wu[:, at])
        square = u * u
        tangent = jnp.tanh(ROOT * u * (1.0 + 0.044715 * square))
        half = 0.5 * (1.0 + tangent)
        r.b_act[0:128, at] = (u * half).astype(BF16)
        act = r.b_act.at[:, at]
        to_core_full(act)
        slope = half + 0.5 * u * (1.0 - tangent * tangent) * ROOT * (1.0 + 3.0 * 0.044715 * square)
        r.gu[:, at] = (r.gact[:, at] * slope).astype(BF16)
        grad_hidden_two = grad_hidden_two + nt(r.gu[:, at], r.wu[:, at])
    r.gres[...] = r.cot[...].astype(F32) + norm_back(grad_hidden_two, normed_two, inverse_two, gain_two)
    r.grb[...] = r.gres[...].astype(BF16)
    r.gmix[...] = nt(r.grb[...], r.wo[...]).astype(BF16)
    r.gsend[...] = by_pair([r.gmix[:, 128 * j : 128 * j + 128].astype(F32) for j in range(4)]).astype(BF16)
    to_core_half(r.gu, r.b_gu)
    to_core_half(r.grb, r.b_grb)

    ex_g.start()

    one, two = Sum(r_one), Sum(r_two)
    for copy in core_copies[1:10]:
        copy.wait_recv()
    r.down32[...] = tn(r.b_act[...], r.b_cot[...]).reshape(SLABS, 32, 256)
    for i in range(2):
        one.put(
            256 * i,
            tn(r.b_h2[...], r.b_gu[:, 256 * i : 256 * i + 256]).reshape(SLABS, 8, 256),
            tn(r.b_h2[...], r.b_gu[:, 512 + 256 * i : 768 + 256 * i]).reshape(SLABS, 8, 256),
        )
    one.put(512, r.down32[:, 0:8, :], r.down32[:, 16:24, :])
    one.put(768, r.down32[:, 8:16, :], r.down32[:, 24:32, :])
    one.start()

    for j in range(4):
        queries, keys, values = pair(j)
        grads = r.gmix[:, 128 * j : 128 * j + 128]
        grad_probs = nt(values, two_heads(grads))
        probs_x, probs_y = r.px[j], r.py[j]
        grad_scores = (score_grads(probs_x, grad_probs) + score_grads(probs_y, grad_probs)).astype(BF16)
        back = pair_back((probs_x + probs_y).astype(BF16), grad_scores, queries, keys, grads)
        for i in range(3):
            at = slice(512 * i + 128 * j, 512 * i + 128 * j + 128)
            r.dxy[:, at] = back[i]
            r.gp[:, at] = back[i].astype(BF16)
    to_core_half(r.gp, r.b_gp)

    r.out32[...] = tn(r.b_mixed[...], r.b_grb[...])
    for copy in core_copies[0:1] + core_copies[10:]:
        copy.wait_recv()
    for i in range(3):
        at = slice(256 * i, 256 * i + 256)
        r.qkv32[:, at] = tn(r.b_h1[...], r.b_gp[:, at])

    ex_g.wait()
    r.g32[...] = r.grecv[...].astype(F32).reshape(512, 128)
    for j in range(4):
        queries, keys, values = line(j)
        grads = r.g32[pl.ds(j, 128, stride=4), :].astype(BF16)
        probs = r.pz[j]
        grad_scores = score_grads(probs, nt(values, two_heads(grads))).astype(BF16)
        back = pair_back(probs.astype(BF16), grad_scores, queries, keys, grads)
        for i in range(3):
            r.d32[i, pl.ds(j, 128, stride=4), :] = back[i]

    for copy in h_copies:
        copy.wait_recv()
    line_grads = jnp.concatenate([r.d32[i].astype(BF16) for i in range(3)], axis=1)
    for i in range(4):
        hidden_lines = r.hline[i].astype(F32).reshape(512, 128).astype(BF16)
        r.zpart[128 * i : 128 * i + 128, :] = tn(hidden_lines, line_grads)
    r.zpart_b[...] = r.zpart[...].astype(BF16)

    def outer(owner):
        return pl.ds(pl.multiple_of(owner * 256, 128), 128)

    z_copies = [
        remote(r.zpart_b.at[:, outer(1 - core)], r.zpeer.at[0], r.ss_core.at[11], r.rs_core.at[11], other),
        remote(r.zpart_b.at[:, pl.ds(128, 128)], r.zpeer.at[1], r.ss_core.at[12], r.rs_core.at[12], other),
    ]
    one.middle()
    pair_at = slab % 4
    at_outer = pl.ds(pl.multiple_of(core * 256 + pair_at * 128, 128), 128)
    at_keys = pl.ds(pl.multiple_of((1 - core) * 512 + (pair_at % 2) * 128, 128), 128)
    owned = jnp.where(core == pair_at // 2, 1.0, 0.0)
    z_copies[0].wait_recv()
    r.qkv32[:, at_outer] = r.qkv32[:, at_outer] + (r.zpart[:, outer(core)] + r.zpeer[0].astype(F32))
    z_copies[1].wait_recv()
    r.qkv32[:, at_keys] = r.qkv32[:, at_keys] + owned * (r.zpart[:, 128:256] + r.zpeer[1].astype(F32))

    def rows(ref, at):
        return ref[:, at : at + 256].reshape(SLABS, 8, 256)

    two.put(0, rows(r.qkv32, 0), rows(r.qkv32, 256))
    two.put(256, rows(r.qkv32, 512), rows(r.out32, 0))
    two.start()
    for i in range(3):
        r.dsend[:, :, 128 * i : 128 * i + 128] = r.d32[i].reshape(SLABS, 8, 128).astype(BF16)
    one.second()
    ex_d.start()
    two.second()
    one.along_z()
    two.along_z()

    ex_d.wait()
    for i in range(3):
        from_z = r.drecv[:, :, 128 * i : 128 * i + 128].astype(F32).reshape(16, 4, 8, 128)
        for j in range(4):
            at = slice(512 * i + 128 * j, 512 * i + 128 * j + 128)
            r.dxy[:, at] = r.dxy[:, at] + from_z[:, j].reshape(128, 128)
    grad_hidden_one = nt(r.dxy[...].astype(BF16), r.wq[...])
    normed_one, inverse_one = norm_stats(r.flat[...])
    first, second = to_grid(r.gres[...] + norm_back(grad_hidden_one, normed_one, inverse_one, gain_one))
    o_tok[0] = first.astype(BF16)
    o_tok[1] = second.astype(BF16)

    one.gather()
    two.gather()

    own_rows = pl.ds(pl.multiple_of((slab // 2) * 16, 16), 16)

    def weight_rows(ref):
        both = ref[own_rows, :].astype(F32)
        return jnp.where(slab % 2 == 0, both[0:8], both[8:16])

    for c, full in enumerate(one.finish()):
        full = full * factor
        o_up[:, 1024 * c : 1024 * c + 512] = full[0:8, 0:512]
        o_up[:, 1024 * c + 512 : 1024 * c + 1024] = full[8:16, 0:512]
        at = slice(256 * c, 256 * c + 256)
        o_down[0:8, at] = full[0:8, 512:768]
        o_down[8:16, at] = full[0:8, 768:1024]
        o_down[16:24, at] = full[8:16, 512:768]
        o_down[24:32, at] = full[8:16, 768:1024]

    def over_gain(rows, gain):
        lane = lax.broadcasted_iota(jnp.int32, (8, 512), 1)
        row = lax.broadcasted_iota(jnp.int32, (8, 512), 0)
        own = jnp.sum(jnp.where(lane == slab * 8 + row, gain, 0.0), axis=1, keepdims=True)
        return jnp.broadcast_to(jnp.sum(rows, axis=1, keepdims=True) / own, (8, 128))

    o_g2[...] = over_gain(o_up[...] * weight_rows(r.wu), gain_two)
    for c, full in enumerate(two.finish()):
        full = full * factor
        o_qkv[:, 768 * c : 768 * c + 256] = full[0:8, 0:256]
        o_qkv[:, 768 * c + 256 : 768 * c + 512] = full[8:16, 0:256]
        o_qkv[:, 768 * c + 512 : 768 * c + 768] = full[0:8, 256:512]
        o_out[:, 256 * c : 256 * c + 256] = full[8:16, 256:512]
    o_g1[...] = over_gain(o_qkv[...] * weight_rows(r.wq), gain_one)

    for exchange in (ex_q, ex_o, ex_g, ex_d):
        exchange.drain()
    for copy in core_copies + h_copies + z_copies:
        copy.wait_send()
    one.drain()
    two.drain()


def results_kernel(tok, qkv, out, up, down, g1, g2, o_tok, o_qkv, o_out, o_up, o_down, o_g1, o_g2):
    for src, dst in ((tok, o_tok), (qkv, o_qkv), (out, o_out), (up, o_up), (down, o_down)):
        dst[...] = src[...]
    row = lax.broadcasted_iota(jnp.int32, (8, 128), 0)
    lane = lax.broadcasted_iota(jnp.int32, (8, 128), 1)
    for src, dst in ((g1, o_g1), (g2, o_g2)):
        dst[...] = jnp.sum(jnp.where(row == lane, src[...], 0.0), axis=0)[0:8]


def body(tokens, cotangent, w_qkv, w_out, w_up, w_down, gain_attn, gain_mlp):
    width = tokens.shape[-1]
    factor = 1.0 / math.sqrt(128 * lax.axis_size("slab") * lax.axis_size("case"))
    shapes = scratch()
    leaves, tree = jax.tree.flatten(shapes)
    vmem, any_space = pl.BlockSpec(memory_space=pltpu.VMEM), pl.BlockSpec(memory_space=pl.ANY)
    outs = ((8, 1536), (8, 512), (8, 2048), (32, 512), (8, 128), (8, 128))
    result = pl.pallas_call(
        functools.partial(kernel, factor, tree),
        out_shape=[jax.ShapeDtypeStruct((2, 8, 8, width), BF16)] + [jax.ShapeDtypeStruct(s, F32) for s in outs],
        in_specs=[any_space] * 8,
        out_specs=[vmem] * 7,
        scratch_shapes=leaves,
        compiler_params=pltpu.CompilerParams(
            collective_id=1, has_side_effects=True, vmem_limit_bytes=56 * 1024 * 1024
        ),
        cost_estimate=pl.CostEstimate(flops=3_500_000_000, bytes_accessed=7_000_000, transcendentals=0),
    )(
        tokens.reshape(2, 8, 8, width),
        cotangent.reshape(2, 8, 8, width),
        w_qkv,
        w_out,
        w_up,
        w_down,
        gain_attn.reshape(1, width),
        gain_mlp.reshape(1, width),
    )
    result = pl.pallas_call(
        results_kernel,
        out_shape=[jax.ShapeDtypeStruct((2, 8, 8, width), BF16)]
        + [jax.ShapeDtypeStruct(s, F32) for s in outs[:4] + ((8,), (8,))],
        in_specs=[vmem] * 7,
        out_specs=[vmem] * 7,
    )(*result)
    return (result[0].reshape(tokens.shape), *result[1:])


def solution(mesh):
    grid = P("case", "slab", None, None, None)
    return jax.shard_map(
        body,
        mesh=mesh,
        in_specs=(grid, grid, P(), P(), P(), P(), P(), P()),
        out_specs=(grid, P("slab", None), P("slab", None), P("slab", None), P("slab", None), P("slab"), P("slab")),
        check_vma=False,
    )
```

```python
import functools
import math
import types

import jax
import jax.numpy as jnp
from jax import lax
from jax.experimental import pallas as pl
from jax.experimental.pallas import tpu as pltpu
from jax.sharding import PartitionSpec as P

MESH = pl.DeviceIdType.MESH
F32 = jnp.float32
BF16 = jnp.bfloat16
EPSILON = 1e-06
ROOT = math.sqrt(2.0 / math.pi)
LOWEST = -1e30
SLABS = 64


def places():
    slab, case = lax.axis_index("slab"), lax.axis_index("case")
    return slab // 16, (slab // 2) % 8, slab % 2, case // 2, case % 2


def device(x, z, y_hi, y_lo, core):
    return ((x * 8 + z) * 2 + y_hi, y_lo * 2 + core)


def remote(src, dst, send_sem, recv_sem, to):
    copy = pltpu.make_async_remote_copy(
        src_ref=src, dst_ref=dst, send_sem=send_sem, recv_sem=recv_sem, device_id=to, device_id_type=MESH
    )
    copy.start()
    return copy


def nn(a, b):
    return lax.dot_general(a, b, (((1,), (0,)), ((), ())), preferred_element_type=F32)


def nt(a, b):
    return lax.dot_general(a, b, (((1,), (1,)), ((), ())), preferred_element_type=F32)


def tn(a, b):
    return lax.dot_general(a, b, (((0,), (0,)), ((), ())), preferred_element_type=F32)


def to_rows(grid):
    first, second = grid[0], grid[1]
    low = lax.broadcasted_iota(jnp.int32, first.shape, 1) < 4
    even = jnp.where(low, first, pltpu.roll(second, 4, 1))
    odd = jnp.where(low, pltpu.roll(first, 4, 1), second)
    return jnp.stack([even, odd], axis=1).reshape(128, first.shape[-1])


def to_grid(rows):
    split = rows.reshape(8, 2, 8, rows.shape[-1])
    even, odd = split[:, 0], split[:, 1]
    low = lax.broadcasted_iota(jnp.int32, even.shape, 1) < 4
    first = jnp.where(low, even, pltpu.roll(odd, 4, 1))
    second = jnp.where(low, pltpu.roll(even, 4, 1), odd)
    return first, second


def norm_stats(values):
    inverse = lax.rsqrt(jnp.mean(values * values, axis=-1, keepdims=True) + EPSILON)
    return values * inverse, inverse


def norm_back(grad_normed, normed, inverse, gain):
    scaled = grad_normed * gain
    return inverse * (scaled - normed * jnp.mean(scaled * normed, axis=-1, keepdims=True))


def two_heads(pair):
    lane = lax.broadcasted_iota(jnp.int32, (128, 128), 1)
    first = jnp.where(lane < 64, 1.0, 0.0).astype(BF16)
    second = jnp.where(lane < 64, 0.0, 1.0).astype(BF16)
    return jnp.concatenate([pair * first, pair * second], axis=0)


def over_keys(across):
    return jnp.concatenate([across[:, 0:128], across[:, 128:256]], axis=0)


def line_probs(scores, mask):
    if mask is not None:
        scores = jnp.where(mask, scores, LOWEST)
    weights = jnp.exp(scores - jnp.max(scores, axis=0, keepdims=True))
    return weights * (1.0 / jnp.sum(weights, axis=0, keepdims=True))


def line_masks():
    keys = lax.broadcasted_iota(jnp.int32, (128, 256), 0)
    queries = lax.broadcasted_iota(jnp.int32, (128, 256), 1) & 127
    apart = keys ^ queries
    return (apart & 0x74) == 0, (apart & 0x0F) == 0


def pair_scores(queries, keys):
    return nt(keys, two_heads(queries * jnp.array(0.125, BF16)))


def pair_out(probs, values):
    return tn(over_keys(probs), two_heads(values))


def score_grads(probs, grad_probs):
    return probs * (grad_probs - jnp.sum(probs * grad_probs, axis=0, keepdims=True))


def pair_back(rounded, grad_scores, queries, keys, grads):
    both = two_heads(grads)
    grad_values = nn(rounded, both)
    grad_keys = nn(grad_scores, two_heads(queries * jnp.array(0.125, BF16)))
    grad_queries = tn(over_keys(grad_scores), two_heads(keys)) * 0.125
    return grad_queries, grad_keys, grad_values


class Ring:
    def __init__(self, me, dev, part, relay, fin, ss, rs):
        self.me, self.dev, self.part, self.relay, self.fin, self.ss, self.rs = me, dev, part, relay, fin, ss, rs
        self.right, self.left, self.over = (me + 1) % 4, (me + 3) % 4, (me + 2) % 4
        self.copies = []

    def send(self, src, dst, to):
        n = len(self.copies)
        self.copies.append(remote(src, dst, self.ss.at[n], self.rs.at[n], self.dev(to)))

    def start(self):
        if self.relay is None:
            for n, to in enumerate((self.over, self.right, self.left)):
                for h in range(2):
                    self.send(self.part(to, h), self.fin.at[n, h], to)
            return
        self.send(self.part(self.over, 0), self.relay.at[0], self.right)
        self.send(self.part(self.over, 1), self.relay.at[1], self.left)
        self.send(self.part(self.right, 1), self.fin.at[0, 1], self.right)
        self.send(self.part(self.left, 0), self.fin.at[0, 0], self.left)

    def middle(self):
        for h, to in ((0, self.right), (1, self.left)):
            self.copies[h].wait_recv()
            ref = self.part(to, h)
            ref[...] = (ref[...].astype(F32) + self.relay[h].astype(F32)).astype(BF16)
            self.send(ref, self.fin.at[1, h], to)

    def finish(self):
        for copy in self.copies[0 if self.relay is None else 2 :]:
            copy.wait_recv()

    def result(self, h):
        total = self.part(self.me, h)[...].astype(F32)
        for n in range(3 if self.relay is None else 2):
            total = total + self.fin[n, h].astype(F32)
        return total.astype(BF16)

    def drain(self):
        for copy in self.copies:
            copy.wait_send()


def sum_shapes(wide, relays):
    vm, dma, part = pltpu.VMEM, pltpu.SemaphoreType.DMA, wide // 2
    shapes = dict(
        buf=vm((4, 8, 2, 16, wide), BF16),
        fin_a=vm((3, 2, 2, 2, 16, wide), BF16), fin_b=vm((3, 2, 2, 4, 16, part), BF16),
        a1=vm((4, 2, 16, wide), BF16), b1=vm((4, 4, 16, part), BF16),
        fin_a2=vm((3, 2, 2, 16, part), BF16), fin_b2=vm((3, 2, 2, 16, part), BF16),
        zbuf=vm((8, 16, part), BF16), zrecv=vm((7, 16, part), BF16), gath=vm((4, 16, part), BF16),
        ss_ring=dma((4, 6)), rs_ring=dma((4, 6)), ss_z=dma((7,)), rs_z=dma((7,)), ss_g=dma((3,)), rs_g=dma((3,)),
    )
    if relays:
        shapes.update(relay_a=vm((2, 2, 2, 16, wide), BF16), relay_b=vm((2, 2, 4, 16, part), BF16))
    return shapes


class Sum:
    def __init__(self, ref):
        self.ref = ref
        x, z, y_hi, y_lo, core = places()
        self.place = (x, z, y_hi, y_lo, core)
        y = y_hi * 2 + y_lo
        part = ref.zbuf.shape[-1]

        def lanes(lo):
            return pl.ds(pl.multiple_of(lo * part, 128), part)

        def dev_x(i):
            return device(i, z, y_hi, y_lo, core)

        def dev_y(i):
            return device(x, z, i // 2, i % 2, core)

        sems = [(ref.ss_ring.at[i], ref.rs_ring.at[i]) for i in range(4)]
        relay_a, relay_b = getattr(ref, "relay_a", None), getattr(ref, "relay_b", None)
        self.a = Ring(x, dev_x, lambda i, h: ref.buf.at[i, pl.ds(2 * h, 2)], relay_a, ref.fin_a, *sems[0])
        self.b = Ring(
            y, dev_y, lambda i, h: ref.buf.at[pl.ds(2 * h, 2), pl.ds(4, 4), i // 2, :, lanes(i % 2)],
            relay_b, ref.fin_b, *sems[1],
        )
        self.a2 = Ring(
            y, dev_y, lambda i, h: ref.a1.at[pl.ds(2 * h, 2), i // 2, :, lanes(i % 2)],
            None, ref.fin_a2, *sems[2],
        )
        self.b2 = Ring(x, dev_x, lambda i, h: ref.b1.at[i, pl.ds(2 * h, 2)], None, ref.fin_b2, *sems[3])
        self.copies = []

    def put(self, at, upper, lower):
        width = upper.shape[-1]
        both = jnp.concatenate([upper, lower], axis=1).astype(BF16)
        self.ref.buf[:, :, :, :, at : at + width] = both.reshape(4, 8, 2, 16, width)

    def start(self):
        self.a.start()
        self.b.start()

    def middle(self):
        self.a.middle()
        self.b.middle()

    def second(self):
        self.a.finish()
        for h in range(2):
            self.ref.a1[2 * h : 2 * h + 2] = self.a.result(h)
        self.a2.start()
        self.b.finish()
        for h in range(2):
            self.ref.b1[2 * h : 2 * h + 2] = self.b.result(h)
        self.b2.start()

    def along_z(self):
        ref = self.ref
        x, z, y_hi, y_lo, core = self.place
        self.a2.finish()
        for h in range(2):
            ref.zbuf[2 * h : 2 * h + 2] = self.a2.result(h)
        self.b2.finish()
        for h in range(2):
            ref.zbuf[4 + 2 * h : 6 + 2 * h] = self.b2.result(h)
        for d in range(1, 8):
            to = (z + d) % 8
            self.copies.append(
                remote(ref.zbuf.at[to], ref.zrecv.at[d - 1], ref.ss_z.at[d - 1], ref.rs_z.at[d - 1],
                       device(x, to, y_hi, y_lo, core))
            )

    def gather(self):
        ref = self.ref
        x, z, y_hi, y_lo, core = self.place
        total = ref.zbuf[z].astype(F32)
        for d in range(7):
            self.copies[d].wait_recv()
            total = total + ref.zrecv[d].astype(F32)
        mine = y_lo * 2 + core
        ref.gath[mine] = total.astype(BF16)
        self.copies += share(ref.gath, ref.ss_g, ref.rs_g)

    def finish(self):
        for copy in self.copies[7:]:
            copy.wait_recv()
        gath = self.ref.gath
        return [jnp.concatenate([gath[c].astype(F32), gath[2 + c].astype(F32)], axis=1) for c in range(2)]

    def drain(self):
        for copy in self.copies:
            copy.wait_send()
        for ring in (self.a, self.b, self.a2, self.b2):
            ring.drain()


def share(ref, send_sem, recv_sem):
    x, z, y_hi, y_lo, core = places()
    mine = y_lo * 2 + core
    return [
        remote(ref.at[mine], ref.at[mine], send_sem.at[n], recv_sem.at[n],
               device(x, z, y_hi, (y_lo + dy) % 2, (core + dc) % 2))
        for n, (dy, dc) in enumerate(((1, 1), (1, 0), (0, 1)))
    ]


def far_first(k, half):
    return half + ((k + 1) // 2) * (1 - 2 * (k % 2))


class Exchange:
    def __init__(self, send, recv, ss, rs):
        self.send, self.recv, self.ss, self.rs = send, recv, ss, rs

    def start(self):
        me = lax.axis_index("slab")
        x, z, y_hi, y_lo, core = places()

        def one(n, carry):
            kz, kx, ky = n // 8, (n // 2) % 4, n % 2
            dz, dx = far_first(kz, 4), far_first(kx, 2)
            to = device((x + dx) % 4, (z + dz) % 8, (y_hi + 1 - ky) % 2, y_lo, core)
            remote(self.send.at[to[0]], self.recv.at[me], self.ss, self.rs, to)
            return carry

        lax.fori_loop(0, SLABS - 1, one, 0)
        self.recv[me] = self.send[me]

    def wait(self):
        got = self.send.at[pl.ds(0, SLABS - 1)]
        pltpu.make_async_copy(got, got, self.rs).wait()

    def drain(self):
        sent = self.send.at[pl.ds(0, SLABS - 1)]
        pltpu.make_async_copy(sent, sent, self.ss).wait()


def by_pair(blocks):
    width = blocks[0].shape[-1]
    return jnp.stack([b.reshape(16, 8, width) for b in blocks], axis=1).reshape(SLABS, 8, width)


def scratch():
    vm, dma = pltpu.VMEM, pltpu.SemaphoreType.DMA
    return dict(
        wq=vm((512, 1536), BF16), wo=vm((512, 512), BF16), wu=vm((512, 2048), BF16), wd=vm((2048, 512), BF16),
        sw=dma((8,)),
        tok=vm((2, 8, 8, 512), BF16), cot_in=vm((2, 8, 8, 512), BF16), ga=vm((1, 512), F32), gm=vm((1, 512), F32),
        qkv=vm((128, 1536), BF16),
        qsend=vm((SLABS, 8, 384), BF16), qrecv=vm((SLABS, 8, 384), BF16),
        hsend=vm((SLABS, 8, 128), BF16), hrecv=vm((SLABS, 8, 128), BF16),
        osend=vm((SLABS, 8, 128), BF16), orecv=vm((SLABS, 8, 128), BF16),
        gsend=vm((SLABS, 8, 128), BF16), grecv=vm((SLABS, 8, 128), BF16),
        dsend=vm((SLABS, 8, 384), BF16), drecv=vm((SLABS, 8, 384), BF16),
        hline=vm((4, SLABS, 8, 128), BF16), ss_h=dma((3,)), rs_h=dma((3,)),
        ss_x=dma((5,)), rs_x=dma((5,)),
        z32=vm((3, 512, 128), F32), o32=vm((512, 128), F32), g32=vm((512, 128), F32), d32=vm((3, 512, 128), F32),
        px=vm((4, 128, 256), F32), py=vm((4, 128, 256), F32), pz=vm((4, 128, 256), F32),
        oxy=vm((128, 512), F32), dxy=vm((128, 1536), F32), gmix=vm((128, 512), BF16),
        gact=vm((128, 2048), F32), flat=vm((128, 512), F32), gres=vm((128, 512), F32),
        b_h1=vm((256, 512), BF16), b_mixed=vm((256, 512), BF16), b_h2=vm((256, 512), BF16), b_act=vm((256, 2048), BF16),
        cot=vm((128, 512), BF16), gu=vm((128, 2048), BF16), grb=vm((128, 512), BF16), gp=vm((128, 1536), BF16),
        b_cot=vm((256, 256), BF16), b_gu=vm((256, 1024), BF16), b_grb=vm((256, 256), BF16), b_gp=vm((256, 768), BF16),
        ss_core=dma((13,)), rs_core=dma((13,)),
        zpart=vm((512, 384), F32), zpart_b=vm((512, 384), BF16), zpeer=vm((2, 512, 128), BF16),
        down32=vm((SLABS, 32, 256), F32), out32=vm((512, 256), F32), qkv32=vm((512, 768), F32),
        one=sum_shapes(1024, True), two=sum_shapes(512, False),
    )


def kernel(factor, tree, tok_h, cot_h, wq_h, wo_h, wu_h, wd_h, ga_h, gm_h, o_tok, o_qkv, o_out, o_up, o_down, o_g1, o_g2, *refs):
    r = jax.tree.unflatten(tree, refs)
    r, r_one, r_two = types.SimpleNamespace(**r), types.SimpleNamespace(**r["one"]), types.SimpleNamespace(**r["two"])
    x, z, y_hi, y_lo, core = places()
    slab, case = lax.axis_index("slab"), lax.axis_index("case")
    other = device(x, z, y_hi, y_lo, 1 - core)

    loads = [
        pltpu.make_async_copy(src, dst, r.sw.at[n])
        for n, (src, dst) in enumerate(
            ((tok_h, r.tok), (ga_h, r.ga), (wq_h, r.wq), (cot_h, r.cot_in), (gm_h, r.gm), (wd_h, r.wd), (wo_h, r.wo), (wu_h, r.wu))
        )
    ]
    for load in loads[0:5]:
        load.start()

    barrier = pltpu.get_barrier_semaphore()

    def greet(d, carry):
        pl.semaphore_signal(barrier, inc=1, device_id=((slab + d) % SLABS, case), device_id_type=MESH)
        return carry

    lax.fori_loop(1, SLABS, greet, 0)
    for peer in (
        other,
        device(x, z, y_hi, 1 - y_lo, core),
        device(x, z, y_hi, 1 - y_lo, 1 - core),
        device(x, z, 1 - y_hi, 1 - y_lo, core),
    ):
        pl.semaphore_signal(barrier, inc=1, device_id=peer, device_id_type=MESH)

    loads[0].wait()
    loads[1].wait()
    gain_one = r.ga[...]
    r.flat[...] = to_rows(r.tok[...].astype(F32))
    normed_one, inverse_one = norm_stats(r.flat[...])
    hidden_one = normed_one * gain_one
    r.b_h1[0:128, :] = hidden_one.astype(BF16)
    r.hsend[...] = by_pair([hidden_one[:, 128 * j : 128 * j + 128] for j in range(4)]).astype(BF16)
    loads[2].wait()
    for i in range(3):
        r.qkv[:, 512 * i : 512 * i + 512] = nn(r.b_h1[0:128, :], r.wq[:, 512 * i : 512 * i + 512]).astype(BF16)
    for i in range(3):
        r.qsend[:, :, 128 * i : 128 * i + 128] = by_pair(
            [r.qkv[:, 512 * i + 128 * j : 512 * i + 128 * j + 128].astype(F32) for j in range(4)]
        ).astype(BF16)
    for load in loads[5:]:
        load.start()
    pl.semaphore_wait(barrier, SLABS + 3)
    ex_q = Exchange(r.qsend, r.qrecv, r.ss_x.at[0], r.rs_x.at[0])
    ex_o = Exchange(r.osend, r.orecv, r.ss_x.at[1], r.rs_x.at[1])
    ex_g = Exchange(r.gsend, r.grecv, r.ss_x.at[2], r.rs_x.at[2])
    ex_d = Exchange(r.dsend, r.drecv, r.ss_x.at[3], r.rs_x.at[3])
    ex_h = Exchange(r.hsend, r.hrecv, r.ss_x.at[4], r.rs_x.at[4])
    ex_q.start()
    ex_h.start()

    core_copies = []

    def to_core_full(ref):
        n = len(core_copies)
        core_copies.append(
            remote(ref.at[pl.ds(0, 128)], ref.at[pl.ds(128, 128)], r.ss_core.at[n], r.rs_core.at[n], other)
        )

    def to_core_half(src, dst):
        n, half = len(core_copies), dst.shape[-1]
        theirs = src.at[:, pl.ds(pl.multiple_of((1 - core) * half, 128), half)]
        core_copies.append(remote(theirs, dst.at[pl.ds(128, 128)], r.ss_core.at[n], r.rs_core.at[n], other))
        dst[0:128, :] = src[:, pl.ds(pl.multiple_of(core * half, 128), half)]

    loads[3].wait()
    loads[4].wait()
    gain_two = r.gm[...]
    r.cot[...] = to_rows(r.cot_in[...].astype(F32)).astype(BF16)
    to_core_full(r.b_h1)
    to_core_half(r.cot, r.b_cot)

    def pair(j):
        return [r.qkv[:, 512 * i + 128 * j : 512 * i + 128 * j + 128] for i in range(3)]

    mask_x, mask_y = line_masks()
    for j in range(4):
        queries, keys, values = pair(j)
        scores = pair_scores(queries, keys)
        r.px[j] = line_probs(scores, mask_x)
        r.py[j] = line_probs(scores, mask_y)
        r.oxy[:, 128 * j : 128 * j + 128] = pair_out((r.px[j] + r.py[j]).astype(BF16), values)

    loads[5].wait()
    for i in range(4):
        at = slice(512 * i, 512 * i + 512)
        r.gact[:, at] = nt(r.cot[...], r.wd[at, :])

    ex_q.wait()
    for i in range(3):
        r.z32[i] = r.qrecv[:, :, 128 * i : 128 * i + 128].astype(F32).reshape(512, 128)

    def line(j):
        return [r.z32[i, pl.ds(j, 128, stride=4), :].astype(BF16) for i in range(3)]

    for j in range(4):
        queries, keys, values = line(j)
        probs = line_probs(pair_scores(queries, keys), None)
        r.pz[j] = probs
        r.o32[pl.ds(j, 128, stride=4), :] = pair_out(probs.astype(BF16), values)
    r.osend[...] = r.o32[...].reshape(SLABS, 8, 128).astype(BF16)
    ex_o.start()
    ex_h.wait()
    r.hline[slab % 4] = r.hrecv[...]

    loads[6].wait()
    loads[7].wait()
    ex_o.wait()
    h_at, h_copies = slab % 4, []
    for n, (dz, dy) in enumerate(((1, 1), (0, 1), (1, 0))):
        to = device(x, z + dz * (1 - 2 * (z % 2)), (y_hi + dy) % 2, y_lo, core)
        h_copies.append(remote(r.hline.at[h_at], r.hline.at[h_at], r.ss_h.at[n], r.rs_h.at[n], to))
    from_z = r.orecv[...].astype(F32).reshape(16, 4, 8, 128)
    for j in range(4):
        at = slice(128 * j, 128 * j + 128)
        r.b_mixed[0:128, at] = (r.oxy[:, at] + from_z[:, j].reshape(128, 128)).astype(BF16)
    residual = (r.flat[...] + nn(r.b_mixed[0:128, :], r.wo[...])).astype(BF16)
    normed_two, inverse_two = norm_stats(residual.astype(F32))
    r.b_h2[0:128, :] = (normed_two * gain_two).astype(BF16)
    to_core_full(r.b_h2)
    to_core_full(r.b_mixed)
    grad_hidden_two = jnp.zeros((128, 512), F32)
    for i in range(4):
        at = slice(512 * i, 512 * i + 512)
        u = nn(r.b_h2[0:128, :], r.wu[:, at])
        square = u * u
        tangent = jnp.tanh(ROOT * u * (1.0 + 0.044715 * square))
        half = 0.5 * (1.0 + tangent)
        r.b_act[0:128, at] = (u * half).astype(BF16)
        act = r.b_act.at[:, at]
        to_core_full(act)
        slope = half + 0.5 * u * (1.0 - tangent * tangent) * ROOT * (1.0 + 3.0 * 0.044715 * square)
        r.gu[:, at] = (r.gact[:, at] * slope).astype(BF16)
        grad_hidden_two = grad_hidden_two + nt(r.gu[:, at], r.wu[:, at])
    r.gres[...] = r.cot[...].astype(F32) + norm_back(grad_hidden_two, normed_two, inverse_two, gain_two)
    r.grb[...] = r.gres[...].astype(BF16)
    r.gmix[...] = nt(r.grb[...], r.wo[...]).astype(BF16)
    r.gsend[...] = by_pair([r.gmix[:, 128 * j : 128 * j + 128].astype(F32) for j in range(4)]).astype(BF16)
    to_core_half(r.gu, r.b_gu)
    to_core_half(r.grb, r.b_grb)

    ex_g.start()

    one, two = Sum(r_one), Sum(r_two)
    for copy in core_copies[1:10]:
        copy.wait_recv()
    r.down32[...] = tn(r.b_act[...], r.b_cot[...]).reshape(SLABS, 32, 256)
    for i in range(2):
        one.put(
            256 * i,
            tn(r.b_h2[...], r.b_gu[:, 256 * i : 256 * i + 256]).reshape(SLABS, 8, 256),
            tn(r.b_h2[...], r.b_gu[:, 512 + 256 * i : 768 + 256 * i]).reshape(SLABS, 8, 256),
        )
    one.put(512, r.down32[:, 0:8, :], r.down32[:, 16:24, :])
    one.put(768, r.down32[:, 8:16, :], r.down32[:, 24:32, :])
    one.start()

    for j in range(4):
        queries, keys, values = pair(j)
        grads = r.gmix[:, 128 * j : 128 * j + 128]
        grad_probs = nt(values, two_heads(grads))
        probs_x, probs_y = r.px[j], r.py[j]
        grad_scores = (score_grads(probs_x, grad_probs) + score_grads(probs_y, grad_probs)).astype(BF16)
        back = pair_back((probs_x + probs_y).astype(BF16), grad_scores, queries, keys, grads)
        for i in range(3):
            at = slice(512 * i + 128 * j, 512 * i + 128 * j + 128)
            r.dxy[:, at] = back[i]
            r.gp[:, at] = back[i].astype(BF16)
    to_core_half(r.gp, r.b_gp)

    r.out32[...] = tn(r.b_mixed[...], r.b_grb[...])
    for copy in core_copies[0:1] + core_copies[10:]:
        copy.wait_recv()
    for i in range(3):
        at = slice(256 * i, 256 * i + 256)
        r.qkv32[:, at] = tn(r.b_h1[...], r.b_gp[:, at])

    ex_g.wait()
    r.g32[...] = r.grecv[...].astype(F32).reshape(512, 128)
    for j in range(4):
        queries, keys, values = line(j)
        grads = r.g32[pl.ds(j, 128, stride=4), :].astype(BF16)
        probs = r.pz[j]
        grad_scores = score_grads(probs, nt(values, two_heads(grads))).astype(BF16)
        back = pair_back(probs.astype(BF16), grad_scores, queries, keys, grads)
        for i in range(3):
            r.d32[i, pl.ds(j, 128, stride=4), :] = back[i]

    for copy in h_copies:
        copy.wait_recv()
    line_grads = jnp.concatenate([r.d32[i].astype(BF16) for i in range(3)], axis=1)
    for i in range(4):
        hidden_lines = r.hline[i].astype(F32).reshape(512, 128).astype(BF16)
        r.zpart[128 * i : 128 * i + 128, :] = tn(hidden_lines, line_grads)
    r.zpart_b[...] = r.zpart[...].astype(BF16)

    def outer(owner):
        return pl.ds(pl.multiple_of(owner * 256, 128), 128)

    z_copies = [
        remote(r.zpart_b.at[:, outer(1 - core)], r.zpeer.at[0], r.ss_core.at[11], r.rs_core.at[11], other),
        remote(r.zpart_b.at[:, pl.ds(128, 128)], r.zpeer.at[1], r.ss_core.at[12], r.rs_core.at[12], other),
    ]
    one.middle()
    pair_at = slab % 4
    at_outer = pl.ds(pl.multiple_of(core * 256 + pair_at * 128, 128), 128)
    at_keys = pl.ds(pl.multiple_of((1 - core) * 512 + (pair_at % 2) * 128, 128), 128)
    owned = jnp.where(core == pair_at // 2, 1.0, 0.0)
    z_copies[0].wait_recv()
    r.qkv32[:, at_outer] = r.qkv32[:, at_outer] + (r.zpart[:, outer(core)] + r.zpeer[0].astype(F32))
    z_copies[1].wait_recv()
    r.qkv32[:, at_keys] = r.qkv32[:, at_keys] + owned * (r.zpart[:, 128:256] + r.zpeer[1].astype(F32))

    def rows(ref, at):
        return ref[:, at : at + 256].reshape(SLABS, 8, 256)

    two.put(0, rows(r.qkv32, 0), rows(r.qkv32, 256))
    two.put(256, rows(r.qkv32, 512), rows(r.out32, 0))
    two.start()
    for i in range(3):
        r.dsend[:, :, 128 * i : 128 * i + 128] = r.d32[i].reshape(SLABS, 8, 128).astype(BF16)
    one.second()
    ex_d.start()
    two.second()
    one.along_z()
    two.along_z()

    ex_d.wait()
    for i in range(3):
        from_z = r.drecv[:, :, 128 * i : 128 * i + 128].astype(F32).reshape(16, 4, 8, 128)
        for j in range(4):
            at = slice(512 * i + 128 * j, 512 * i + 128 * j + 128)
            r.dxy[:, at] = r.dxy[:, at] + from_z[:, j].reshape(128, 128)
    grad_hidden_one = nt(r.dxy[...].astype(BF16), r.wq[...])
    normed_one, inverse_one = norm_stats(r.flat[...])
    first, second = to_grid(r.gres[...] + norm_back(grad_hidden_one, normed_one, inverse_one, gain_one))
    o_tok[0] = first.astype(BF16)
    o_tok[1] = second.astype(BF16)

    one.gather()
    two.gather()

    own_rows = pl.ds(pl.multiple_of((slab // 2) * 16, 16), 16)

    def weight_rows(ref):
        both = ref[own_rows, :].astype(F32)
        return jnp.where(slab % 2 == 0, both[0:8], both[8:16])

    for c, full in enumerate(one.finish()):
        full = full * factor
        o_up[:, 1024 * c : 1024 * c + 512] = full[0:8, 0:512]
        o_up[:, 1024 * c + 512 : 1024 * c + 1024] = full[8:16, 0:512]
        at = slice(256 * c, 256 * c + 256)
        o_down[0:8, at] = full[0:8, 512:768]
        o_down[8:16, at] = full[0:8, 768:1024]
        o_down[16:24, at] = full[8:16, 512:768]
        o_down[24:32, at] = full[8:16, 768:1024]

    def over_gain(rows, gain):
        lane = lax.broadcasted_iota(jnp.int32, (8, 512), 1)
        row = lax.broadcasted_iota(jnp.int32, (8, 512), 0)
        own = jnp.sum(jnp.where(lane == slab * 8 + row, gain, 0.0), axis=1, keepdims=True)
        return jnp.broadcast_to(jnp.sum(rows, axis=1, keepdims=True) / own, (8, 128))

    o_g2[...] = over_gain(o_up[...] * weight_rows(r.wu), gain_two)
    for c, full in enumerate(two.finish()):
        full = full * factor
        o_qkv[:, 768 * c : 768 * c + 256] = full[0:8, 0:256]
        o_qkv[:, 768 * c + 256 : 768 * c + 512] = full[8:16, 0:256]
        o_qkv[:, 768 * c + 512 : 768 * c + 768] = full[0:8, 256:512]
        o_out[:, 256 * c : 256 * c + 256] = full[8:16, 256:512]
    o_g1[...] = over_gain(o_qkv[...] * weight_rows(r.wq), gain_one)

    for exchange in (ex_q, ex_h, ex_o, ex_g, ex_d):
        exchange.drain()
    for copy in core_copies + h_copies + z_copies:
        copy.wait_send()
    one.drain()
    two.drain()


def results_kernel(tok, qkv, out, up, down, g1, g2, o_tok, o_qkv, o_out, o_up, o_down, o_g1, o_g2):
    for src, dst in ((tok, o_tok), (qkv, o_qkv), (out, o_out), (up, o_up), (down, o_down)):
        dst[...] = src[...]
    row = lax.broadcasted_iota(jnp.int32, (8, 128), 0)
    lane = lax.broadcasted_iota(jnp.int32, (8, 128), 1)
    for src, dst in ((g1, o_g1), (g2, o_g2)):
        dst[...] = jnp.sum(jnp.where(row == lane, src[...], 0.0), axis=0)[0:8]


def body(tokens, cotangent, w_qkv, w_out, w_up, w_down, gain_attn, gain_mlp):
    width = tokens.shape[-1]
    factor = 1.0 / math.sqrt(128 * lax.axis_size("slab") * lax.axis_size("case"))
    shapes = scratch()
    leaves, tree = jax.tree.flatten(shapes)
    vmem, any_space = pl.BlockSpec(memory_space=pltpu.VMEM), pl.BlockSpec(memory_space=pl.ANY)
    outs = ((8, 1536), (8, 512), (8, 2048), (32, 512), (8, 128), (8, 128))
    result = pl.pallas_call(
        functools.partial(kernel, factor, tree),
        out_shape=[jax.ShapeDtypeStruct((2, 8, 8, width), BF16)] + [jax.ShapeDtypeStruct(s, F32) for s in outs],
        in_specs=[any_space] * 8,
        out_specs=[vmem] * 7,
        scratch_shapes=leaves,
        compiler_params=pltpu.CompilerParams(
            collective_id=1, has_side_effects=True, vmem_limit_bytes=56 * 1024 * 1024
        ),
        cost_estimate=pl.CostEstimate(flops=3_500_000_000, bytes_accessed=7_000_000, transcendentals=0),
    )(
        tokens.reshape(2, 8, 8, width),
        cotangent.reshape(2, 8, 8, width),
        w_qkv,
        w_out,
        w_up,
        w_down,
        gain_attn.reshape(1, width),
        gain_mlp.reshape(1, width),
    )
    result = pl.pallas_call(
        results_kernel,
        out_shape=[jax.ShapeDtypeStruct((2, 8, 8, width), BF16)]
        + [jax.ShapeDtypeStruct(s, F32) for s in outs[:4] + ((8,), (8,))],
        in_specs=[vmem] * 7,
        out_specs=[vmem] * 7,
    )(*result)
    return (result[0].reshape(tokens.shape), *result[1:])


def solution(mesh):
    grid = P("case", "slab", None, None, None)
    return jax.shard_map(
        body,
        mesh=mesh,
        in_specs=(grid, grid, P(), P(), P(), P(), P(), P()),
        out_specs=(grid, P("slab", None), P("slab", None), P("slab", None), P("slab", None), P("slab"), P("slab")),
        check_vma=False,
    )
```

```python
import functools
import math
import types

import jax
import jax.numpy as jnp
from jax import lax
from jax.experimental import pallas as pl
from jax.experimental.pallas import tpu as pltpu
from jax.sharding import PartitionSpec as P

MESH = pl.DeviceIdType.MESH
F32 = jnp.float32
BF16 = jnp.bfloat16
EPSILON = 1e-06
ROOT = math.sqrt(2.0 / math.pi)
LOWEST = -1e30
SLABS = 64


def places():
    slab, case = lax.axis_index("slab"), lax.axis_index("case")
    return slab // 16, (slab // 2) % 8, slab % 2, case // 2, case % 2


def device(x, z, y_hi, y_lo, core):
    return ((x * 8 + z) * 2 + y_hi, y_lo * 2 + core)


def remote(src, dst, send_sem, recv_sem, to):
    copy = pltpu.make_async_remote_copy(
        src_ref=src, dst_ref=dst, send_sem=send_sem, recv_sem=recv_sem, device_id=to, device_id_type=MESH
    )
    copy.start()
    return copy


def nn(a, b):
    return lax.dot_general(a, b, (((1,), (0,)), ((), ())), preferred_element_type=F32)


def nt(a, b):
    return lax.dot_general(a, b, (((1,), (1,)), ((), ())), preferred_element_type=F32)


def tn(a, b):
    return lax.dot_general(a, b, (((0,), (0,)), ((), ())), preferred_element_type=F32)


def to_rows(grid):
    first, second = grid[0], grid[1]
    low = lax.broadcasted_iota(jnp.int32, first.shape, 1) < 4
    even = jnp.where(low, first, pltpu.roll(second, 4, 1))
    odd = jnp.where(low, pltpu.roll(first, 4, 1), second)
    return jnp.stack([even, odd], axis=1).reshape(128, first.shape[-1])


def to_grid(rows):
    split = rows.reshape(8, 2, 8, rows.shape[-1])
    even, odd = split[:, 0], split[:, 1]
    low = lax.broadcasted_iota(jnp.int32, even.shape, 1) < 4
    first = jnp.where(low, even, pltpu.roll(odd, 4, 1))
    second = jnp.where(low, pltpu.roll(even, 4, 1), odd)
    return first, second


def norm_stats(values):
    inverse = lax.rsqrt(jnp.mean(values * values, axis=-1, keepdims=True) + EPSILON)
    return values * inverse, inverse


def norm_back(grad_normed, normed, inverse, gain):
    scaled = grad_normed * gain
    return inverse * (scaled - normed * jnp.mean(scaled * normed, axis=-1, keepdims=True))


def two_heads(pair):
    lane = lax.broadcasted_iota(jnp.int32, (128, 128), 1)
    first = jnp.where(lane < 64, 1.0, 0.0).astype(BF16)
    second = jnp.where(lane < 64, 0.0, 1.0).astype(BF16)
    return jnp.concatenate([pair * first, pair * second], axis=0)


def over_keys(across):
    return jnp.concatenate([across[:, 0:128], across[:, 128:256]], axis=0)


def line_probs(scores, mask):
    if mask is not None:
        scores = jnp.where(mask, scores, LOWEST)
    weights = jnp.exp(scores - jnp.max(scores, axis=0, keepdims=True))
    return weights * (1.0 / jnp.sum(weights, axis=0, keepdims=True))


def line_masks():
    keys = lax.broadcasted_iota(jnp.int32, (128, 256), 0)
    queries = lax.broadcasted_iota(jnp.int32, (128, 256), 1) & 127
    apart = keys ^ queries
    return (apart & 0x74) == 0, (apart & 0x0F) == 0


def pair_scores(queries, keys):
    return nt(keys, two_heads(queries * jnp.array(0.125, BF16)))


def pair_out(probs, values):
    return tn(over_keys(probs), two_heads(values))


def score_grads(probs, grad_probs):
    return probs * (grad_probs - jnp.sum(probs * grad_probs, axis=0, keepdims=True))


def pair_back(rounded, grad_scores, queries, keys, grads):
    both = two_heads(grads)
    grad_values = nn(rounded, both)
    grad_keys = nn(grad_scores, two_heads(queries * jnp.array(0.125, BF16)))
    grad_queries = tn(over_keys(grad_scores), two_heads(keys)) * 0.125
    return grad_queries, grad_keys, grad_values


class Ring:
    def __init__(self, me, dev, part, relay, fin, ss, rs):
        self.me, self.dev, self.part, self.relay, self.fin, self.ss, self.rs = me, dev, part, relay, fin, ss, rs
        self.right, self.left, self.over = (me + 1) % 4, (me + 3) % 4, (me + 2) % 4
        self.copies = []

    def send(self, src, dst, to):
        n = len(self.copies)
        self.copies.append(remote(src, dst, self.ss.at[n], self.rs.at[n], self.dev(to)))

    def start(self):
        if self.relay is None:
            for n, to in enumerate((self.over, self.right, self.left)):
                for h in range(2):
                    self.send(self.part(to, h), self.fin.at[n, h], to)
            return
        self.send(self.part(self.over, 0), self.relay.at[0], self.right)
        self.send(self.part(self.over, 1), self.relay.at[1], self.left)
        self.send(self.part(self.right, 1), self.fin.at[0, 1], self.right)
        self.send(self.part(self.left, 0), self.fin.at[0, 0], self.left)

    def middle(self):
        for h, to in ((0, self.right), (1, self.left)):
            self.copies[h].wait_recv()
            ref = self.part(to, h)
            ref[...] = (ref[...].astype(F32) + self.relay[h].astype(F32)).astype(BF16)
            self.send(ref, self.fin.at[1, h], to)

    def finish(self):
        for copy in self.copies[0 if self.relay is None else 2 :]:
            copy.wait_recv()

    def result(self, h):
        total = self.part(self.me, h)[...].astype(F32)
        for n in range(3 if self.relay is None else 2):
            total = total + self.fin[n, h].astype(F32)
        return total.astype(BF16)

    def drain(self):
        for copy in self.copies:
            copy.wait_send()


def sum_shapes(wide, relays):
    vm, dma, part = pltpu.VMEM, pltpu.SemaphoreType.DMA, wide // 2
    shapes = dict(
        buf=vm((4, 8, 2, 16, wide), BF16),
        fin_a=vm((3, 2, 2, 2, 16, wide), BF16), fin_b=vm((3, 2, 2, 4, 16, part), BF16),
        a1=vm((4, 2, 16, wide), BF16), b1=vm((4, 4, 16, part), BF16),
        fin_a2=vm((3, 2, 2, 16, part), BF16), fin_b2=vm((3, 2, 2, 16, part), BF16),
        zbuf=vm((8, 16, part), BF16), zrecv=vm((7, 16, part), BF16), gath=vm((4, 16, part), BF16),
        ss_ring=dma((4, 6)), rs_ring=dma((4, 6)), ss_z=dma((7,)), rs_z=dma((7,)), ss_g=dma((3,)), rs_g=dma((3,)),
    )
    if relays:
        shapes.update(relay_a=vm((2, 2, 2, 16, wide), BF16), relay_b=vm((2, 2, 4, 16, part), BF16))
    return shapes


class Sum:
    def __init__(self, ref):
        self.ref = ref
        x, z, y_hi, y_lo, core = places()
        self.place = (x, z, y_hi, y_lo, core)
        y = y_hi * 2 + y_lo
        part = ref.zbuf.shape[-1]

        def lanes(lo):
            return pl.ds(pl.multiple_of(lo * part, 128), part)

        def dev_x(i):
            return device(i, z, y_hi, y_lo, core)

        def dev_y(i):
            return device(x, z, i // 2, i % 2, core)

        sems = [(ref.ss_ring.at[i], ref.rs_ring.at[i]) for i in range(4)]
        relay_a, relay_b = getattr(ref, "relay_a", None), getattr(ref, "relay_b", None)
        self.a = Ring(x, dev_x, lambda i, h: ref.buf.at[i, pl.ds(2 * h, 2)], relay_a, ref.fin_a, *sems[0])
        self.b = Ring(
            y, dev_y, lambda i, h: ref.buf.at[pl.ds(2 * h, 2), pl.ds(4, 4), i // 2, :, lanes(i % 2)],
            relay_b, ref.fin_b, *sems[1],
        )
        self.a2 = Ring(
            y, dev_y, lambda i, h: ref.a1.at[pl.ds(2 * h, 2), i // 2, :, lanes(i % 2)],
            None, ref.fin_a2, *sems[2],
        )
        self.b2 = Ring(x, dev_x, lambda i, h: ref.b1.at[i, pl.ds(2 * h, 2)], None, ref.fin_b2, *sems[3])
        self.copies = []

    def put(self, at, upper, lower):
        width = upper.shape[-1]
        both = jnp.concatenate([upper, lower], axis=1).astype(BF16)
        self.ref.buf[:, :, :, :, at : at + width] = both.reshape(4, 8, 2, 16, width)

    def start(self):
        self.a.start()
        self.b.start()

    def middle(self):
        self.a.middle()
        self.b.middle()

    def second(self):
        self.a.finish()
        for h in range(2):
            self.ref.a1[2 * h : 2 * h + 2] = self.a.result(h)
        self.a2.start()
        self.b.finish()
        for h in range(2):
            self.ref.b1[2 * h : 2 * h + 2] = self.b.result(h)
        self.b2.start()

    def along_z(self):
        ref = self.ref
        x, z, y_hi, y_lo, core = self.place
        self.a2.finish()
        for h in range(2):
            ref.zbuf[2 * h : 2 * h + 2] = self.a2.result(h)
        self.b2.finish()
        for h in range(2):
            ref.zbuf[4 + 2 * h : 6 + 2 * h] = self.b2.result(h)
        for d in range(1, 8):
            to = (z + d) % 8
            self.copies.append(
                remote(ref.zbuf.at[to], ref.zrecv.at[d - 1], ref.ss_z.at[d - 1], ref.rs_z.at[d - 1],
                       device(x, to, y_hi, y_lo, core))
            )

    def gather(self):
        ref = self.ref
        x, z, y_hi, y_lo, core = self.place
        total = ref.zbuf[z].astype(F32)
        for d in range(7):
            self.copies[d].wait_recv()
            total = total + ref.zrecv[d].astype(F32)
        mine = y_lo * 2 + core
        ref.gath[mine] = total.astype(BF16)
        self.copies += share(ref.gath, ref.ss_g, ref.rs_g)

    def finish(self):
        for copy in self.copies[7:]:
            copy.wait_recv()
        gath = self.ref.gath
        return [jnp.concatenate([gath[c].astype(F32), gath[2 + c].astype(F32)], axis=1) for c in range(2)]

    def drain(self):
        for copy in self.copies:
            copy.wait_send()
        for ring in (self.a, self.b, self.a2, self.b2):
            ring.drain()


def share(ref, send_sem, recv_sem):
    x, z, y_hi, y_lo, core = places()
    mine = y_lo * 2 + core
    return [
        remote(ref.at[mine], ref.at[mine], send_sem.at[n], recv_sem.at[n],
               device(x, z, y_hi, (y_lo + dy) % 2, (core + dc) % 2))
        for n, (dy, dc) in enumerate(((1, 1), (1, 0), (0, 1)))
    ]


def far_first(k, half):
    return half + ((k + 1) // 2) * (1 - 2 * (k % 2))


class Exchange:
    def __init__(self, send, recv, ss, rs):
        self.send, self.recv, self.ss, self.rs = send, recv, ss, rs

    def start(self):
        me = lax.axis_index("slab")
        x, z, y_hi, y_lo, core = places()

        def one(n, carry):
            kz, kx, ky = n // 8, (n // 2) % 4, n % 2
            dz, dx = far_first(kz, 4), far_first(kx, 2)
            to = device((x + dx) % 4, (z + dz) % 8, (y_hi + 1 - ky) % 2, y_lo, core)
            remote(self.send.at[to[0]], self.recv.at[me], self.ss, self.rs, to)
            return carry

        lax.fori_loop(0, SLABS - 1, one, 0)
        self.recv[me] = self.send[me]

    def wait(self):
        got = self.send.at[pl.ds(0, SLABS - 1)]
        pltpu.make_async_copy(got, got, self.rs).wait()

    def drain(self):
        sent = self.send.at[pl.ds(0, SLABS - 1)]
        pltpu.make_async_copy(sent, sent, self.ss).wait()


def by_pair(blocks):
    width = blocks[0].shape[-1]
    return jnp.stack([b.reshape(16, 8, width) for b in blocks], axis=1).reshape(SLABS, 8, width)


def scratch():
    vm, dma = pltpu.VMEM, pltpu.SemaphoreType.DMA
    return dict(
        wq=vm((512, 1536), BF16), wo=vm((512, 512), BF16), wu=vm((512, 2048), BF16), wd=vm((2048, 512), BF16),
        sw=dma((8,)),
        tok=vm((2, 8, 8, 512), BF16), cot_in=vm((2, 8, 8, 512), BF16), ga=vm((1, 512), F32), gm=vm((1, 512), F32),
        qkv=vm((128, 1536), BF16),
        qsend=vm((SLABS, 8, 384), BF16), qrecv=vm((SLABS, 8, 384), BF16),
        hsend=vm((SLABS, 8, 128), BF16), hrecv=vm((SLABS, 8, 128), BF16),
        osend=vm((SLABS, 8, 128), BF16), orecv=vm((SLABS, 8, 128), BF16),
        gsend=vm((SLABS, 8, 128), BF16), grecv=vm((SLABS, 8, 128), BF16),
        dsend=vm((SLABS, 8, 384), BF16), drecv=vm((SLABS, 8, 384), BF16),
        hline=vm((4, SLABS, 8, 128), BF16), ss_h=dma((3,)), rs_h=dma((3,)),
        ss_x=dma((5,)), rs_x=dma((5,)),
        z32=vm((3, 512, 128), F32), o32=vm((512, 128), F32), g32=vm((512, 128), F32), d32=vm((3, 512, 128), F32),
        px=vm((4, 128, 256), F32), py=vm((4, 128, 256), F32), pz=vm((4, 128, 256), F32),
        oxy=vm((128, 512), F32), dxy=vm((128, 1536), F32), gmix=vm((128, 512), BF16),
        gact=vm((128, 2048), F32), flat=vm((128, 512), F32), gres=vm((128, 512), F32),
        b_h1=vm((256, 512), BF16), b_mixed=vm((256, 512), BF16), b_h2=vm((256, 512), BF16), b_act=vm((256, 2048), BF16),
        cot=vm((128, 512), BF16), gu=vm((128, 2048), BF16), grb=vm((128, 512), BF16), gp=vm((128, 1536), BF16),
        b_cot=vm((256, 256), BF16), b_gu=vm((256, 1024), BF16), b_grb=vm((256, 256), BF16), b_gp=vm((256, 768), BF16),
        ss_core=dma((13,)), rs_core=dma((13,)),
        zpart=vm((512, 384), F32), zpart_b=vm((512, 384), BF16), zpeer=vm((2, 512, 128), BF16),
        down32=vm((SLABS, 32, 256), F32), out32=vm((512, 256), F32), qkv32=vm((512, 768), F32),
        one=sum_shapes(1024, True), two=sum_shapes(512, True),
    )


def kernel(factor, tree, tok_h, cot_h, wq_h, wo_h, wu_h, wd_h, ga_h, gm_h, o_tok, o_qkv, o_out, o_up, o_down, o_g1, o_g2, *refs):
    r = jax.tree.unflatten(tree, refs)
    r, r_one, r_two = types.SimpleNamespace(**r), types.SimpleNamespace(**r["one"]), types.SimpleNamespace(**r["two"])
    x, z, y_hi, y_lo, core = places()
    slab, case = lax.axis_index("slab"), lax.axis_index("case")
    other = device(x, z, y_hi, y_lo, 1 - core)

    loads = [
        pltpu.make_async_copy(src, dst, r.sw.at[n])
        for n, (src, dst) in enumerate(
            ((tok_h, r.tok), (ga_h, r.ga), (wq_h, r.wq), (cot_h, r.cot_in), (gm_h, r.gm), (wd_h, r.wd), (wo_h, r.wo), (wu_h, r.wu))
        )
    ]
    for load in loads[0:5]:
        load.start()

    barrier = pltpu.get_barrier_semaphore()

    def greet(d, carry):
        pl.semaphore_signal(barrier, inc=1, device_id=((slab + d) % SLABS, case), device_id_type=MESH)
        return carry

    lax.fori_loop(1, SLABS, greet, 0)
    for peer in (
        other,
        device(x, z, y_hi, 1 - y_lo, core),
        device(x, z, y_hi, 1 - y_lo, 1 - core),
        device(x, z, 1 - y_hi, 1 - y_lo, core),
    ):
        pl.semaphore_signal(barrier, inc=1, device_id=peer, device_id_type=MESH)

    loads[0].wait()
    loads[1].wait()
    gain_one = r.ga[...]
    r.flat[...] = to_rows(r.tok[...].astype(F32))
    normed_one, inverse_one = norm_stats(r.flat[...])
    hidden_one = normed_one * gain_one
    r.b_h1[0:128, :] = hidden_one.astype(BF16)
    r.hsend[...] = by_pair([hidden_one[:, 128 * j : 128 * j + 128] for j in range(4)]).astype(BF16)
    loads[2].wait()
    for i in range(3):
        r.qkv[:, 512 * i : 512 * i + 512] = nn(r.b_h1[0:128, :], r.wq[:, 512 * i : 512 * i + 512]).astype(BF16)
    for i in range(3):
        r.qsend[:, :, 128 * i : 128 * i + 128] = by_pair(
            [r.qkv[:, 512 * i + 128 * j : 512 * i + 128 * j + 128].astype(F32) for j in range(4)]
        ).astype(BF16)
    for load in loads[5:]:
        load.start()
    pl.semaphore_wait(barrier, SLABS + 3)
    ex_q = Exchange(r.qsend, r.qrecv, r.ss_x.at[0], r.rs_x.at[0])
    ex_o = Exchange(r.osend, r.orecv, r.ss_x.at[1], r.rs_x.at[1])
    ex_g = Exchange(r.gsend, r.grecv, r.ss_x.at[2], r.rs_x.at[2])
    ex_d = Exchange(r.dsend, r.drecv, r.ss_x.at[3], r.rs_x.at[3])
    ex_h = Exchange(r.hsend, r.hrecv, r.ss_x.at[4], r.rs_x.at[4])
    ex_q.start()
    ex_h.start()

    core_copies = []

    def to_core_full(ref):
        n = len(core_copies)
        core_copies.append(
            remote(ref.at[pl.ds(0, 128)], ref.at[pl.ds(128, 128)], r.ss_core.at[n], r.rs_core.at[n], other)
        )

    def to_core_half(src, dst):
        n, half = len(core_copies), dst.shape[-1]
        theirs = src.at[:, pl.ds(pl.multiple_of((1 - core) * half, 128), half)]
        core_copies.append(remote(theirs, dst.at[pl.ds(128, 128)], r.ss_core.at[n], r.rs_core.at[n], other))
        dst[0:128, :] = src[:, pl.ds(pl.multiple_of(core * half, 128), half)]

    loads[3].wait()
    loads[4].wait()
    gain_two = r.gm[...]
    r.cot[...] = to_rows(r.cot_in[...].astype(F32)).astype(BF16)
    to_core_full(r.b_h1)
    to_core_half(r.cot, r.b_cot)

    def pair(j):
        return [r.qkv[:, 512 * i + 128 * j : 512 * i + 128 * j + 128] for i in range(3)]

    mask_x, mask_y = line_masks()
    for j in range(4):
        queries, keys, values = pair(j)
        scores = pair_scores(queries, keys)
        r.px[j] = line_probs(scores, mask_x)
        r.py[j] = line_probs(scores, mask_y)
        r.oxy[:, 128 * j : 128 * j + 128] = pair_out((r.px[j] + r.py[j]).astype(BF16), values)

    loads[5].wait()
    for i in range(4):
        at = slice(512 * i, 512 * i + 512)
        r.gact[:, at] = nt(r.cot[...], r.wd[at, :])

    ex_q.wait()
    for i in range(3):
        r.z32[i] = r.qrecv[:, :, 128 * i : 128 * i + 128].astype(F32).reshape(512, 128)

    def line(j):
        return [r.z32[i, pl.ds(j, 128, stride=4), :].astype(BF16) for i in range(3)]

    for j in range(4):
        queries, keys, values = line(j)
        probs = line_probs(pair_scores(queries, keys), None)
        r.pz[j] = probs
        r.o32[pl.ds(j, 128, stride=4), :] = pair_out(probs.astype(BF16), values)
    r.osend[...] = r.o32[...].reshape(SLABS, 8, 128).astype(BF16)
    ex_o.start()
    ex_h.wait()
    r.hline[slab % 4] = r.hrecv[...]

    loads[6].wait()
    loads[7].wait()
    ex_o.wait()
    h_at, h_copies = slab % 4, []
    for n, (dz, dy) in enumerate(((1, 1), (0, 1), (1, 0))):
        to = device(x, z + dz * (1 - 2 * (z % 2)), (y_hi + dy) % 2, y_lo, core)
        h_copies.append(remote(r.hline.at[h_at], r.hline.at[h_at], r.ss_h.at[n], r.rs_h.at[n], to))
    from_z = r.orecv[...].astype(F32).reshape(16, 4, 8, 128)
    for j in range(4):
        at = slice(128 * j, 128 * j + 128)
        r.b_mixed[0:128, at] = (r.oxy[:, at] + from_z[:, j].reshape(128, 128)).astype(BF16)
    residual = (r.flat[...] + nn(r.b_mixed[0:128, :], r.wo[...])).astype(BF16)
    normed_two, inverse_two = norm_stats(residual.astype(F32))
    r.b_h2[0:128, :] = (normed_two * gain_two).astype(BF16)
    to_core_full(r.b_h2)
    to_core_full(r.b_mixed)
    grad_hidden_two = jnp.zeros((128, 512), F32)
    for i in range(4):
        at = slice(512 * i, 512 * i + 512)
        u = nn(r.b_h2[0:128, :], r.wu[:, at])
        square = u * u
        tangent = jnp.tanh(ROOT * u * (1.0 + 0.044715 * square))
        half = 0.5 * (1.0 + tangent)
        r.b_act[0:128, at] = (u * half).astype(BF16)
        act = r.b_act.at[:, at]
        to_core_full(act)
        slope = half + 0.5 * u * (1.0 - tangent * tangent) * ROOT * (1.0 + 3.0 * 0.044715 * square)
        r.gu[:, at] = (r.gact[:, at] * slope).astype(BF16)
        grad_hidden_two = grad_hidden_two + nt(r.gu[:, at], r.wu[:, at])
    r.gres[...] = r.cot[...].astype(F32) + norm_back(grad_hidden_two, normed_two, inverse_two, gain_two)
    r.grb[...] = r.gres[...].astype(BF16)
    r.gmix[...] = nt(r.grb[...], r.wo[...]).astype(BF16)
    r.gsend[...] = by_pair([r.gmix[:, 128 * j : 128 * j + 128].astype(F32) for j in range(4)]).astype(BF16)
    to_core_half(r.gu, r.b_gu)
    to_core_half(r.grb, r.b_grb)

    ex_g.start()

    one, two = Sum(r_one), Sum(r_two)
    for copy in core_copies[1:10]:
        copy.wait_recv()
    r.down32[...] = tn(r.b_act[...], r.b_cot[...]).reshape(SLABS, 32, 256)
    for i in range(2):
        one.put(
            256 * i,
            tn(r.b_h2[...], r.b_gu[:, 256 * i : 256 * i + 256]).reshape(SLABS, 8, 256),
            tn(r.b_h2[...], r.b_gu[:, 512 + 256 * i : 768 + 256 * i]).reshape(SLABS, 8, 256),
        )
    one.put(512, r.down32[:, 0:8, :], r.down32[:, 16:24, :])
    one.put(768, r.down32[:, 8:16, :], r.down32[:, 24:32, :])
    one.start()

    for j in range(4):
        queries, keys, values = pair(j)
        grads = r.gmix[:, 128 * j : 128 * j + 128]
        grad_probs = nt(values, two_heads(grads))
        probs_x, probs_y = r.px[j], r.py[j]
        grad_scores = (score_grads(probs_x, grad_probs) + score_grads(probs_y, grad_probs)).astype(BF16)
        back = pair_back((probs_x + probs_y).astype(BF16), grad_scores, queries, keys, grads)
        for i in range(3):
            at = slice(512 * i + 128 * j, 512 * i + 128 * j + 128)
            r.dxy[:, at] = back[i]
            r.gp[:, at] = back[i].astype(BF16)
    to_core_half(r.gp, r.b_gp)

    r.out32[...] = tn(r.b_mixed[...], r.b_grb[...])
    for copy in core_copies[0:1] + core_copies[10:]:
        copy.wait_recv()
    for i in range(3):
        at = slice(256 * i, 256 * i + 256)
        r.qkv32[:, at] = tn(r.b_h1[...], r.b_gp[:, at])

    ex_g.wait()
    r.g32[...] = r.grecv[...].astype(F32).reshape(512, 128)
    for j in range(4):
        queries, keys, values = line(j)
        grads = r.g32[pl.ds(j, 128, stride=4), :].astype(BF16)
        probs = r.pz[j]
        grad_scores = score_grads(probs, nt(values, two_heads(grads))).astype(BF16)
        back = pair_back(probs.astype(BF16), grad_scores, queries, keys, grads)
        for i in range(3):
            r.d32[i, pl.ds(j, 128, stride=4), :] = back[i]

    for copy in h_copies:
        copy.wait_recv()
    line_grads = jnp.concatenate([r.d32[i].astype(BF16) for i in range(3)], axis=1)
    for i in range(4):
        hidden_lines = r.hline[i].astype(F32).reshape(512, 128).astype(BF16)
        r.zpart[128 * i : 128 * i + 128, :] = tn(hidden_lines, line_grads)
    r.zpart_b[...] = r.zpart[...].astype(BF16)

    def outer(owner):
        return pl.ds(pl.multiple_of(owner * 256, 128), 128)

    z_copies = [
        remote(r.zpart_b.at[:, outer(1 - core)], r.zpeer.at[0], r.ss_core.at[11], r.rs_core.at[11], other),
        remote(r.zpart_b.at[:, pl.ds(128, 128)], r.zpeer.at[1], r.ss_core.at[12], r.rs_core.at[12], other),
    ]
    one.middle()
    pair_at = slab % 4
    at_outer = pl.ds(pl.multiple_of(core * 256 + pair_at * 128, 128), 128)
    at_keys = pl.ds(pl.multiple_of((1 - core) * 512 + (pair_at % 2) * 128, 128), 128)
    owned = jnp.where(core == pair_at // 2, 1.0, 0.0)
    z_copies[0].wait_recv()
    r.qkv32[:, at_outer] = r.qkv32[:, at_outer] + (r.zpart[:, outer(core)] + r.zpeer[0].astype(F32))
    z_copies[1].wait_recv()
    r.qkv32[:, at_keys] = r.qkv32[:, at_keys] + owned * (r.zpart[:, 128:256] + r.zpeer[1].astype(F32))

    def rows(ref, at):
        return ref[:, at : at + 256].reshape(SLABS, 8, 256)

    two.put(0, rows(r.qkv32, 0), rows(r.qkv32, 256))
    two.put(256, rows(r.qkv32, 512), rows(r.out32, 0))
    two.start()
    for i in range(3):
        r.dsend[:, :, 128 * i : 128 * i + 128] = r.d32[i].reshape(SLABS, 8, 128).astype(BF16)
    one.second()
    two.middle()
    ex_d.start()
    two.second()
    one.along_z()
    two.along_z()

    ex_d.wait()
    for i in range(3):
        from_z = r.drecv[:, :, 128 * i : 128 * i + 128].astype(F32).reshape(16, 4, 8, 128)
        for j in range(4):
            at = slice(512 * i + 128 * j, 512 * i + 128 * j + 128)
            r.dxy[:, at] = r.dxy[:, at] + from_z[:, j].reshape(128, 128)
    grad_hidden_one = nt(r.dxy[...].astype(BF16), r.wq[...])
    normed_one, inverse_one = norm_stats(r.flat[...])
    first, second = to_grid(r.gres[...] + norm_back(grad_hidden_one, normed_one, inverse_one, gain_one))
    o_tok[0] = first.astype(BF16)
    o_tok[1] = second.astype(BF16)

    one.gather()
    two.gather()

    own_rows = pl.ds(pl.multiple_of((slab // 2) * 16, 16), 16)

    def weight_rows(ref):
        both = ref[own_rows, :].astype(F32)
        return jnp.where(slab % 2 == 0, both[0:8], both[8:16])

    for c, full in enumerate(one.finish()):
        full = full * factor
        o_up[:, 1024 * c : 1024 * c + 512] = full[0:8, 0:512]
        o_up[:, 1024 * c + 512 : 1024 * c + 1024] = full[8:16, 0:512]
        at = slice(256 * c, 256 * c + 256)
        o_down[0:8, at] = full[0:8, 512:768]
        o_down[8:16, at] = full[0:8, 768:1024]
        o_down[16:24, at] = full[8:16, 512:768]
        o_down[24:32, at] = full[8:16, 768:1024]

    def over_gain(rows, gain):
        lane = lax.broadcasted_iota(jnp.int32, (8, 512), 1)
        row = lax.broadcasted_iota(jnp.int32, (8, 512), 0)
        own = jnp.sum(jnp.where(lane == slab * 8 + row, gain, 0.0), axis=1, keepdims=True)
        return jnp.broadcast_to(jnp.sum(rows, axis=1, keepdims=True) / own, (8, 128))

    o_g2[...] = over_gain(o_up[...] * weight_rows(r.wu), gain_two)
    for c, full in enumerate(two.finish()):
        full = full * factor
        o_qkv[:, 768 * c : 768 * c + 256] = full[0:8, 0:256]
        o_qkv[:, 768 * c + 256 : 768 * c + 512] = full[8:16, 0:256]
        o_qkv[:, 768 * c + 512 : 768 * c + 768] = full[0:8, 256:512]
        o_out[:, 256 * c : 256 * c + 256] = full[8:16, 256:512]
    o_g1[...] = over_gain(o_qkv[...] * weight_rows(r.wq), gain_one)

    for exchange in (ex_q, ex_h, ex_o, ex_g, ex_d):
        exchange.drain()
    for copy in core_copies + h_copies + z_copies:
        copy.wait_send()
    one.drain()
    two.drain()


def results_kernel(tok, qkv, out, up, down, g1, g2, o_tok, o_qkv, o_out, o_up, o_down, o_g1, o_g2):
    for src, dst in ((tok, o_tok), (qkv, o_qkv), (out, o_out), (up, o_up), (down, o_down)):
        dst[...] = src[...]
    row = lax.broadcasted_iota(jnp.int32, (8, 128), 0)
    lane = lax.broadcasted_iota(jnp.int32, (8, 128), 1)
    for src, dst in ((g1, o_g1), (g2, o_g2)):
        dst[...] = jnp.sum(jnp.where(row == lane, src[...], 0.0), axis=0)[0:8]


def body(tokens, cotangent, w_qkv, w_out, w_up, w_down, gain_attn, gain_mlp):
    width = tokens.shape[-1]
    factor = 1.0 / math.sqrt(128 * lax.axis_size("slab") * lax.axis_size("case"))
    shapes = scratch()
    leaves, tree = jax.tree.flatten(shapes)
    vmem, any_space = pl.BlockSpec(memory_space=pltpu.VMEM), pl.BlockSpec(memory_space=pl.ANY)
    outs = ((8, 1536), (8, 512), (8, 2048), (32, 512), (8, 128), (8, 128))
    result = pl.pallas_call(
        functools.partial(kernel, factor, tree),
        out_shape=[jax.ShapeDtypeStruct((2, 8, 8, width), BF16)] + [jax.ShapeDtypeStruct(s, F32) for s in outs],
        in_specs=[any_space] * 8,
        out_specs=[vmem] * 7,
        scratch_shapes=leaves,
        compiler_params=pltpu.CompilerParams(
            collective_id=1, has_side_effects=True, vmem_limit_bytes=56 * 1024 * 1024
        ),
        cost_estimate=pl.CostEstimate(flops=3_500_000_000, bytes_accessed=7_000_000, transcendentals=0),
    )(
        tokens.reshape(2, 8, 8, width),
        cotangent.reshape(2, 8, 8, width),
        w_qkv,
        w_out,
        w_up,
        w_down,
        gain_attn.reshape(1, width),
        gain_mlp.reshape(1, width),
    )
    result = pl.pallas_call(
        results_kernel,
        out_shape=[jax.ShapeDtypeStruct((2, 8, 8, width), BF16)]
        + [jax.ShapeDtypeStruct(s, F32) for s in outs[:4] + ((8,), (8,))],
        in_specs=[vmem] * 7,
        out_specs=[vmem] * 7,
    )(*result)
    return (result[0].reshape(tokens.shape), *result[1:])


def solution(mesh):
    grid = P("case", "slab", None, None, None)
    return jax.shard_map(
        body,
        mesh=mesh,
        in_specs=(grid, grid, P(), P(), P(), P(), P(), P()),
        out_specs=(grid, P("slab", None), P("slab", None), P("slab", None), P("slab", None), P("slab"), P("slab")),
        check_vma=False,
    )
```
